128 devices in a mesh: leaf: 64 (over x, y, z), rhs: 2 (over core).
Axes of the slice: x: 4, y: 4, z: 4, core: 2. Of those that a mesh axis runs over, the one named last changes fastest.
Arguments:
- points: float32 [524288, 64], P('leaf', 'rhs'), may hold values from -6 to 6
- vectors: float32 [524288, 64], P('leaf', 'rhs'), may hold values from -6 to 6
- leaf_basis: float32 [524288, 64], P('leaf'), may hold values from -0.375 to 0.375
- skel_lv0: float32 [131072, 64], P('leaf'), may hold values from -5 to 5
- skel_lv1: float32 [65536, 64], P('leaf'), may hold values from -5 to 5
- skel_lv2: float32 [32768, 64], P('leaf'), may hold values from -5 to 5
- transfer_lv1: float32 [131072, 64], P('leaf'), may hold values from -0.5 to 0.5
- transfer_lv2: float32 [65536, 64], P('leaf'), may hold values from -0.5 to 0.5
- transfer_root: float32 [32768, 64], P('leaf'), may hold values from -0.25 to 0.25
- root_skeleton_points: float32 [4096, 64], replicated, may hold values from -5 to 5
- near_mask: int32 [2048, 8], P('leaf'), may hold values from 0 to 1, as said below
- far_lv0: int32 [2048, 4], P('leaf'), may hold values 0 or 1
- far_lv1: int32 [1024, 4], P('leaf'), may hold values 0 or 1
- far_lv2: int32 [512, 4], P('leaf'), may hold values 0 or 1
Outputs:
- product: float32 [524288, 64], P('leaf', 'rhs')
The draws below stay inside these ranges and needn't reach their ends.
Inputs may be any that keep to these rules, and one draw needn't show every extreme that they name: `near_mask`: Symmetric: the entry of leaf i at offset +d equals the entry of leaf i + d at offset -d; entries whose partner lies outside the 2048 leaves are 0.
All inputs are finite; a program needn't handle non-finite values. No bound on the sum of `far_lv0` or of `far_lv1` or of `far_lv2` on one device may be relied on, other than what follows from the above.
Results may differ from the reference program's by a relative error of at most 0.0003.
Values sent between devices are 32-bit elements; how exact they have to be, the bound alone decides.
No kernel may reach another device: no remote copies, remote signals or barrier semaphores. Data moves between devices by JAX's collectives and lax.ppermute only.
A program may use at most 128 MiB of HBM per device.

```python
import jax
import jax.numpy as jnp
from jax import lax

DIM = 64
RANK = 64
NRHS = 64
LEAF = 256
REACH = 4
FREACH = 2
LEAVES_DEV = 32
NLEAF = 2048
NPTS = 524288
N_LEAF = 64


def draw_near_mask(key, part):
    key = jax.random.fold_in(key, 7)
    key_caps, key_bands = jax.random.split(key)
    devices = NLEAF // LEAVES_DEV
    device_caps = jax.random.randint(key_caps, (devices,), 1, REACH + 1)
    device_caps = device_caps.at[0].set(REACH)
    leaf_bands = jax.random.randint(key_bands, (NLEAF,), 1, REACH + 1)
    leaf_bands = jnp.minimum(leaf_bands, jnp.repeat(device_caps, LEAVES_DEV))
    leaf_bands = leaf_bands.at[:REACH + 1].set(REACH)
    offsets = jnp.concatenate([-jnp.arange(REACH, 0, -1), jnp.arange(1, REACH + 1)]).astype(jnp.int32)
    leaf_ids = jnp.arange(NLEAF, dtype=jnp.int32)
    partner = leaf_ids[:, None] + offsets[None, :]
    inside = (partner >= 0) & (partner < NLEAF)
    partner_band = leaf_bands[jnp.clip(partner, 0, NLEAF - 1)]
    linked = inside & (jnp.abs(offsets)[None, :] <= jnp.minimum(leaf_bands[:, None], partner_band))
    return linked.astype(jnp.int32)


def touch_ends(entries, rng, smallest, largest):
    extent = entries.shape
    place = [jax.random.randint(jax.random.fold_in(rng, axis), (), 0, extent[axis]) for axis in range(len(extent))]
    entries = entries.at[tuple(place)].set(smallest)
    longest = extent.index(max(extent))
    place[longest] = (place[longest] + 1) % extent[longest]
    return entries.at[tuple(place)].set(largest)


def level_of(own_key, dims, pieces, low, largest):
    def one(position, blocks):
        steps = jax.random.uniform(jax.random.fold_in(jax.random.fold_in(own_key, 6), position), (blocks,), jnp.float32, low / len(pieces), largest / len(pieces))
        return jnp.repeat(jnp.exp(steps), dims[position] // blocks).reshape((-1,) + (1,) * (len(dims) - position - 1))

    gain = one(*pieces[0])
    for cut in pieces[1:]:
        gain = gain * one(*cut)
    return gain


def normal_values(key, shape, scale, reach, pieces=(), kind=jnp.bfloat16):
    entries = jax.random.normal(key, shape, jnp.float32) * scale
    if len(pieces) > 0:
        entries = level_of(key, shape, pieces, -0.22, 0.18) * entries
    return jnp.clip(entries, min=-reach, max=reach).astype(kind)


def setup_inputs(seed: int = 0) -> dict:
    seeds = jax.random.split(jax.random.key(seed), 15)
    points = normal_values(seeds[0], (NPTS, DIM), 1.0, 6.0, ((0, 64), (1, 2)), jnp.float32)
    vectors = normal_values(seeds[1], (NPTS, NRHS), 1.0, 6.0, ((0, 64), (1, 2)), jnp.float32)
    leaf_basis = normal_values(seeds[2], (NPTS, RANK), LEAF ** -0.5, 0.375, ((0, 64),), jnp.float32)
    skel_lv0 = normal_values(seeds[3], (NLEAF * RANK, DIM), 0.7, 5.0, ((0, 64),), jnp.float32)
    skel_lv1 = normal_values(seeds[4], (NLEAF // 2 * RANK, DIM), 0.7, 5.0, ((0, 64),), jnp.float32)
    skel_lv2 = normal_values(seeds[5], (NLEAF // 4 * RANK, DIM), 0.7, 5.0, ((0, 64),), jnp.float32)
    transfer_lv1 = normal_values(seeds[6], (NLEAF * RANK, RANK), (2 * RANK) ** -0.5, 0.5, ((0, 64),), jnp.float32)
    transfer_lv2 = normal_values(seeds[7], (NLEAF // 2 * RANK, RANK), (2 * RANK) ** -0.5, 0.5, ((0, 64),), jnp.float32)
    transfer_root = normal_values(seeds[8], (NLEAF // 4 * RANK, RANK), (LEAVES_DEV // 4 * RANK) ** -0.5, 0.25, ((0, 64),), jnp.float32)
    root_skeleton_points = normal_values(seeds[9], (N_LEAF * RANK, DIM), 0.7, 5.0, (), jnp.float32)
    near_mask = draw_near_mask(jax.random.fold_in(seeds[14], 71), 0)
    far_lv0 = touch_ends((jax.random.randint(seeds[11], (NLEAF, 2 * FREACH), 0, 4) < 3).astype(jnp.int32), jax.random.fold_in(seeds[11], 1), 0, 1)
    far_lv1 = touch_ends((jax.random.randint(seeds[12], (NLEAF // 2, 2 * FREACH), 0, 4) < 3).astype(jnp.int32), jax.random.fold_in(seeds[12], 1), 0, 1)
    far_lv2 = touch_ends((jax.random.randint(seeds[13], (NLEAF // 4, 2 * FREACH), 0, 4) < 3).astype(jnp.int32), jax.random.fold_in(seeds[13], 1), 0, 1)
    return {"points": points, "vectors": vectors, "leaf_basis": leaf_basis, "skel_lv0": skel_lv0, "skel_lv1": skel_lv1, "skel_lv2": skel_lv2, "transfer_lv1": transfer_lv1, "transfer_lv2": transfer_lv2, "transfer_root": transfer_root, "root_skeleton_points": root_skeleton_points, "near_mask": near_mask, "far_lv0": far_lv0, "far_lv1": far_lv1, "far_lv2": far_lv2}


KERNEL_SCALE = 1.0 / 24.0
PRECISE = lax.Precision.HIGHEST


def kernel_block(left_pts, right_pts):
    inner_product = jnp.einsum("bmd,bnd->bmn", left_pts, right_pts, precision=PRECISE)
    left_squared_norm = jnp.sum(left_pts * left_pts, axis=-1)
    right_squared_norm = jnp.sum(right_pts * right_pts, axis=-1)
    return jnp.exp((2.0 * inner_product - left_squared_norm[:, :, None] - right_squared_norm[:, None, :]) * KERNEL_SCALE)


def upward(children, transfer, fan_out):
    parents = transfer.shape[0] // (fan_out * RANK)
    transfer_mats = transfer.reshape(parents, fan_out, RANK, RANK)
    grouped = children.reshape(parents, fan_out, RANK, children.shape[2])
    return jnp.einsum("pckq,pckr->pqr", transfer_mats, grouped, precision=PRECISE)


def downward(parent_field, transfer, fan_out):
    parents = transfer.shape[0] // (fan_out * RANK)
    transfer_mats = transfer.reshape(parents, fan_out, RANK, RANK)
    spread = jnp.einsum("pckq,pqr->pckr", transfer_mats, parent_field, precision=PRECISE)
    return spread.reshape(parents * fan_out, RANK, parent_field.shape[2])


def couple_level(coeffs, skeleton, far_mask):
    count = coeffs.shape[0]
    mask_f = far_mask.astype(jnp.float32)
    pad_c = jnp.pad(coeffs, ((FREACH, FREACH), (0, 0), (0, 0)))
    pad_s = jnp.pad(skeleton, ((FREACH, FREACH), (0, 0), (0, 0)))
    result = jnp.zeros_like(coeffs)
    for offset in list(range(-FREACH, 0)) + list(range(1, FREACH + 1)):
        column = FREACH + offset if offset < 0 else FREACH + offset - 1
        src_c = pad_c[FREACH + offset: FREACH + offset + count]
        src_s = pad_s[FREACH + offset: FREACH + offset + count]
        coupling = kernel_block(skeleton, src_s)
        block_term = jnp.einsum("bkq,bqr->bkr", coupling, src_c, precision=PRECISE)
        result = result + mask_f[:, column][:, None, None] * block_term
    return result


def near_field(leaf_points, leaf_vector, near_mask):
    mask_f = near_mask.astype(jnp.float32)
    pad_p = jnp.pad(leaf_points, ((REACH, REACH), (0, 0), (0, 0)))
    pad_v = jnp.pad(leaf_vector, ((REACH, REACH), (0, 0), (0, 0)))

    def device_group(group_index):
        first_leaf = group_index * LEAVES_DEV
        targets = lax.dynamic_slice_in_dim(leaf_points, first_leaf, LEAVES_DEV, 0)
        mask_rows = lax.dynamic_slice_in_dim(mask_f, first_leaf, LEAVES_DEV, 0)
        result = jnp.zeros((LEAVES_DEV, LEAF, NRHS), jnp.float32)
        for offset in range(-REACH, REACH + 1):
            src_p = lax.dynamic_slice_in_dim(pad_p, first_leaf + REACH + offset, LEAVES_DEV, 0)
            src_v = lax.dynamic_slice_in_dim(pad_v, first_leaf + REACH + offset, LEAVES_DEV, 0)
            block_term = jnp.einsum("bmn,bnr->bmr", kernel_block(targets, src_p), src_v, precision=PRECISE)
            if offset == 0:
                result = result + block_term
            else:
                column = REACH + offset if offset < 0 else REACH + offset - 1
                result = result + mask_rows[:, column][:, None, None] * block_term
        return result

    blocks = lax.map(device_group, jnp.arange(N_LEAF, dtype=jnp.int32))
    return blocks.reshape(NLEAF, LEAF, NRHS)


def root_couple(coeff_root, skel_roots):
    root_ids = jnp.arange(N_LEAF, dtype=jnp.int32)

    def one_root(root_index):
        own_skel = lax.dynamic_slice_in_dim(skel_roots, root_index, 1, 0)
        coupling = kernel_block(jnp.broadcast_to(own_skel, skel_roots.shape), skel_roots)
        weight = (jnp.abs(root_ids - root_index) >= 2).astype(jnp.float32)
        return jnp.einsum("skq,sqr->kr", coupling * weight[:, None, None], coeff_root, precision=PRECISE)

    return lax.map(one_root, root_ids)


def reference(points, vectors, leaf_basis, skel_lv0, skel_lv1, skel_lv2, transfer_lv1, transfer_lv2, transfer_root, root_skeleton_points, near_mask, far_lv0, far_lv1, far_lv2):
    leaf_points = points.reshape(NLEAF, LEAF, DIM)
    leaf_vector = vectors.reshape(NLEAF, LEAF, NRHS)
    basis = leaf_basis.reshape(NLEAF, LEAF, RANK)
    near_part = near_field(leaf_points, leaf_vector, near_mask)
    coeff_lv0 = jnp.einsum("lpk,lpr->lkr", basis, leaf_vector, precision=PRECISE)
    coeff_lv1 = upward(coeff_lv0, transfer_lv1, 2)
    coeff_lv2 = upward(coeff_lv1, transfer_lv2, 2)
    coeff_root = upward(coeff_lv2, transfer_root, LEAVES_DEV // 4)
    field_root = root_couple(coeff_root, root_skeleton_points.reshape(N_LEAF, RANK, DIM))
    field_lv2 = couple_level(coeff_lv2, skel_lv2.reshape(-1, RANK, DIM), far_lv2) + downward(field_root, transfer_root, LEAVES_DEV // 4)
    field_lv1 = couple_level(coeff_lv1, skel_lv1.reshape(-1, RANK, DIM), far_lv1) + downward(field_lv2, transfer_lv2, 2)
    field_lv0 = couple_level(coeff_lv0, skel_lv0.reshape(-1, RANK, DIM), far_lv0) + downward(field_lv1, transfer_lv1, 2)
    far_part = jnp.einsum("lpk,lkr->lpr", basis, field_lv0, precision=PRECISE)
    return (near_part + far_part).reshape(NPTS, NRHS)
```

```python
import math

import jax
import jax.numpy as jnp
from jax import lax
from jax.experimental import pallas as pl
from jax.experimental.pallas import tpu as pltpu
from jax.sharding import PartitionSpec as P

DIM = 64
RANK = 64
LEAF = 256
REACH = 4
FREACH = 2
LEAVES_DEV = 32
RHS_DEV = 32
CHIPS = 64

HALF = LEAVES_DEV // 2
WINDOW = HALF + 2 * REACH
HALO = REACH * LEAF
EDGE = FREACH * RANK
MSG = HALO + 3 * EDGE + 2 * EDGE
GROUP = 8
SCALE = math.sqrt(2.0 / 24.0 * math.log2(math.e))
CUT = -32768.0

F32 = jnp.float32
BF16 = jnp.bfloat16
VMEM_LIMIT = 60 * 2**20

NN = (((1,), (0,)), ((), ()))
NT = (((1,), (1,)), ((), ()))


def mul(left, right, dims=NN):
    return lax.dot_general(left, right, dims, preferred_element_type=F32)


def split(x):
    high = x.astype(BF16)
    return high, (x - high.astype(F32)).astype(BF16)


def mul3(left, right, dims=NN):
    rows = left.shape[0]
    left_high, left_low = split(left)
    right_high, right_low = split(right)
    both = mul(jnp.concatenate([left_high, left_low], 0), right_high, dims)
    return both[:rows] + both[rows:] + mul(left_high, right_low, dims)


def augment(points, source_extra=None, target_extra=None):
    high, low = split(points * SCALE)
    high_f, low_f = high.astype(F32), low.astype(F32)
    norm = 0.5 * jnp.sum(high_f * (high_f + 2.0 * low_f), axis=0, keepdims=True)
    first = norm.astype(BF16).astype(F32)
    second = (norm - first).astype(BF16).astype(F32)
    third = (norm - first - second).astype(BF16).astype(F32)
    width = points.shape[1]
    row = lax.broadcasted_iota(jnp.int32, (8, width), 0)

    def rows_of(start, ones):
        picked = jnp.where(row == start, -first, 0.0)
        picked = jnp.where(row == start + 1, -second, picked)
        picked = jnp.where(row == start + 2, -third, picked)
        return jnp.where((row >= ones) & (row < ones + 3), 1.0, picked)

    nothing = jnp.zeros((8, width), F32)
    rest = jnp.zeros((DIM - 16, width), BF16)

    def block(start, ones, extra):
        tail = jnp.concatenate([rows_of(start, ones), nothing if extra is None else extra], 0)
        return tail.astype(BF16), rest

    source = jnp.concatenate([high, low, high, *block(0, 3, source_extra)], 0)
    target = jnp.concatenate([high, high, low, *block(3, 0, target_extra)], 0)
    return source, target


def weights(exponent):
    return split(jnp.exp2(exponent))


def up_kernel(
    vec, basis, lv1, lv2, root, first_pts, last_pts, first_vec, last_vec,
    first_s0, last_s0, first_s1, last_s1, first_s2, last_s2,
    coeff0, coeff1, coeff2, blocks, to_left, to_right,
):
    def leaf_pair(pair, carry):
        parts = []
        for side in range(2):
            lanes = pl.ds(pl.multiple_of((2 * pair + side) * LEAF, LEAF), LEAF)
            parts.append(mul3(vec[:, lanes], basis[:, lanes], NT))
        coeff0[:, pl.ds(pl.multiple_of(pair * 128, 128), 128)] = jnp.concatenate(parts, 1)
        return carry

    lax.fori_loop(0, LEAVES_DEV // 2, leaf_pair, 0, unroll=4)

    def up_level(children, transfer, parents, count):
        for pair in range(count // 2):
            parts = []
            for side in range(2):
                lanes = slice((2 * pair + side) * 128, (2 * pair + side + 1) * 128)
                parts.append(mul3(children[:, lanes], transfer[:, lanes], NT))
            parents[:, pair * 128 : (pair + 1) * 128] = jnp.concatenate(parts, 1)

    up_level(coeff0, lv1, coeff1, LEAVES_DEV // 2)
    up_level(coeff1, lv2, coeff2, LEAVES_DEV // 4)
    top = mul3(coeff2[...], root[...], NT)
    twice = jnp.concatenate([top, top], 1)
    lane = lax.broadcasted_iota(jnp.int32, (RHS_DEV, 128), 1)
    parity = lax.rem(lax.axis_index("leaf"), 2)
    placed = jnp.where(lane // RANK == parity, twice, 0.0)
    blocks[...] = jnp.broadcast_to(placed[None], (CHIPS, RHS_DEV, 128))

    def message(out, pts, vecs, skels, last):
        out[0:RHS_DEV, 0:HALO] = pts[...]
        out[RHS_DEV:, 0:HALO] = vecs[...]
        lanes = HALO
        for skel in skels:
            out[:, lanes : lanes + EDGE] = skel[...]
            lanes += EDGE
        ends = [ref[:, ref.shape[1] - EDGE :] if last else ref[:, :EDGE] for ref in (coeff0, coeff1, coeff2)]
        out[:RHS_DEV, lanes : lanes + EDGE] = ends[0]
        out[RHS_DEV:, lanes : lanes + EDGE] = ends[1]
        out[:RHS_DEV, lanes + EDGE :] = ends[2]
        out[RHS_DEV:, lanes + EDGE :] = jnp.zeros((RHS_DEV, EDGE), F32)

    message(to_left, first_pts, first_vec, (first_s0, first_s1, first_s2), False)
    message(to_right, last_pts, last_vec, (last_s0, last_s1, last_s2), True)


def near_kernel(
    mask, own_pts, own_vec, other_pts, other_vec, left_own, left_other, right_own, right_other,
    own_out, other_out, win_pts, win_vec, source, target, vec_t, pairs, sems,
):
    core = lax.axis_index("rhs")
    body_lanes = (WINDOW - REACH) * LEAF

    def copies(side):
        if side == 0:
            main_from, main_to, halo_to = 0, HALO, 0
            halos = (left_own, left_other)
        else:
            main_from, main_to, halo_to = LEAVES_DEV * LEAF - body_lanes, 0, body_lanes
            halos = (right_own, right_other)
        jobs = []
        for half, (pts, vecs, halo) in enumerate(
            ((own_pts, own_vec, halos[0]), (other_pts, other_vec, halos[1]))
        ):
            rows = pl.ds(half * 32, 32)
            main = pl.ds(main_to, body_lanes)
            edge = pl.ds(halo_to, HALO)
            jobs.append((pts.at[:, pl.ds(main_from, body_lanes)], win_pts.at[rows, main]))
            jobs.append((vecs.at[:, pl.ds(main_from, body_lanes)], win_vec.at[rows, main]))
            jobs.append((halo.at[pl.ds(0, 32), pl.ds(0, HALO)], win_pts.at[rows, edge]))
            jobs.append((halo.at[pl.ds(32, 32), pl.ds(0, HALO)], win_vec.at[rows, edge]))
        return [pltpu.make_async_copy(a, b, sems.at[k]) for k, (a, b) in enumerate(jobs)]

    for side in range(2):

        @pl.when(core == side)
        def _():
            for job in copies(side):
                job.start()

    own_out[...] = jnp.zeros_like(own_out)
    other_out[...] = jnp.zeros_like(other_out)

    count = jnp.int32(0)
    for leaf in range(HALF):
        for offset in range(-REACH, REACH + 1):
            pairs[count] = (leaf + REACH + offset) * 32 + leaf
            if offset == 0:
                count = count + 1
            else:
                column = REACH + offset if offset < 0 else REACH + offset - 1
                count = count + mask[column, core * HALF + leaf]
    for extra in range(GROUP):
        pairs[count + extra] = WINDOW * 32

    source[WINDOW] = jnp.zeros((4 * DIM, LEAF), BF16).reshape(LEAF, 4 * DIM)
    vec_t[WINDOW] = jnp.zeros((2 * 64, LEAF), BF16)

    for side in range(2):

        @pl.when(core == side)
        def _():
            for job in copies(side):
                job.wait()

    def prepare(leaf, carry):
        lanes = pl.ds(pl.multiple_of(leaf * LEAF, LEAF), LEAF)
        from_side, to_side = augment(win_pts[:, lanes])
        source[leaf] = from_side.T
        target[leaf] = to_side
        vec_t[leaf] = jnp.concatenate(split(win_vec[:, lanes]), 0)
        return carry

    lax.fori_loop(0, WINDOW, prepare, 0, unroll=2)

    def step(index, carry):
        found = []
        for k in range(GROUP):
            code = pairs[index * GROUP + k]
            src, tgt = lax.shift_right_logical(code, 5), lax.bitwise_and(code, 31)
            high, low = weights(mul(source[src], target[tgt + REACH]))
            both = mul(vec_t[src], high)
            found.append((tgt, both[:64] + both[64:] + mul(vec_t[src, :64], low)))
        for tgt, term in found:
            lanes = pl.ds(pl.multiple_of(tgt * LEAF, LEAF), LEAF)
            own_out[:, lanes] += term[:32]
            other_out[:, lanes] += term[32:]
        return carry

    lax.fori_loop(0, (count + GROUP - 1) // GROUP, step, 0)


def couple_kernel(
    m0, m1, m2, s0, s1, s2, c0, c1, c2, left, right, roots,
    out0, out1, out2, root_high, root_low,
):
    lane_cluster = lax.broadcasted_iota(jnp.int32, (8, 256), 1) // RANK
    row = lax.broadcasted_iota(jnp.int32, (8, 256), 0)
    row_wide = lax.broadcasted_iota(jnp.int32, (8, 512), 0)
    indicator = jnp.where(row_wide == lax.broadcasted_iota(jnp.int32, (8, 512), 1) // RANK, 1.0, 0.0)

    def level(mask, skel, coeff, out, place, rows, coeff_place):
        count = skel.shape[1] // RANK
        skel_lanes = slice(HALO + place * EDGE, HALO + (place + 1) * EDGE)
        coeff_lanes = slice(HALO + 3 * EDGE + coeff_place * EDGE, HALO + 3 * EDGE + (coeff_place + 1) * EDGE)
        pts = jnp.concatenate([left[:, skel_lanes], skel[...], right[:, skel_lanes]], 1)
        cof = jnp.concatenate([left[rows, coeff_lanes], coeff[...], right[rows, coeff_lanes]], 1)
        cluster = lax.broadcasted_iota(jnp.int32, (count, count * RANK), 0)
        owner = lax.broadcasted_iota(jnp.int32, (count, count * RANK), 1) // RANK
        spread = jnp.where(cluster == owner, 1.0, 0.0).astype(BF16)
        allowed = mul(mask[...].astype(F32).astype(BF16), spread)
        for group in range(count // 4):
            lanes = slice(group * 256, (group + 1) * 256)
            penalty = jnp.full((8, 256), CUT, F32)
            for column, offset in enumerate((0, 1, 3, 4)):
                linked = (row == lane_cluster + offset) & (allowed[column : column + 1, lanes] > 0.5)
                penalty = jnp.where(linked, 0.0, penalty)
            from_side, _ = augment(pts[:, group * 256 : group * 256 + 512], indicator, None)
            _, to_side = augment(skel[:, lanes], None, penalty)
            high, low = weights(mul(from_side.T, to_side))
            cof_high, cof_low = split(cof[:, group * 256 : group * 256 + 512])
            both = mul(jnp.concatenate([cof_high, cof_low], 0), high)
            out[:, lanes] = both[:RHS_DEV] + both[RHS_DEV:] + mul(cof_high, low)

    level(m0, s0, c0, out0, 0, slice(0, 32), 0)
    level(m1, s1, c1, out1, 1, slice(32, 64), 0)
    level(m2, s2, c2, out2, 2, slice(0, 32), 1)

    me = lax.axis_index("leaf")
    one_row = lax.broadcasted_iota(jnp.int32, (8, RANK), 0)
    one = jnp.where(one_row == 0, 1.0, 0.0)
    pair = roots[:, pl.ds(pl.multiple_of((me // 2) * 128, 128), 128)]
    own = jnp.where(lax.broadcasted_iota(jnp.int32, (DIM, 128), 1) // RANK == lax.rem(me, 2), pair, 0.0)
    own = own[:, :RANK] + own[:, RANK:]
    own_side = augment(own, one, None)[0].T
    for part in range(8):
        lanes = slice(part * 512, (part + 1) * 512)
        first = lax.broadcasted_iota(jnp.int32, (8, 512), 0) == 0
        cluster = part * 8 + lax.broadcasted_iota(jnp.int32, (8, 512), 1) // RANK
        penalty = jnp.where(first & (jnp.abs(cluster - me) < 2), CUT, 0.0)
        high, low = weights(mul(own_side, augment(roots[:, lanes], None, penalty)[1]))
        root_high[:, lanes] = high
        root_low[:, lanes] = low


def down_kernel(
    gathered, root_high, root_low, f0, f1, f2, lv1, lv2, root, basis, own_near, other_near, out,
    field0, field1, field2,
):
    parts = [gathered[2 * k] + gathered[2 * k + 1] for k in range(CHIPS // 2)]
    cof_high, cof_low = split(jnp.concatenate(parts, 1))
    both = mul(jnp.concatenate([cof_high, cof_low], 0), root_high[...], NT)
    top = both[:RHS_DEV] + both[RHS_DEV:] + mul(cof_high, root_low[...], NT)
    field2[...] = f2[...] + mul3(top, root[...])

    def down_level(parents, transfer, coupled, children, count):
        for parent in range(count):
            lanes = slice(parent * 128, (parent + 1) * 128)
            above = parents[:, parent * RANK : (parent + 1) * RANK]
            children[:, lanes] = coupled[:, lanes] + mul3(above, transfer[:, lanes])

    down_level(field2, lv2, f1, field1, LEAVES_DEV // 4)
    down_level(field1, lv1, f0, field0, LEAVES_DEV // 2)

    core = lax.axis_index("rhs")

    def leaf_pair(near, first_leaf, pair):
        fields = field0[:, pl.ds(pl.multiple_of(first_leaf * RANK + pair * 128, 128), 128)]
        for side in range(2):
            leaf = first_leaf + 2 * pair + side
            lanes = pl.ds(pl.multiple_of(leaf * LEAF, LEAF), LEAF)
            near_lanes = pl.ds((2 * pair + side) * LEAF, LEAF)
            far = mul3(fields[:, side * RANK : (side + 1) * RANK], basis[:, lanes])
            out[:, lanes] = near[:, near_lanes] + far

    for pair in range(HALF // 2):
        leaf_pair(own_near, core * HALF, pair)
        leaf_pair(other_near, (1 - core) * HALF, pair)


def whole(*shape):
    return pl.BlockSpec(shape, lambda step: (0,) * len(shape))


def at(shape, *index):
    return pl.BlockSpec(shape, lambda step: index)


def shapes(*dims):
    return [jax.ShapeDtypeStruct(dim, F32) for dim in dims]


def params():
    return pltpu.CompilerParams(vmem_limit_bytes=VMEM_LIMIT)


def cost(flops, bytes_accessed, transcendentals=0):
    return pl.CostEstimate(flops=flops, bytes_accessed=bytes_accessed, transcendentals=transcendentals)


SWAP = [(0, 1), (1, 0)]
RIGHT = [(i, i + 1) for i in range(CHIPS - 1)]
LEFT = [(i + 1, i) for i in range(CHIPS - 1)]


def per_device(
    points, vectors, leaf_basis, skel_lv0, skel_lv1, skel_lv2, transfer_lv1, transfer_lv2,
    transfer_root, root_skeleton_points, near_mask, far_lv0, far_lv1, far_lv2,
):
    pts, vec, basis = points.T, vectors.T, leaf_basis.T
    s0, s1, s2 = skel_lv0.T, skel_lv1.T, skel_lv2.T
    lv1, lv2, root = transfer_lv1.T, transfer_lv2.T, transfer_root.T
    roots = root_skeleton_points.T
    lanes = LEAVES_DEV * LEAF

    other_pts = lax.ppermute(pts, "rhs", SWAP)
    other_vec = lax.ppermute(vec, "rhs", SWAP)

    edge = (DIM, EDGE)
    coeff0, coeff1, coeff2, blocks, to_left, to_right = pl.pallas_call(
        up_kernel,
        out_shape=shapes(
            (RHS_DEV, 2048), (RHS_DEV, 1024), (RHS_DEV, 512), (CHIPS, RHS_DEV, 128), (DIM, MSG), (DIM, MSG)
        ),
        in_specs=[
            whole(RHS_DEV, lanes), whole(RANK, lanes), whole(RANK, 2048), whole(RANK, 1024), whole(RANK, 512),
            at((32, HALO), 0, 0), at((32, HALO), 0, lanes // HALO - 1),
            at((32, HALO), 0, 0), at((32, HALO), 0, lanes // HALO - 1),
            at(edge, 0, 0), at(edge, 0, 15), at(edge, 0, 0), at(edge, 0, 7), at(edge, 0, 0), at(edge, 0, 3),
        ],
        out_specs=[
            whole(RHS_DEV, 2048), whole(RHS_DEV, 1024), whole(RHS_DEV, 512), whole(CHIPS, RHS_DEV, 128),
            whole(DIM, MSG), whole(DIM, MSG),
        ],
        grid=(1,),
        compiler_params=params(),
        cost_estimate=cost(6 * 10**8, 6 * 10**6),
        name="up",
    )(vec, basis, lv1, lv2, root, pts, pts, vec, vec, s0, s0, s1, s1, s2, s2)

    right_own = lax.ppermute(to_left, "leaf", LEFT)
    left_own = lax.ppermute(to_right, "leaf", RIGHT)
    gathered = lax.all_to_all(blocks, "leaf", split_axis=0, concat_axis=0, tiled=True)
    right_other = lax.ppermute(right_own, "rhs", SWAP)
    left_other = lax.ppermute(left_own, "rhs", SWAP)

    anywhere = pl.BlockSpec(memory_space=pl.ANY)
    own_near, other_near = pl.pallas_call(
        near_kernel,
        out_shape=shapes((32, lanes // 2), (32, lanes // 2)),
        in_specs=[pl.BlockSpec(memory_space=pltpu.SMEM)] + [anywhere] * 8,
        scratch_shapes=[
            pltpu.VMEM((DIM, WINDOW * LEAF), F32),
            pltpu.VMEM((64, WINDOW * LEAF), F32),
            pltpu.VMEM((WINDOW + 1, LEAF, 4 * DIM), BF16),
            pltpu.VMEM((WINDOW + 1, 4 * DIM, LEAF), BF16),
            pltpu.VMEM((WINDOW + 1, 128, LEAF), BF16),
            pltpu.SMEM((HALF * (2 * REACH + 1) + GROUP,), jnp.int32),
            pltpu.SemaphoreType.DMA((8,)),
        ],
        compiler_params=params(),
        cost_estimate=cost(10**10, 5 * 10**6, 5 * 10**6),
        name="near",
    )(near_mask.T, pts, vec, other_pts, other_vec, left_own, left_other, right_own, right_other)
    other_half = lax.ppermute(other_near, "rhs", SWAP)

    f0, f1, f2, root_high, root_low = pl.pallas_call(
        couple_kernel,
        out_shape=shapes((RHS_DEV, 2048), (RHS_DEV, 1024), (RHS_DEV, 512))
        + [jax.ShapeDtypeStruct((RANK, CHIPS * RANK), BF16)] * 2,
        compiler_params=params(),
        cost_estimate=cost(2 * 10**9, 4 * 10**6, 2 * 10**6),
        name="couple",
    )(far_lv0.T, far_lv1.T, far_lv2.T, s0, s1, s2, coeff0, coeff1, coeff2, left_own, right_own, roots)

    out = pl.pallas_call(
        down_kernel,
        out_shape=jax.ShapeDtypeStruct((RHS_DEV, lanes), F32),
        scratch_shapes=[pltpu.VMEM((RHS_DEV, width), F32) for width in (2048, 1024, 512)],
        compiler_params=params(),
        cost_estimate=cost(10**9, 8 * 10**6),
        name="down",
    )(gathered, root_high, root_low, f0, f1, f2, lv1, lv2, root, basis, own_near, other_half)
    return out.T


def solution(mesh):
    split_both = P("leaf", "rhs")
    placed = (split_both, split_both) + (P("leaf", None),) * 7 + (P(),) + (P("leaf", None),) * 4
    return jax.shard_map(per_device, mesh=mesh, in_specs=placed, out_specs=split_both, check_vma=False)
```

```python
import math

import jax
import jax.numpy as jnp
from jax import lax
from jax.experimental import pallas as pl
from jax.experimental.pallas import tpu as pltpu
from jax.sharding import PartitionSpec as P

DIM = 64
RANK = 64
LEAF = 256
REACH = 4
FREACH = 2
LEAVES_DEV = 32
RHS_DEV = 32
CHIPS = 64

HALF = LEAVES_DEV // 2
WINDOW = HALF + 2 * REACH
HALO = REACH * LEAF
EDGE = FREACH * RANK
LANES = LEAVES_DEV * LEAF
GROUP = 8
SCALE = math.sqrt(2.0 / 24.0 * math.log2(math.e))
CUT = -32768.0

F32 = jnp.float32
BF16 = jnp.bfloat16

NN = (((1,), (0,)), ((), ()))
NT = (((1,), (1,)), ((), ()))


def mul(left, right, dims=NN):
    return lax.dot_general(left, right, dims, preferred_element_type=F32)


def split(x):
    high = x.astype(BF16)
    return high, (x - high.astype(F32)).astype(BF16)


def mul3(left, right, dims=NN):
    rows = left.shape[0]
    left_high, left_low = split(left)
    right_high, right_low = split(right)
    both = mul(jnp.concatenate([left_high, left_low], 0), right_high, dims)
    return both[:rows] + both[rows:] + mul(left_high, right_low, dims)


def augment(points, source_extra=None, target_extra=None):
    high, low = split(points * SCALE)
    high_f, low_f = high.astype(F32), low.astype(F32)
    norm = 0.5 * jnp.sum(high_f * (high_f + 2.0 * low_f), axis=0, keepdims=True)
    first = norm.astype(BF16).astype(F32)
    second = (norm - first).astype(BF16).astype(F32)
    third = (norm - first - second).astype(BF16).astype(F32)
    width = points.shape[1]
    row = lax.broadcasted_iota(jnp.int32, (8, width), 0)

    def rows_of(start, ones):
        picked = jnp.where(row == start, -first, 0.0)
        picked = jnp.where(row == start + 1, -second, picked)
        picked = jnp.where(row == start + 2, -third, picked)
        return jnp.where((row >= ones) & (row < ones + 3), 1.0, picked)

    nothing = jnp.zeros((8, width), F32)
    rest = jnp.zeros((DIM - 16, width), BF16)

    def block(start, ones, extra):
        tail = jnp.concatenate([rows_of(start, ones), nothing if extra is None else extra], 0)
        return tail.astype(BF16), rest

    source = jnp.concatenate([high, low, high, *block(0, 3, source_extra)], 0)
    target = jnp.concatenate([high, high, low, *block(3, 0, target_extra)], 0)
    return source, target


def weights(exponent):
    return split(jnp.exp2(exponent))


def fetch(jobs, sems):
    return [pltpu.make_async_copy(src, dst, sems.at[k]) for k, (src, dst) in enumerate(jobs)]


def edge_lanes(last, width, size):
    return pl.ds(pl.multiple_of(jnp.where(last, width - size, 0), size), size)


def up_kernel(
    vec, basis, lv1, lv2, root, pts, s0, s1, s2,
    c0, c1, c2, blocks, near_msg, cross_msg,
    vec_v, basis_v, lv1_v, lv2_v, root_v, coeff0, coeff1, coeff2, top_v, near_v, cross_v, sems, out_sems,
):
    core = lax.axis_index("rhs")
    near_last, cross_last = core == 0, core == 1
    jobs = []
    for chunk in range(4):
        lanes = pl.ds(chunk * 2048, 2048)
        jobs.append((vec.at[:, lanes], vec_v.at[:, lanes]))
        jobs.append((basis.at[:, lanes], basis_v.at[:, lanes]))
    jobs += [(lv1, lv1_v), (lv2, lv2_v), (root, root_v)]
    for place, skel in enumerate((s0, s1, s2)):
        lanes = edge_lanes(near_last, skel.shape[1], EDGE)
        jobs.append((skel.at[:, lanes], near_v.at[:, pl.ds(HALO + (2 + place) * EDGE, EDGE)]))
    for msg, last in ((near_v, near_last), (cross_v, cross_last)):
        for part, array in enumerate((pts, vec)):
            lanes = edge_lanes(last, LANES, HALO)
            jobs.append((array.at[:, lanes], msg.at[pl.ds(part * 32, 32), pl.ds(0, HALO)]))
    copies = fetch(jobs, sems)
    for copy in copies:
        copy.start()

    for chunk in range(4):
        copies[2 * chunk].wait()
        copies[2 * chunk + 1].wait()
        for pair in range(4 * chunk, 4 * chunk + 4):
            parts = []
            for side in range(2):
                lanes = slice((2 * pair + side) * LEAF, (2 * pair + side + 1) * LEAF)
                parts.append(mul3(vec_v[:, lanes], basis_v[:, lanes], NT))
            coeff0[:, pair * 128 : (pair + 1) * 128] = jnp.concatenate(parts, 1)

    def up_level(children, transfer, parents, count):
        for pair in range(count // 2):
            parts = []
            for side in range(2):
                lanes = slice((2 * pair + side) * 128, (2 * pair + side + 1) * 128)
                parts.append(mul3(children[:, lanes], transfer[:, lanes], NT))
            parents[:, pair * 128 : (pair + 1) * 128] = jnp.concatenate(parts, 1)

    copies[8].wait()
    up_level(coeff0, lv1_v, coeff1, LEAVES_DEV // 2)
    copies[9].wait()
    up_level(coeff1, lv2_v, coeff2, LEAVES_DEV // 4)
    for copy in copies[11:]:
        copy.wait()
    for msg, last in ((near_v, near_last), (cross_v, cross_last)):
        ends = [
            jnp.where(last, ref[:, ref.shape[1] - EDGE :], ref[:, :EDGE]) for ref in (coeff0, coeff1, coeff2)
        ]
        msg[:RHS_DEV, HALO : HALO + EDGE] = ends[0]
        msg[RHS_DEV:, HALO : HALO + EDGE] = ends[1]
        msg[:RHS_DEV, HALO + EDGE : HALO + 2 * EDGE] = ends[2]
        msg[RHS_DEV:, HALO + EDGE : HALO + 2 * EDGE] = jnp.zeros((RHS_DEV, EDGE), F32)
    stores = fetch(
        [
            (near_v, near_msg), (cross_v, cross_msg), (coeff0, c0), (coeff1, c1), (coeff2, c2), (top_v, blocks)
        ],
        out_sems,
    )
    for store in stores[:5]:
        store.start()
    copies[10].wait()
    top = mul3(coeff2[...], root_v[...], NT)
    twice = jnp.concatenate([top, top], 1)
    lane = lax.broadcasted_iota(jnp.int32, (RHS_DEV, 128), 1)
    parity = lax.rem(lax.axis_index("leaf"), 2)
    placed = jnp.where(lane // RANK == parity, twice, 0.0)
    top_v[...] = jnp.broadcast_to(placed[None], (CHIPS, RHS_DEV, 128))
    stores[5].start()
    for store in stores:
        store.wait()


def edge_penalty(mask, core):
    count = mask.shape[1]
    first = core == 0
    linked = [
        [jnp.where(first, mask[0, 0], mask[3, count - 2]), jnp.where(first, 0, mask[2, count - 1])],
        [jnp.where(first, mask[1, 0], 0), jnp.where(first, mask[0, 1], mask[3, count - 1])],
    ]
    row = lax.broadcasted_iota(jnp.int32, (8, EDGE), 0)
    cluster = lax.broadcasted_iota(jnp.int32, (8, EDGE), 1) // RANK
    penalty = jnp.zeros((8, EDGE), F32)
    for source in range(2):
        for target in range(2):
            value = jnp.where(linked[source][target] > 0, 0.0, CUT)
            penalty = jnp.where((row == source) & (cluster == target), value, penalty)
    return penalty


def near_kernel(
    mask_any, m0_any, m1_any, m2_any, s0, s1, s2, own_pts, own_vec, other_pts, other_vec, near_msg, cross_msg,
    own_out, other_out, win_pts, win_vec, source, target, vec_t, mask, m0, m1, m2, skel_own, skel_halo,
    ends_own, ends_other, pairs, sems,
):
    core = lax.axis_index("rhs")
    body_lanes = (WINDOW - REACH) * LEAF
    main_from = pl.multiple_of(core * (LANES - body_lanes), HALO)
    main_to = pl.multiple_of((1 - core) * HALO, HALO)
    halo_to = pl.multiple_of(core * body_lanes, HALO)
    jobs = [(mask_any, mask), (m0_any, m0), (m1_any, m1), (m2_any, m2)]
    for half, (pts, vecs, halo) in enumerate(
        ((own_pts, own_vec, near_msg), (other_pts, other_vec, cross_msg))
    ):
        rows = pl.ds(half * 32, 32)
        main = pl.ds(main_to, body_lanes)
        edge = pl.ds(halo_to, HALO)
        jobs.append((pts.at[:, pl.ds(main_from, body_lanes)], win_pts.at[rows, main]))
        jobs.append((vecs.at[:, pl.ds(main_from, body_lanes)], win_vec.at[rows, main]))
        jobs.append((halo.at[pl.ds(0, 32), pl.ds(0, HALO)], win_pts.at[rows, edge]))
        jobs.append((halo.at[pl.ds(32, 32), pl.ds(0, HALO)], win_vec.at[rows, edge]))
    ends_at = pl.ds(HALO, 2 * EDGE)
    jobs += [(near_msg.at[:, ends_at], ends_own), (cross_msg.at[:, ends_at], ends_other)]
    jobs.append((near_msg.at[:, pl.ds(HALO + 2 * EDGE, 3 * EDGE)], skel_halo))
    for place, skel in enumerate((s0, s1, s2)):
        lanes = edge_lanes(core == 1, skel.shape[1], EDGE)
        jobs.append((skel.at[:, lanes], skel_own.at[:, pl.ds(place * EDGE, EDGE)]))
    copies = fetch(jobs, sems)
    for copy in copies:
        copy.start()

    own_out[:, : LANES // 2] = jnp.zeros((32, LANES // 2), F32)
    other_out[:, : LANES // 2] = jnp.zeros((32, LANES // 2), F32)

    copies[0].wait()
    count = jnp.int32(0)
    for leaf in range(HALF):
        for offset in range(-REACH, REACH + 1):
            pairs[count] = (leaf + REACH + offset) * 32 + leaf
            if offset == 0:
                count = count + 1
            else:
                column = REACH + offset if offset < 0 else REACH + offset - 1
                count = count + mask[column, core * HALF + leaf]
    for extra in range(GROUP):
        pairs[count + extra] = WINDOW * 32

    source[WINDOW] = jnp.zeros((4 * DIM, LEAF), BF16).reshape(LEAF, 4 * DIM)
    vec_t[WINDOW] = jnp.zeros((2 * 64, LEAF), BF16)

    for copy in copies[1:]:
        copy.wait()

    def prepare(leaf, carry):
        lanes = pl.ds(pl.multiple_of(leaf * LEAF, LEAF), LEAF)
        from_side, to_side = augment(win_pts[:, lanes])
        source[leaf] = from_side.T
        target[leaf] = to_side
        vec_t[leaf] = jnp.concatenate(split(win_vec[:, lanes]), 0)
        return carry

    lax.fori_loop(0, WINDOW, prepare, 0, unroll=2)

    row = lax.broadcasted_iota(jnp.int32, (8, EDGE), 0)
    indicator = jnp.where(row == lax.broadcasted_iota(jnp.int32, (8, EDGE), 1) // RANK, 1.0, 0.0)
    for place, far_mask in enumerate((m0, m1, m2)):
        lanes = slice(place * EDGE, (place + 1) * EDGE)
        from_side, _ = augment(skel_halo[:, lanes], indicator, None)
        _, to_side = augment(skel_own[:, lanes], None, edge_penalty(far_mask, core))
        high, low = weights(mul(from_side.T, to_side))
        rows = slice(place % 2 * 32, place % 2 * 32 + 32)
        at = slice(place // 2 * EDGE, (place // 2 + 1) * EDGE)
        cof_high, cof_low = split(jnp.concatenate([ends_own[rows, at], ends_other[rows, at]], 0))
        both = mul(jnp.concatenate([cof_high, cof_low], 0), high)
        term = both[:64] + both[64:] + mul(cof_high, low)
        lanes = slice(LANES // 2 + place * EDGE, LANES // 2 + (place + 1) * EDGE)
        own_out[:, lanes] = term[:32]
        other_out[:, lanes] = term[32:]

    def step(index, carry):
        found = []
        for k in range(GROUP):
            code = pairs[index * GROUP + k]
            src, tgt = lax.shift_right_logical(code, 5), lax.bitwise_and(code, 31)
            high, low = weights(mul(source[src], target[tgt + REACH]))
            both = mul(vec_t[src], high)
            found.append((tgt, both[:64] + both[64:] + mul(vec_t[src, :64], low)))
        for tgt, term in found:
            lanes = pl.ds(pl.multiple_of(tgt * LEAF, LEAF), LEAF)
            own_out[:, lanes] += term[:32]
            other_out[:, lanes] += term[32:]
        return carry

    lax.fori_loop(0, (count + GROUP - 1) // GROUP, step, 0)


def couple_kernel(
    m0_any, m1_any, m2_any, s0_any, s1_any, s2_any, c0_any, c1_any, c2_any,
    f0, f1, f2,
    m0, m1, m2, s0, s1, s2, c0, c1, c2, out0, out1, out2, sems, out_sems,
):
    copies = fetch(
        [
            (m2_any, m2), (s2_any, s2), (c2_any, c2), (m1_any, m1), (s1_any, s1), (c1_any, c1),
            (m0_any, m0), (s0_any, s0), (c0_any, c0),
        ],
        sems,
    )
    for copy in copies:
        copy.start()
    stores = fetch([(out2, f2), (out1, f1), (out0, f0)], out_sems)
    gap = jnp.zeros((DIM, EDGE), F32)
    lane_cluster = lax.broadcasted_iota(jnp.int32, (8, 256), 1) // RANK
    row = lax.broadcasted_iota(jnp.int32, (8, 256), 0)
    row_wide = lax.broadcasted_iota(jnp.int32, (8, 512), 0)
    indicator = jnp.where(row_wide == lax.broadcasted_iota(jnp.int32, (8, 512), 1) // RANK, 1.0, 0.0)

    def level(mask, skel, coeff, out, place):
        count = skel.shape[1] // RANK
        for copy in copies[3 * place : 3 * place + 3]:
            copy.wait()
        pts = jnp.concatenate([gap, skel[...], gap], 1)
        cof = jnp.concatenate([gap[:RHS_DEV], coeff[...], gap[:RHS_DEV]], 1)
        cluster = lax.broadcasted_iota(jnp.int32, (count, count * RANK), 0)
        owner = lax.broadcasted_iota(jnp.int32, (count, count * RANK), 1) // RANK
        spread = jnp.where(cluster == owner, 1.0, 0.0).astype(BF16)
        allowed = mul(mask[...].astype(F32).astype(BF16), spread)
        for group in range(count // 4):
            lanes = slice(group * 256, (group + 1) * 256)
            penalty = jnp.full((8, 256), CUT, F32)
            for column, offset in enumerate((0, 1, 3, 4)):
                linked = (row == lane_cluster + offset) & (allowed[column : column + 1, lanes] > 0.5)
                penalty = jnp.where(linked, 0.0, penalty)
            from_side, _ = augment(pts[:, group * 256 : group * 256 + 512], indicator, None)
            _, to_side = augment(skel[:, lanes], None, penalty)
            high, low = weights(mul(from_side.T, to_side))
            cof_high, cof_low = split(cof[:, group * 256 : group * 256 + 512])
            both = mul(jnp.concatenate([cof_high, cof_low], 0), high)
            out[:, lanes] = both[:RHS_DEV] + both[RHS_DEV:] + mul(cof_high, low)

        stores[place].start()

    level(m2, s2, c2, out2, 0)
    level(m1, s1, c1, out1, 1)
    level(m0, s0, c0, out0, 2)
    for store in stores:
        store.wait()


def down_kernel(
    gathered_any, roots_any, lv1_any, lv2_any, root_any, basis_any, f0_any, f1_any, f2_any, own_any, other_any,
    out_any, field0, field1, field2, gathered, roots, lv1, lv2, root, basis, f0, f1, f2, own_near, other_near,
    out, sems, out_sems,
):
    quarter = LANES // 4
    jobs = [
        (roots_any, roots), (gathered_any, gathered), (root_any, root), (f2_any, f2), (own_any, own_near),
        (other_any, other_near), (lv2_any, lv2), (f1_any, f1), (lv1_any, lv1), (f0_any, f0),
    ]
    for chunk in range(4):
        lanes = pl.ds(chunk * quarter, quarter)
        jobs.append((basis_any.at[:, lanes], basis.at[:, lanes]))
    copies = fetch(jobs, sems)
    for copy in copies:
        copy.start()
    core = lax.axis_index("rhs")

    copies[0].wait()
    me = lax.axis_index("leaf")
    one = jnp.where(lax.broadcasted_iota(jnp.int32, (8, RANK), 0) == 0, 1.0, 0.0)
    pair = roots[:, pl.ds(pl.multiple_of((me // 2) * 128, 128), 128)]
    own = jnp.where(lax.broadcasted_iota(jnp.int32, (DIM, 128), 1) // RANK == lax.rem(me, 2), pair, 0.0)
    own_side = augment(own[:, :RANK] + own[:, RANK:], one, None)[0].T
    kernels = []
    for part in range(8):
        lanes = slice(part * 512, (part + 1) * 512)
        first = lax.broadcasted_iota(jnp.int32, (8, 512), 0) == 0
        cluster = part * 8 + lax.broadcasted_iota(jnp.int32, (8, 512), 1) // RANK
        penalty = jnp.where(first & (jnp.abs(cluster - me) < 2), CUT, 0.0)
        kernels.append(weights(mul(own_side, augment(roots[:, lanes], None, penalty)[1])))

    copies[1].wait()
    top = jnp.zeros((RHS_DEV, RANK), F32)
    for part, (high, low) in enumerate(kernels):
        pieces = [gathered[2 * k] + gathered[2 * k + 1] for k in range(4 * part, 4 * part + 4)]
        cof_high, cof_low = split(jnp.concatenate(pieces, 1))
        both = mul(jnp.concatenate([cof_high, cof_low], 0), high, NT)
        top = top + both[:RHS_DEV] + both[RHS_DEV:] + mul(cof_high, low, NT)

    for copy in copies[2:6]:
        copy.wait()

    def coupled(ref, place):
        width = ref.shape[1]
        lanes = slice(LANES // 2 + place * EDGE, LANES // 2 + (place + 1) * EDGE)
        mine, theirs = own_near[:, lanes], other_near[:, lanes]
        ref[:, :EDGE] += jnp.where(core == 0, mine, theirs)
        ref[:, width - EDGE :] += jnp.where(core == 0, theirs, mine)

    coupled(f2, 2)
    field2[...] = f2[...] + mul3(top, root[...])

    def down_level(parents, transfer, coupled, children, count):
        for parent in range(count):
            lanes = slice(parent * 128, (parent + 1) * 128)
            above = parents[:, parent * RANK : (parent + 1) * RANK]
            children[:, lanes] = coupled[:, lanes] + mul3(above, transfer[:, lanes])

    copies[6].wait()
    copies[7].wait()
    coupled(f1, 1)
    down_level(field2, lv2, f1, field1, LEAVES_DEV // 4)
    copies[8].wait()
    copies[9].wait()
    coupled(f0, 0)
    down_level(field1, lv1, f0, field0, LEAVES_DEV // 2)

    for copy in copies[10:]:
        copy.wait()
    stores = []
    for part in range(4):
        near, near_from = (own_near, other_near)[part // 2], part % 2 * quarter
        start = pl.multiple_of((core if part < 2 else 1 - core) * 2 * quarter + near_from, quarter)
        for pair in range(LEAVES_DEV // 8):
            fields = field0[:, pl.ds(pl.multiple_of(start // 4 + pair * 128, 128), 128)]
            for side in range(2):
                offset = (2 * pair + side) * LEAF
                lanes = pl.ds(pl.multiple_of(start + offset, LEAF), LEAF)
                far = mul3(fields[:, side * RANK : (side + 1) * RANK], basis[:, lanes])
                out[:, lanes] = near[:, near_from + offset : near_from + offset + LEAF] + far
        lanes = pl.ds(start, quarter)
        store = pltpu.make_async_copy(out.at[:, lanes], out_any.at[:, lanes], out_sems.at[part])
        store.start()
        stores.append(store)
    for store in stores:
        store.wait()


def shapes(*dims):
    return [jax.ShapeDtypeStruct(dim, F32) for dim in dims]


def cost(flops, bytes_accessed, transcendentals=0):
    return pl.CostEstimate(flops=flops, bytes_accessed=bytes_accessed, transcendentals=transcendentals)


SWAP = [(0, 1), (1, 0)]
NEAR_WAY = [pair for i in range(CHIPS - 1) for pair in ((2 * i, 2 * i + 2), (2 * i + 3, 2 * i + 1))]
CROSS_WAY = [pair for i in range(CHIPS - 1) for pair in ((2 * i + 1, 2 * i + 2), (2 * i + 2, 2 * i + 1))]


def call(kernel, outputs, inputs, scratch, estimate, name, out_place=pl.ANY):
    def spec(place):
        return pl.BlockSpec(memory_space=place)

    several = isinstance(outputs, list)
    return pl.pallas_call(
        kernel,
        out_shape=outputs,
        in_specs=[spec(pl.ANY)] * len(inputs),
        out_specs=[spec(out_place)] * len(outputs) if several else spec(out_place),
        scratch_shapes=scratch,
        compiler_params=pltpu.CompilerParams(vmem_limit_bytes=64 * 2**20),
        cost_estimate=estimate,
        name=name,
    )(*inputs)


def vmem(*dims):
    return [pltpu.VMEM(dim, F32) for dim in dims]


def like(*arrays):
    return [pltpu.VMEM(array.shape, array.dtype) for array in arrays]


def dma_sems(count):
    return pltpu.SemaphoreType.DMA((count,))


def up_call(vec, basis, lv1, lv2, root, pts, s0, s1, s2):
    coeffs = ((RHS_DEV, 2048), (RHS_DEV, 1024), (RHS_DEV, 512))
    return call(
        up_kernel,
        shapes(*coeffs, (CHIPS, RHS_DEV, 128), (DIM, HALO + 5 * EDGE), (DIM, HALO + 2 * EDGE)),
        (vec, basis, lv1, lv2, root, pts, s0, s1, s2),
        like(vec, basis, lv1, lv2, root)
        + vmem(*coeffs, (CHIPS, RHS_DEV, 128), (DIM, HALO + 5 * EDGE), (DIM, HALO + 2 * EDGE))
        + [dma_sems(18), dma_sems(6)],
        cost(6 * 10**8, 6 * 10**6),
        "up",
    )


def near_call(mask, m0, m1, m2, s0, s1, s2, pts, vec, other_pts, other_vec, near_msg, cross_msg):
    width = LANES // 2 + 3 * EDGE
    return call(
        near_kernel,
        shapes((32, width), (32, width)),
        (mask, m0, m1, m2, s0, s1, s2, pts, vec, other_pts, other_vec, near_msg, cross_msg),
        vmem((DIM, WINDOW * LEAF), (64, WINDOW * LEAF))
        + [
            pltpu.VMEM((WINDOW + 1, LEAF, 4 * DIM), BF16),
            pltpu.VMEM((WINDOW + 1, 4 * DIM, LEAF), BF16),
            pltpu.VMEM((WINDOW + 1, 128, LEAF), BF16),
        ]
        + [pltpu.SMEM(array.shape, jnp.int32) for array in (mask, m0, m1, m2)]
        + vmem((DIM, 3 * EDGE), (DIM, 3 * EDGE), (DIM, 2 * EDGE), (DIM, 2 * EDGE))
        + [pltpu.SMEM((HALF * (2 * REACH + 1) + GROUP,), jnp.int32), dma_sems(18)],
        cost(10**10, 5 * 10**6, 5 * 10**6),
        "near",
        pltpu.MemorySpace.VMEM,
    )


def couple_call(m0, m1, m2, s0, s1, s2, c0, c1, c2):
    coeffs = (c0, c1, c2)
    return call(
        couple_kernel,
        shapes(*[c.shape for c in coeffs]),
        (m0, m1, m2, s0, s1, s2, *coeffs),
        like(m0, m1, m2, s0, s1, s2, *coeffs, *coeffs) + [dma_sems(9), dma_sems(3)],
        cost(2 * 10**9, 4 * 10**6, 2 * 10**6),
        "couple",
    )


def down_call(gathered, roots, lv1, lv2, root, basis, f0, f1, f2, own_near, other_near):
    inputs = (gathered, roots, lv1, lv2, root, basis, f0, f1, f2, own_near, other_near)
    return call(
        down_kernel,
        jax.ShapeDtypeStruct((RHS_DEV, LANES), F32),
        inputs,
        like(f0, f1, f2, *inputs) + vmem((RHS_DEV, LANES)) + [dma_sems(14), dma_sems(4)],
        cost(2 * 10**9, 8 * 10**6),
        "down",
    )


def per_device(
    points, vectors, leaf_basis, skel_lv0, skel_lv1, skel_lv2, transfer_lv1, transfer_lv2,
    transfer_root, root_skeleton_points, near_mask, far_lv0, far_lv1, far_lv2,
):
    pts, vec, basis = points.T, vectors.T, leaf_basis.T
    skels = (skel_lv0.T, skel_lv1.T, skel_lv2.T)
    lv1, lv2, root = transfer_lv1.T, transfer_lv2.T, transfer_root.T
    far = (far_lv0.T, far_lv1.T, far_lv2.T)
    both = ("leaf", "rhs")

    other_pts = lax.ppermute(pts, "rhs", SWAP)
    other_vec = lax.ppermute(vec, "rhs", SWAP)
    *coeffs, blocks, near_msg, cross_msg = up_call(vec, basis, lv1, lv2, root, pts, *skels)
    near_msg = lax.ppermute(near_msg, both, NEAR_WAY)
    cross_msg = lax.ppermute(cross_msg, both, CROSS_WAY)
    gathered = lax.all_to_all(blocks, "leaf", split_axis=0, concat_axis=0, tiled=True)
    own_near, other_near = near_call(
        near_mask.T, *far, *skels, pts, vec, other_pts, other_vec, near_msg, cross_msg
    )
    other_near = lax.ppermute(other_near, "rhs", SWAP)
    fields = couple_call(*far, *skels, *coeffs)
    return down_call(
        gathered, root_skeleton_points.T, lv1, lv2, root, basis, *fields, own_near, other_near
    ).T


def solution(mesh):
    split_both = P("leaf", "rhs")
    placed = (split_both, split_both) + (P("leaf", None),) * 7 + (P(),) + (P("leaf", None),) * 4
    return jax.shard_map(per_device, mesh=mesh, in_specs=placed, out_specs=split_both, check_vma=False)
```

```python
import math

import jax
import jax.numpy as jnp
from jax import lax
from jax.experimental import pallas as pl
from jax.experimental.pallas import tpu as pltpu
from jax.sharding import PartitionSpec as P

DIM = 64
RANK = 64
LEAF = 256
REACH = 4
FREACH = 2
LEAVES_DEV = 32
RHS_DEV = 32
CHIPS = 64

HALF = LEAVES_DEV // 2
WINDOW = HALF + 2 * REACH
HALO = REACH * LEAF
EDGE = FREACH * RANK
LANES = LEAVES_DEV * LEAF
NEAR_OUT = HALF * LEAF + 3 * EDGE
CUT_AT = HALF * LEAF // 2
GROUP = 32
REST = 8
SCALE = math.sqrt(2.0 / 24.0 * math.log2(math.e))
CUT = -32768.0

F32 = jnp.float32
BF16 = jnp.bfloat16

NN = (((1,), (0,)), ((), ()))
NT = (((1,), (1,)), ((), ()))


def mul(left, right, dims=NN):
    return lax.dot_general(left, right, dims, preferred_element_type=F32)


def split(x):
    high = x.astype(BF16)
    return high, (x - high.astype(F32)).astype(BF16)


def mul3(left, right, dims=NN):
    rows = left.shape[0]
    left_high, left_low = split(left)
    right_high, right_low = split(right)
    both = mul(jnp.concatenate([left_high, left_low], 0), right_high, dims)
    return both[:rows] + both[rows:] + mul(left_high, right_low, dims)


def augment(points, source_extra=None, target_extra=None):
    high, low = split(points * SCALE)
    high_f, low_f = high.astype(F32), low.astype(F32)
    norm = 0.5 * jnp.sum(high_f * (high_f + 2.0 * low_f), axis=0, keepdims=True)
    first = norm.astype(BF16).astype(F32)
    second = (norm - first).astype(BF16).astype(F32)
    third = (norm - first - second).astype(BF16).astype(F32)
    width = points.shape[1]
    row = lax.broadcasted_iota(jnp.int32, (8, width), 0)

    def rows_of(start, ones):
        picked = jnp.where(row == start, -first, 0.0)
        picked = jnp.where(row == start + 1, -second, picked)
        picked = jnp.where(row == start + 2, -third, picked)
        return jnp.where((row >= ones) & (row < ones + 3), 1.0, picked)

    nothing = jnp.zeros((8, width), F32)
    rest = jnp.zeros((DIM - 16, width), BF16)

    def block(start, ones, extra):
        tail = jnp.concatenate([rows_of(start, ones), nothing if extra is None else extra], 0)
        return tail.astype(BF16), rest

    source = jnp.concatenate([high, low, high, *block(0, 3, source_extra)], 0)
    target = jnp.concatenate([high, high, low, *block(3, 0, target_extra)], 0)
    return source, target


def weights(exponent):
    return split(jnp.exp2(exponent))


def fetch(jobs, sems):
    return [pltpu.make_async_copy(src, dst, sems.at[k]) for k, (src, dst) in enumerate(jobs)]


def edge_lanes(last, width, size):
    return pl.ds(pl.multiple_of(jnp.where(last, width - size, 0), size), size)


def up_kernel(
    vec, basis, lv1, lv2, root, pts, s0, s1, s2,
    c0, c1, c2, blocks, near_msg, cross_msg,
    vec_v, basis_v, lv1_v, lv2_v, root_v, coeff0, coeff1, coeff2, top_v, near_v, cross_v, sems, out_sems,
):
    core = lax.axis_index("rhs")
    near_last, cross_last = core == 0, core == 1
    jobs = []
    for chunk in range(2):
        lanes = pl.ds(chunk * 4096, 4096)
        jobs.append((vec.at[:, lanes], vec_v.at[:, lanes]))
        jobs.append((basis.at[:, lanes], basis_v.at[:, lanes]))
    jobs += [(lv1, lv1_v), (lv2, lv2_v), (root, root_v)]
    for place, skel in enumerate((s0, s1, s2)):
        lanes = edge_lanes(near_last, skel.shape[1], EDGE)
        jobs.append((skel.at[:, lanes], near_v.at[:, pl.ds(HALO + (2 + place) * EDGE, EDGE)]))
    for msg, last in ((near_v, near_last), (cross_v, cross_last)):
        for part, array in enumerate((pts, vec)):
            lanes = edge_lanes(last, LANES, HALO)
            jobs.append((array.at[:, lanes], msg.at[pl.ds(part * 32, 32), pl.ds(0, HALO)]))
    copies = fetch(jobs, sems)
    for copy in copies:
        copy.start()

    for chunk in range(2):
        copies[2 * chunk].wait()
        copies[2 * chunk + 1].wait()
        for pair in range(8 * chunk, 8 * chunk + 8):
            parts = []
            for side in range(2):
                lanes = slice((2 * pair + side) * LEAF, (2 * pair + side + 1) * LEAF)
                parts.append(mul3(vec_v[:, lanes], basis_v[:, lanes], NT))
            coeff0[:, pair * 128 : (pair + 1) * 128] = jnp.concatenate(parts, 1)

    def up_level(children, transfer, parents, count):
        for pair in range(count // 2):
            parts = []
            for side in range(2):
                lanes = slice((2 * pair + side) * 128, (2 * pair + side + 1) * 128)
                parts.append(mul3(children[:, lanes], transfer[:, lanes], NT))
            parents[:, pair * 128 : (pair + 1) * 128] = jnp.concatenate(parts, 1)

    for copy in copies[7:]:
        copy.wait()
    body, ends_at, skel_at = pl.ds(0, HALO), pl.ds(HALO, 2 * EDGE), pl.ds(HALO + 2 * EDGE, 3 * EDGE)
    stores = fetch(
        [
            (near_v.at[:, body], near_msg.at[:, body]), (cross_v.at[:, body], cross_msg.at[:, body]),
            (near_v.at[:, skel_at], near_msg.at[:, skel_at]), (coeff0, c0), (coeff1, c1), (coeff2, c2),
            (near_v.at[:, ends_at], near_msg.at[:, ends_at]),
            (cross_v.at[:, ends_at], cross_msg.at[:, ends_at]), (top_v, blocks),
        ],
        out_sems,
    )
    for store in stores[:4]:
        store.start()
    copies[4].wait()
    up_level(coeff0, lv1_v, coeff1, LEAVES_DEV // 2)
    copies[5].wait()
    up_level(coeff1, lv2_v, coeff2, LEAVES_DEV // 4)
    for msg, last in ((near_v, near_last), (cross_v, cross_last)):
        ends = [
            jnp.where(last, ref[:, ref.shape[1] - EDGE :], ref[:, :EDGE]) for ref in (coeff0, coeff1, coeff2)
        ]
        msg[:RHS_DEV, HALO : HALO + EDGE] = ends[0]
        msg[RHS_DEV:, HALO : HALO + EDGE] = ends[1]
        msg[:RHS_DEV, HALO + EDGE : HALO + 2 * EDGE] = ends[2]
        msg[RHS_DEV:, HALO + EDGE : HALO + 2 * EDGE] = jnp.zeros((RHS_DEV, EDGE), F32)
    for store in stores[4:8]:
        store.start()
    copies[6].wait()
    top = mul3(coeff2[...], root_v[...], NT)
    packed = jnp.concatenate([top[: RHS_DEV // 2], top[RHS_DEV // 2 :]], 1)
    top_v[...] = jnp.broadcast_to(packed[None], (CHIPS, RHS_DEV // 2, 2 * RANK))
    stores[8].start()
    for store in stores:
        store.wait()


def edge_penalty(mask, core):
    count = mask.shape[1]
    first = core == 0
    linked = [
        [jnp.where(first, mask[0, 0], mask[3, count - 2]), jnp.where(first, 0, mask[2, count - 1])],
        [jnp.where(first, mask[1, 0], 0), jnp.where(first, mask[0, 1], mask[3, count - 1])],
    ]
    row = lax.broadcasted_iota(jnp.int32, (8, EDGE), 0)
    cluster = lax.broadcasted_iota(jnp.int32, (8, EDGE), 1) // RANK
    penalty = jnp.zeros((8, EDGE), F32)
    for source in range(2):
        for target in range(2):
            value = jnp.where(linked[source][target] > 0, 0.0, CUT)
            penalty = jnp.where((row == source) & (cluster == target), value, penalty)
    return penalty


def near_kernel(
    mask_any, m0_any, m1_any, m2_any, s0, s1_any, s2_any, c1_any, c2_any, own_pts, own_vec, other_pts, other_vec,
    near_msg, cross_msg, own_any, first_any, rest_any, f1_any, f2_any,
    own_out, other_out, f1, f2, m1_v, m2_v, s1, s2, c1, c2, win_pts, win_vec, source, target, vec_t, mask, m0, m1, m2, skel_own, skel_halo,
    ends_own, ends_other, pairs, sems, out_sems,
):
    core = lax.axis_index("rhs")
    body_lanes = (WINDOW - REACH) * LEAF
    main_from = pl.multiple_of(core * (LANES - body_lanes), HALO)
    main_to = pl.multiple_of((1 - core) * HALO, HALO)
    halo_to = pl.multiple_of(core * body_lanes, HALO)
    jobs = [(mask_any, mask), (m0_any, m0), (m1_any, m1), (m2_any, m2)]
    jobs += [(m1_any, m1_v), (s1_any, s1), (c1_any, c1), (m2_any, m2_v), (s2_any, s2), (c2_any, c2)]
    for half, (pts, vecs, halo) in enumerate(
        ((own_pts, own_vec, near_msg), (other_pts, other_vec, cross_msg))
    ):
        rows = pl.ds(half * 32, 32)
        main = pl.ds(main_to, body_lanes)
        edge = pl.ds(halo_to, HALO)
        jobs.append((pts.at[:, pl.ds(main_from, body_lanes)], win_pts.at[rows, main]))
        jobs.append((vecs.at[:, pl.ds(main_from, body_lanes)], win_vec.at[rows, main]))
        jobs.append((halo.at[pl.ds(0, 32), pl.ds(0, HALO)], win_pts.at[rows, edge]))
        jobs.append((halo.at[pl.ds(32, 32), pl.ds(0, HALO)], win_vec.at[rows, edge]))
    ends_at = pl.ds(HALO, 2 * EDGE)
    jobs += [(near_msg.at[:, ends_at], ends_own), (cross_msg.at[:, ends_at], ends_other)]
    jobs.append((near_msg.at[:, pl.ds(HALO + 2 * EDGE, 3 * EDGE)], skel_halo))
    for place, skel in enumerate((s0, s1_any, s2_any)):
        lanes = edge_lanes(core == 1, skel.shape[1], EDGE)
        jobs.append((skel.at[:, lanes], skel_own.at[:, pl.ds(place * EDGE, EDGE)]))
    copies = fetch(jobs, sems)
    for copy in copies:
        copy.start()

    own_out[:, : LANES // 2] = jnp.zeros((32, LANES // 2), F32)
    other_out[:, : LANES // 2] = jnp.zeros((32, LANES // 2), F32)

    copies[0].wait()
    count = jnp.int32(0)
    for leaf in range(HALF):
        for offset in range(-REACH, REACH + 1):
            pairs[count] = (leaf + REACH + offset) * 32 + leaf
            if offset == 0:
                count = count + 1
            else:
                column = REACH + offset if offset < 0 else REACH + offset - 1
                count = count + mask[column, core * HALF + leaf]
    for extra in range(REST):
        pairs[count + extra] = WINDOW * 32

    source[WINDOW] = jnp.zeros((4 * DIM, LEAF), BF16).reshape(LEAF, 4 * DIM)
    vec_t[WINDOW] = jnp.zeros((2 * 64, LEAF), BF16)

    for copy in copies[4:10]:
        copy.wait()
    couple_level(m2_v, s2, c2, f2)
    couple_level(m1_v, s1, c1, f1)
    stores = fetch(
        [
            (f1, f1_any), (f2, f2_any), (own_out, own_any), (other_out.at[:, pl.ds(0, CUT_AT)], first_any),
            (other_out.at[:, pl.ds(CUT_AT, NEAR_OUT - CUT_AT)], rest_any),
        ],
        out_sems,
    )
    for store in stores[:2]:
        store.start()
    for copy in copies[1:4] + copies[10:]:
        copy.wait()

    for leaf in range(WINDOW):
        lanes = slice(leaf * LEAF, (leaf + 1) * LEAF)
        from_side, to_side = augment(win_pts[:, lanes])
        source[leaf] = from_side.T
        if REACH <= leaf < WINDOW - REACH:
            target[leaf - REACH] = to_side
        vec_t[leaf] = jnp.concatenate(split(win_vec[:, lanes]), 0)

    row = lax.broadcasted_iota(jnp.int32, (8, EDGE), 0)
    indicator = jnp.where(row == lax.broadcasted_iota(jnp.int32, (8, EDGE), 1) // RANK, 1.0, 0.0)
    for place, far_mask in enumerate((m0, m1, m2)):
        lanes = slice(place * EDGE, (place + 1) * EDGE)
        from_side, _ = augment(skel_halo[:, lanes], indicator, None)
        _, to_side = augment(skel_own[:, lanes], None, edge_penalty(far_mask, core))
        high, low = weights(mul(from_side.T, to_side))
        rows = slice(place % 2 * 32, place % 2 * 32 + 32)
        at = slice(place // 2 * EDGE, (place // 2 + 1) * EDGE)
        cof_high, cof_low = split(jnp.concatenate([ends_own[rows, at], ends_other[rows, at]], 0))
        both = mul(jnp.concatenate([cof_high, cof_low], 0), high)
        term = both[:64] + both[64:] + mul(cof_high, low)
        lanes = slice(LANES // 2 + place * EDGE, LANES // 2 + (place + 1) * EDGE)
        own_out[:, lanes] = term[:32]
        other_out[:, lanes] = term[32:]

    def steps(start, size, number):
        def step(index, carry):
            found = []
            for k in range(size):
                code = pairs[start + index * size + k]
                src, tgt = lax.shift_right_logical(code, 5), lax.bitwise_and(code, 31)
                high, low = weights(mul(source[src], target[tgt]))
                both = mul(vec_t[src], high)
                found.append((tgt, both[:64] + both[64:] + mul(vec_t[src, :64], low)))
            for tgt, term in found:
                lanes = pl.ds(pl.multiple_of(tgt * LEAF, LEAF), LEAF)
                own_out[:, lanes] += term[:32]
                other_out[:, lanes] += term[32:]
            return carry

        lax.fori_loop(0, number, step, 0)

    full = count // GROUP
    steps(0, GROUP, full)
    steps(full * GROUP, REST, (count - full * GROUP + REST - 1) // REST)
    for store in stores[2:]:
        store.start()
    for store in stores:
        store.wait()


def couple_level(mask, skel, coeff, out):
    width = skel.shape[1]
    count = width // RANK
    cluster = lax.broadcasted_iota(jnp.int32, (count, width), 0)
    owner = lax.broadcasted_iota(jnp.int32, (count, width), 1) // RANK
    spread = jnp.where(cluster == owner, 1.0, 0.0).astype(BF16)
    allowed = mul(mask[...].astype(F32).astype(BF16), spread)
    row = lax.broadcasted_iota(jnp.int32, (8, width), 0)
    owner = lax.broadcasted_iota(jnp.int32, (8, width), 1) // RANK
    penalty = jnp.full((8, width), CUT, F32)
    for column, offset in enumerate((-2, -1, 1, 2)):
        linked = (row == lax.bitwise_and(owner + offset, 7)) & (allowed[column : column + 1] > 0.5)
        penalty = jnp.where(linked, 0.0, penalty)
    target = augment(skel[...], None, penalty)[1]

    wide = width + 2 * EDGE
    row = lax.broadcasted_iota(jnp.int32, (8, wide), 0)
    owner = lax.broadcasted_iota(jnp.int32, (8, wide), 1) // RANK - FREACH
    indicator = jnp.where(row == lax.bitwise_and(owner, 7), 1.0, 0.0)
    gap = jnp.zeros((DIM, EDGE), F32)
    source = augment(jnp.concatenate([gap, skel[...], gap], 1), indicator, None)[0]
    source = [source[:, k * 256 : (k + 1) * 256].T for k in range(wide // 256)]
    gap = gap[:RHS_DEV]
    cof_high, cof_low = split(jnp.concatenate([gap, coeff[...], gap], 1))
    cof = jnp.concatenate([cof_high, cof_low], 0)
    for group in range(count // 4):
        lanes = slice(group * 256, (group + 1) * 256)
        around = slice(group * 256, group * 256 + 512)
        high, low = weights(mul(jnp.concatenate(source[group : group + 2], 0), target[:, lanes]))
        both = mul(cof[:, around], high)
        out[:, lanes] = both[:RHS_DEV] + both[RHS_DEV:] + mul(cof_high[:, around], low)


def down_kernel(
    gathered_any, roots_any, m0_any, s0_any, c0_any, lv1_any, lv2_any, root_any, basis_any, f1_any, f2_any, own_any,
    first_any, rest_any, out_any, f0, field0, field1, field2, gathered, roots, m0, s0, c0, lv1, lv2, root, basis, f1, f2,
    own_near, other_near, out, sems, out_sems,
):
    core = lax.axis_index("rhs")
    quarter = LANES // 4
    copies = fetch(
        [
            (roots_any, roots), (m0_any, m0), (s0_any, s0), (c0_any, c0), (gathered_any, gathered),
            (root_any, root), (f2_any, f2), (own_any, own_near),
            (first_any, other_near.at[:, pl.ds(0, CUT_AT)]),
            (rest_any, other_near.at[:, pl.ds(CUT_AT, NEAR_OUT - CUT_AT)]), (lv2_any, lv2), (f1_any, f1), (lv1_any, lv1), (basis_any, basis),
        ],
        sems,
    )
    for copy in copies:
        copy.start()

    for copy in copies[:4]:
        copy.wait()
    me = lax.axis_index("leaf")
    one = jnp.where(lax.broadcasted_iota(jnp.int32, (8, RANK), 0) == 0, 1.0, 0.0)
    pair = roots[:, pl.ds(pl.multiple_of((me // 2) * 128, 128), 128)]
    own = jnp.where(lax.broadcasted_iota(jnp.int32, (DIM, 128), 1) // RANK == lax.rem(me, 2), pair, 0.0)
    own_side = augment(own[:, :RANK] + own[:, RANK:], one, None)[0].T
    kernels = []
    for part in range(8):
        lanes = slice(part * 512, (part + 1) * 512)
        first = lax.broadcasted_iota(jnp.int32, (8, 512), 0) == 0
        cluster = part * 8 + lax.broadcasted_iota(jnp.int32, (8, 512), 1) // RANK
        penalty = jnp.where(first & (jnp.abs(cluster - me) < 2), CUT, 0.0)
        kernels.append(weights(mul(own_side, augment(roots[:, lanes], None, penalty)[1])))
    couple_level(m0, s0, c0, f0)

    for copy in copies[4:]:
        copy.wait()
    top = jnp.zeros((RHS_DEV, RANK), F32)
    for part, (high, low) in enumerate(kernels):
        pieces = []
        for chip in range(8 * part, 8 * part + 8):
            pieces.append(jnp.concatenate([gathered[chip, :, :RANK], gathered[chip, :, RANK:]], 0))
        cof_high, cof_low = split(jnp.concatenate(pieces, 1))
        both = mul(jnp.concatenate([cof_high, cof_low], 0), high, NT)
        top = top + both[:RHS_DEV] + both[RHS_DEV:] + mul(cof_high, low, NT)

    def coupled(ref, place):
        width = ref.shape[1]
        lanes = slice(LANES // 2 + place * EDGE, LANES // 2 + (place + 1) * EDGE)
        mine, theirs = own_near[:, lanes], other_near[:, lanes]
        ref[:, :EDGE] += jnp.where(core == 0, mine, theirs)
        ref[:, width - EDGE :] += jnp.where(core == 0, theirs, mine)

    coupled(f2, 2)
    field2[...] = f2[...] + mul3(top, root[...])

    def down_level(parents, transfer, coupled, children, count):
        for parent in range(count):
            lanes = slice(parent * 128, (parent + 1) * 128)
            above = parents[:, parent * RANK : (parent + 1) * RANK]
            children[:, lanes] = coupled[:, lanes] + mul3(above, transfer[:, lanes])

    coupled(f1, 1)
    down_level(field2, lv2, f1, field1, LEAVES_DEV // 4)
    coupled(f0, 0)
    down_level(field1, lv1, f0, field0, LEAVES_DEV // 2)

    stores = []
    for part in range(4):
        near, near_from = (own_near, other_near)[part // 2], part % 2 * quarter
        start = pl.multiple_of((core if part < 2 else 1 - core) * 2 * quarter + near_from, quarter)
        for pair in range(LEAVES_DEV // 8):
            fields = field0[:, pl.ds(pl.multiple_of(start // 4 + pair * 128, 128), 128)]
            for side in range(2):
                offset = (2 * pair + side) * LEAF
                lanes = pl.ds(pl.multiple_of(start + offset, LEAF), LEAF)
                far = mul3(fields[:, side * RANK : (side + 1) * RANK], basis[:, lanes])
                out[:, lanes] = near[:, near_from + offset : near_from + offset + LEAF] + far
        lanes = pl.ds(start, quarter)
        store = pltpu.make_async_copy(out.at[:, lanes], out_any.at[:, lanes], out_sems.at[part])
        store.start()
        stores.append(store)
    for store in stores:
        store.wait()


def shapes(*dims):
    return [jax.ShapeDtypeStruct(dim, F32) for dim in dims]


def cost(flops, bytes_accessed, transcendentals=0):
    return pl.CostEstimate(flops=flops, bytes_accessed=bytes_accessed, transcendentals=transcendentals)


SWAP = [(0, 1), (1, 0)]
NEAR_WAY = [pair for i in range(CHIPS - 1) for pair in ((2 * i, 2 * i + 2), (2 * i + 3, 2 * i + 1))]
CROSS_WAY = [pair for i in range(CHIPS - 1) for pair in ((2 * i + 1, 2 * i + 2), (2 * i + 2, 2 * i + 1))]


def call(kernel, outputs, inputs, scratch, estimate, name):
    def spec(place):
        return pl.BlockSpec(memory_space=place)

    several = isinstance(outputs, list)
    return pl.pallas_call(
        kernel,
        out_shape=outputs,
        in_specs=[spec(pl.ANY)] * len(inputs),
        out_specs=[spec(pl.ANY)] * len(outputs) if several else spec(pl.ANY),
        scratch_shapes=scratch,
        compiler_params=pltpu.CompilerParams(vmem_limit_bytes=64 * 2**20),
        cost_estimate=estimate,
        name=name,
    )(*inputs)


def vmem(*dims):
    return [pltpu.VMEM(dim, F32) for dim in dims]


def like(*arrays):
    return [pltpu.VMEM(array.shape, array.dtype) for array in arrays]


def dma_sems(count):
    return pltpu.SemaphoreType.DMA((count,))


def up_call(vec, basis, lv1, lv2, root, pts, s0, s1, s2):
    coeffs = ((RHS_DEV, 2048), (RHS_DEV, 1024), (RHS_DEV, 512))
    return call(
        up_kernel,
        shapes(*coeffs, (CHIPS, RHS_DEV // 2, 2 * RANK), (DIM, HALO + 5 * EDGE), (DIM, HALO + 2 * EDGE)),
        (vec, basis, lv1, lv2, root, pts, s0, s1, s2),
        like(vec, basis, lv1, lv2, root)
        + vmem(*coeffs, (CHIPS, RHS_DEV // 2, 2 * RANK), (DIM, HALO + 5 * EDGE), (DIM, HALO + 2 * EDGE))
        + [dma_sems(14), dma_sems(9)],
        cost(6 * 10**8, 6 * 10**6),
        "up",
    )


def near_call(mask, m0, m1, m2, s0, s1, s2, c1, c2, pts, vec, other_pts, other_vec, near_msg, cross_msg):
    return call(
        near_kernel,
        shapes((32, NEAR_OUT), (32, CUT_AT), (32, NEAR_OUT - CUT_AT), c1.shape, c2.shape),
        (mask, m0, m1, m2, s0, s1, s2, c1, c2, pts, vec, other_pts, other_vec, near_msg, cross_msg),
        vmem((32, NEAR_OUT), (32, NEAR_OUT))
        + like(c1, c2, m1, m2, s1, s2, c1, c2)
        + vmem((DIM, WINDOW * LEAF), (64, WINDOW * LEAF))
        + [
            pltpu.VMEM((WINDOW + 1, LEAF, 4 * DIM), BF16),
            pltpu.VMEM((HALF, 4 * DIM, LEAF), BF16),
            pltpu.VMEM((WINDOW + 1, 128, LEAF), BF16),
        ]
        + [pltpu.SMEM(array.shape, jnp.int32) for array in (mask, m0, m1, m2)]
        + vmem((DIM, 3 * EDGE), (DIM, 3 * EDGE), (DIM, 2 * EDGE), (DIM, 2 * EDGE))
        + [pltpu.SMEM((HALF * (2 * REACH + 1) + REST,), jnp.int32), dma_sems(24), dma_sems(5)],
        cost(10**10, 5 * 10**6, 5 * 10**6),
        "near",
    )


def down_call(gathered, roots, m0, s0, c0, lv1, lv2, root, basis, f1, f2, own_near, first, rest):
    inputs = (gathered, roots, m0, s0, c0, lv1, lv2, root, basis, f1, f2, own_near, first, rest)
    return call(
        down_kernel,
        jax.ShapeDtypeStruct((RHS_DEV, LANES), F32),
        inputs,
        like(c0, c0, f1, f2, *inputs[:-2], own_near) + vmem((RHS_DEV, LANES)) + [dma_sems(14), dma_sems(4)],
        cost(2 * 10**9, 8 * 10**6),
        "down",
    )


def per_device(
    points, vectors, leaf_basis, skel_lv0, skel_lv1, skel_lv2, transfer_lv1, transfer_lv2,
    transfer_root, root_skeleton_points, near_mask, far_lv0, far_lv1, far_lv2,
):
    pts, vec, basis = points.T, vectors.T, leaf_basis.T
    skels = (skel_lv0.T, skel_lv1.T, skel_lv2.T)
    lv1, lv2, root = transfer_lv1.T, transfer_lv2.T, transfer_root.T
    far = (far_lv0.T, far_lv1.T, far_lv2.T)
    both = ("leaf", "rhs")

    other_pts = lax.ppermute(pts, "rhs", SWAP)
    other_vec = lax.ppermute(vec, "rhs", SWAP)
    c0, c1, c2, blocks, near_msg, cross_msg = up_call(vec, basis, lv1, lv2, root, pts, *skels)
    near_msg = lax.ppermute(near_msg, both, NEAR_WAY)
    cross_msg = lax.ppermute(cross_msg, both, CROSS_WAY)
    gathered = lax.all_to_all(blocks, "leaf", split_axis=0, concat_axis=0, tiled=True)
    own_near, first, rest, f1, f2 = near_call(
        near_mask.T, *far, *skels, c1, c2, pts, vec, other_pts, other_vec, near_msg, cross_msg
    )
    first = lax.ppermute(first, "rhs", SWAP)
    rest = lax.ppermute(rest, "rhs", SWAP)
    return down_call(
        gathered, root_skeleton_points.T, far[0], skels[0], c0, lv1, lv2, root, basis, f1, f2, own_near, first, rest
    ).T


def solution(mesh):
    split_both = P("leaf", "rhs")
    placed = (split_both, split_both) + (P("leaf", None),) * 7 + (P(),) + (P("leaf", None),) * 4
    return jax.shard_map(per_device, mesh=mesh, in_specs=placed, out_specs=split_both, check_vma=False)
```

```python
import math

import jax
import jax.numpy as jnp
from jax import lax
from jax.experimental import pallas as pl
from jax.experimental.pallas import tpu as pltpu
from jax.sharding import PartitionSpec as P

DIM = 64
RANK = 64
LEAF = 256
REACH = 4
FREACH = 2
LEAVES_DEV = 32
RHS_DEV = 32
CHIPS = 64

HALF = LEAVES_DEV // 2
WINDOW = HALF + 2 * REACH
HALO = REACH * LEAF
EDGE = FREACH * RANK
LANES = LEAVES_DEV * LEAF
NEAR_OUT = HALF * LEAF + 3 * EDGE
CUT_AT = HALF * LEAF // 2
GROUP = 32
REST = 8
SCALE = math.sqrt(2.0 / 24.0 * math.log2(math.e))
CUT = -32768.0

F32 = jnp.float32
BF16 = jnp.bfloat16

NN = (((1,), (0,)), ((), ()))
NT = (((1,), (1,)), ((), ()))


def mul(left, right, dims=NN):
    return lax.dot_general(left, right, dims, preferred_element_type=F32)


def split(x):
    high = x.astype(BF16)
    return high, (x - high.astype(F32)).astype(BF16)


def mul3(left, right, dims=NN):
    rows = left.shape[0]
    left_high, left_low = split(left)
    right_high, right_low = split(right)
    both = mul(jnp.concatenate([left_high, left_low], 0), right_high, dims)
    return both[:rows] + both[rows:] + mul(left_high, right_low, dims)


def low_lanes(rows):
    return lax.broadcasted_iota(jnp.int32, (rows, 2 * RANK), 1) < RANK


def stack(x):
    return jnp.concatenate(split(x), 0)


def pair_products(pair, rights):
    turned = pltpu.roll(pair, RANK, 1)
    rows = pair.shape[0]
    low = low_lanes(rows)
    out = []
    for left, right in zip((jnp.where(low, pair, turned), jnp.where(low, turned, pair)), rights):
        both = mul(stack(left), stack(right))
        out.append(both[:rows] + both[rows:])
    return out


def augment(points, source_extra=None, target_extra=None):
    high, low = split(points * SCALE)
    high_f, low_f = high.astype(F32), low.astype(F32)
    norm = 0.5 * jnp.sum(high_f * (high_f + 2.0 * low_f), axis=0, keepdims=True)
    first = norm.astype(BF16).astype(F32)
    second = (norm - first).astype(BF16).astype(F32)
    third = (norm - first - second).astype(BF16).astype(F32)
    width = points.shape[1]
    row = lax.broadcasted_iota(jnp.int32, (8, width), 0)

    def rows_of(start, ones):
        picked = jnp.where(row == start, -first, 0.0)
        picked = jnp.where(row == start + 1, -second, picked)
        picked = jnp.where(row == start + 2, -third, picked)
        return jnp.where((row >= ones) & (row < ones + 3), 1.0, picked)

    nothing = jnp.zeros((8, width), F32)
    rest = jnp.zeros((DIM - 16, width), BF16)

    def block(start, ones, extra):
        tail = jnp.concatenate([rows_of(start, ones), nothing if extra is None else extra], 0)
        return tail.astype(BF16), rest

    source = jnp.concatenate([high, low, high, *block(0, 3, source_extra)], 0)
    target = jnp.concatenate([high, high, low, *block(3, 0, target_extra)], 0)
    return source, target


def weights(exponent):
    return split(jnp.exp2(exponent))


def fetch(jobs, sems):
    return [pltpu.make_async_copy(src, dst, sems.at[k]) for k, (src, dst) in enumerate(jobs)]


def edge_lanes(last, width, size):
    return pl.ds(pl.multiple_of(jnp.where(last, width - size, 0), size), size)


def up_kernel(
    vec, basis, lv1, lv2, root, pts, s0, s1, s2,
    c0, c1, c2, blocks, near_msg, cross_msg,
    vec_v, basis_v, lv1_v, lv2_v, root_v, coeff0, coeff1, coeff2, top_v, near_v, cross_v, sems, out_sems,
):
    core = lax.axis_index("rhs")
    near_last, cross_last = core == 0, core == 1
    jobs = []
    for chunk in range(2):
        lanes = pl.ds(chunk * 4096, 4096)
        jobs.append((vec.at[:, lanes], vec_v.at[:, lanes]))
        jobs.append((basis.at[:, lanes], basis_v.at[:, lanes]))
    jobs += [(lv1, lv1_v), (lv2, lv2_v), (root, root_v)]
    for place, skel in enumerate((s0, s1, s2)):
        lanes = edge_lanes(near_last, skel.shape[1], EDGE)
        jobs.append((skel.at[:, lanes], near_v.at[:, pl.ds(HALO + (2 + place) * EDGE, EDGE)]))
    for msg, last in ((near_v, near_last), (cross_v, cross_last)):
        for part, array in enumerate((pts, vec)):
            lanes = edge_lanes(last, LANES, HALO)
            jobs.append((array.at[:, lanes], msg.at[pl.ds(part * 32, 32), pl.ds(0, HALO)]))
    copies = fetch(jobs, sems)
    for copy in copies:
        copy.start()

    for chunk in range(2):
        copies[2 * chunk].wait()
        copies[2 * chunk + 1].wait()
        for pair in range(8 * chunk, 8 * chunk + 8):
            parts = []
            for side in range(2):
                lanes = slice((2 * pair + side) * LEAF, (2 * pair + side + 1) * LEAF)
                parts.append(mul3(vec_v[:, lanes], basis_v[:, lanes], NT))
            coeff0[:, pair * 128 : (pair + 1) * 128] = jnp.concatenate(parts, 1)

    def up_level(children, transfer, parents, count):
        for pair in range(count // 2):
            parts = []
            for side in range(2):
                lanes = slice((2 * pair + side) * 128, (2 * pair + side + 1) * 128)
                parts.append(mul3(children[:, lanes], transfer[:, lanes], NT))
            parents[:, pair * 128 : (pair + 1) * 128] = jnp.concatenate(parts, 1)

    for copy in copies[7:]:
        copy.wait()
    body, ends_at, skel_at = pl.ds(0, HALO), pl.ds(HALO, 2 * EDGE), pl.ds(HALO + 2 * EDGE, 3 * EDGE)
    stores = fetch(
        [
            (near_v.at[:, body], near_msg.at[:, body]), (cross_v.at[:, body], cross_msg.at[:, body]),
            (near_v.at[:, skel_at], near_msg.at[:, skel_at]), (coeff0, c0), (coeff1, c1), (coeff2, c2),
            (near_v.at[:, ends_at], near_msg.at[:, ends_at]),
            (cross_v.at[:, ends_at], cross_msg.at[:, ends_at]), (top_v, blocks),
        ],
        out_sems,
    )
    for store in stores[:4]:
        store.start()
    copies[4].wait()
    up_level(coeff0, lv1_v, coeff1, LEAVES_DEV // 2)
    copies[5].wait()
    up_level(coeff1, lv2_v, coeff2, LEAVES_DEV // 4)
    for msg, last in ((near_v, near_last), (cross_v, cross_last)):
        ends = [
            jnp.where(last, ref[:, ref.shape[1] - EDGE :], ref[:, :EDGE]) for ref in (coeff0, coeff1, coeff2)
        ]
        msg[:RHS_DEV, HALO : HALO + EDGE] = ends[0]
        msg[RHS_DEV:, HALO : HALO + EDGE] = ends[1]
        msg[:RHS_DEV, HALO + EDGE : HALO + 2 * EDGE] = ends[2]
        msg[RHS_DEV:, HALO + EDGE : HALO + 2 * EDGE] = jnp.zeros((RHS_DEV, EDGE), F32)
    for store in stores[4:8]:
        store.start()
    copies[6].wait()
    top = mul3(coeff2[...], root_v[...], NT)
    packed = jnp.concatenate([top[: RHS_DEV // 2], top[RHS_DEV // 2 :]], 1)
    top_v[...] = jnp.broadcast_to(packed[None], (CHIPS, RHS_DEV // 2, 2 * RANK))
    stores[8].start()
    for store in stores:
        store.wait()


def edge_penalty(mask, core):
    count = mask.shape[1]
    first = core == 0
    linked = [
        [jnp.where(first, mask[0, 0], mask[3, count - 2]), jnp.where(first, 0, mask[2, count - 1])],
        [jnp.where(first, mask[1, 0], 0), jnp.where(first, mask[0, 1], mask[3, count - 1])],
    ]
    row = lax.broadcasted_iota(jnp.int32, (8, EDGE), 0)
    cluster = lax.broadcasted_iota(jnp.int32, (8, EDGE), 1) // RANK
    penalty = jnp.zeros((8, EDGE), F32)
    for source in range(2):
        for target in range(2):
            value = jnp.where(linked[source][target] > 0, 0.0, CUT)
            penalty = jnp.where((row == source) & (cluster == target), value, penalty)
    return penalty


def near_kernel(
    mask_any, m0_any, m1_any, m2_any, s0, s1_any, s2_any, c1_any, c2_any, own_pts, own_vec, other_pts, other_vec,
    near_msg, cross_msg, own_any, first_any, rest_any, f1_any, f2_any,
    own_out, other_out, f1, f2, m1_v, m2_v, s1, s2, c1, c2, win_pts, win_vec, source, target, vec_t, mask, m0, m1, m2, skel_own, skel_halo,
    ends_own, ends_other, pairs, sems, out_sems,
):
    core = lax.axis_index("rhs")
    body_lanes = (WINDOW - REACH) * LEAF
    main_from = pl.multiple_of(core * (LANES - body_lanes), HALO)
    main_to = pl.multiple_of((1 - core) * HALO, HALO)
    halo_to = pl.multiple_of(core * body_lanes, HALO)
    jobs = [(mask_any, mask), (m0_any, m0), (m1_any, m1), (m2_any, m2)]
    jobs += [(m1_any, m1_v), (s1_any, s1), (c1_any, c1), (m2_any, m2_v), (s2_any, s2), (c2_any, c2)]
    for half, (pts, vecs, halo) in enumerate(
        ((own_pts, own_vec, near_msg), (other_pts, other_vec, cross_msg))
    ):
        rows = pl.ds(half * 32, 32)
        main = pl.ds(main_to, body_lanes)
        edge = pl.ds(halo_to, HALO)
        jobs.append((pts.at[:, pl.ds(main_from, body_lanes)], win_pts.at[rows, main]))
        jobs.append((vecs.at[:, pl.ds(main_from, body_lanes)], win_vec.at[rows, main]))
        jobs.append((halo.at[pl.ds(0, 32), pl.ds(0, HALO)], win_pts.at[rows, edge]))
        jobs.append((halo.at[pl.ds(32, 32), pl.ds(0, HALO)], win_vec.at[rows, edge]))
    ends_at = pl.ds(HALO, 2 * EDGE)
    jobs += [(near_msg.at[:, ends_at], ends_own), (cross_msg.at[:, ends_at], ends_other)]
    jobs.append((near_msg.at[:, pl.ds(HALO + 2 * EDGE, 3 * EDGE)], skel_halo))
    for place, skel in enumerate((s0, s1_any, s2_any)):
        lanes = edge_lanes(core == 1, skel.shape[1], EDGE)
        jobs.append((skel.at[:, lanes], skel_own.at[:, pl.ds(place * EDGE, EDGE)]))
    copies = fetch(jobs, sems)
    for copy in copies:
        copy.start()

    own_out[:, : LANES // 2] = jnp.zeros((32, LANES // 2), F32)
    other_out[:, : LANES // 2] = jnp.zeros((32, LANES // 2), F32)

    copies[0].wait()
    count = jnp.int32(0)
    for leaf in range(HALF):
        for offset in range(-REACH, REACH + 1):
            pairs[count] = (leaf + REACH + offset) * 32 + leaf
            if offset == 0:
                count = count + 1
            else:
                column = REACH + offset if offset < 0 else REACH + offset - 1
                count = count + mask[column, core * HALF + leaf]
    for extra in range(REST):
        pairs[count + extra] = WINDOW * 32

    source[WINDOW] = jnp.zeros((4 * DIM, LEAF), BF16).reshape(LEAF, 4 * DIM)
    vec_t[WINDOW] = jnp.zeros((2 * 64, LEAF), BF16)

    for copy in copies[4:10]:
        copy.wait()
    couple_level(m2_v, s2, c2, f2)
    couple_level(m1_v, s1, c1, f1)
    stores = fetch(
        [
            (f1, f1_any), (f2, f2_any), (own_out, own_any), (other_out.at[:, pl.ds(0, CUT_AT)], first_any),
            (other_out.at[:, pl.ds(CUT_AT, NEAR_OUT - CUT_AT)], rest_any),
        ],
        out_sems,
    )
    for store in stores[:2]:
        store.start()
    for copy in copies[1:4] + copies[10:]:
        copy.wait()

    for leaf in range(WINDOW):
        lanes = slice(leaf * LEAF, (leaf + 1) * LEAF)
        from_side, to_side = augment(win_pts[:, lanes])
        source[leaf] = from_side.T
        if REACH <= leaf < WINDOW - REACH:
            target[leaf - REACH] = to_side
        vec_t[leaf] = jnp.concatenate(split(win_vec[:, lanes]), 0)

    row = lax.broadcasted_iota(jnp.int32, (8, EDGE), 0)
    indicator = jnp.where(row == lax.broadcasted_iota(jnp.int32, (8, EDGE), 1) // RANK, 1.0, 0.0)
    for place, far_mask in enumerate((m0, m1, m2)):
        lanes = slice(place * EDGE, (place + 1) * EDGE)
        from_side, _ = augment(skel_halo[:, lanes], indicator, None)
        _, to_side = augment(skel_own[:, lanes], None, edge_penalty(far_mask, core))
        high, low = weights(mul(from_side.T, to_side))
        rows = slice(place % 2 * 32, place % 2 * 32 + 32)
        at = slice(place // 2 * EDGE, (place // 2 + 1) * EDGE)
        cof_high, cof_low = split(jnp.concatenate([ends_own[rows, at], ends_other[rows, at]], 0))
        both = mul(jnp.concatenate([cof_high, cof_low], 0), high)
        term = both[:64] + both[64:] + mul(cof_high, low)
        lanes = slice(LANES // 2 + place * EDGE, LANES // 2 + (place + 1) * EDGE)
        own_out[:, lanes] = term[:32]
        other_out[:, lanes] = term[32:]

    def steps(start, size, number):
        def step(index, carry):
            found = []
            for k in range(size):
                code = pairs[start + index * size + k]
                src, tgt = lax.shift_right_logical(code, 5), lax.bitwise_and(code, 31)
                high, low = weights(mul(source[src], target[tgt]))
                both = mul(vec_t[src], high)
                found.append((tgt, both[:64] + both[64:] + mul(vec_t[src, :64], low)))
            for tgt, term in found:
                lanes = pl.ds(pl.multiple_of(tgt * LEAF, LEAF), LEAF)
                own_out[:, lanes] += term[:32]
                other_out[:, lanes] += term[32:]
            return carry

        lax.fori_loop(0, number, step, 0)

    done = jnp.int32(0)
    for size in (GROUP, GROUP // 2, REST):
        number = (count - done + REST - 1) // size
        steps(done, size, number)
        done = done + number * size
    for store in stores[2:]:
        store.start()
    for store in stores:
        store.wait()


def couple_level(mask, skel, coeff, out, beside=None):
    width = skel.shape[1]
    count = width // RANK
    cluster = lax.broadcasted_iota(jnp.int32, (count, width), 0)
    owner = lax.broadcasted_iota(jnp.int32, (count, width), 1) // RANK
    spread = jnp.where(cluster == owner, 1.0, 0.0).astype(BF16)
    allowed = mul(mask[...].astype(F32).astype(BF16), spread)
    row = lax.broadcasted_iota(jnp.int32, (8, width), 0)
    owner = lax.broadcasted_iota(jnp.int32, (8, width), 1) // RANK
    penalty = jnp.full((8, width), CUT, F32)
    for column, offset in enumerate((-2, -1, 1, 2)):
        linked = (row == lax.bitwise_and(owner + offset, 7)) & (allowed[column : column + 1] > 0.5)
        penalty = jnp.where(linked, 0.0, penalty)
    target = augment(skel[...], None, penalty)[1]

    wide = width + 2 * EDGE
    row = lax.broadcasted_iota(jnp.int32, (8, wide), 0)
    owner = lax.broadcasted_iota(jnp.int32, (8, wide), 1) // RANK - FREACH
    indicator = jnp.where(row == lax.bitwise_and(owner, 7), 1.0, 0.0)
    gap = jnp.zeros((DIM, EDGE), F32)
    source = augment(jnp.concatenate([gap, skel[...], gap], 1), indicator, None)[0]
    source = [source[:, k * 256 : (k + 1) * 256].T for k in range(wide // 256)]
    gap = gap[:RHS_DEV]
    cof_high, cof_low = split(jnp.concatenate([gap, coeff[...], gap], 1))
    cof = jnp.concatenate([cof_high, cof_low], 0)
    for group in range(count // 4):
        lanes = slice(group * 256, (group + 1) * 256)
        around = slice(group * 256, group * 256 + 512)
        high, low = weights(mul(jnp.concatenate(source[group : group + 2], 0), target[:, lanes]))
        both = mul(cof[:, around], high)
        out[:, lanes] = both[:RHS_DEV] + both[RHS_DEV:] + mul(cof_high[:, around], low)
        if beside is not None:
            beside(group)


def down_kernel(
    gathered_any, roots_any, m0_any, s0_any, c0_any, lv1_any, lv2_any, root_any, basis_any, f1_any, f2_any, own_any,
    first_any, rest_any, out_any, f0, field0, field1, field2, gathered, roots, m0, s0, c0, lv1, lv2, root, basis, f1, f2,
    own_near, other_near, out, sems, out_sems,
):
    core = lax.axis_index("rhs")
    quarter = LANES // 4
    body, ends = pl.ds(0, HALF * LEAF), pl.ds(HALF * LEAF, 3 * EDGE)
    late = pl.ds(HALF * LEAF - CUT_AT, 3 * EDGE)
    second, rest_body = pl.ds(CUT_AT, HALF * LEAF - CUT_AT), pl.ds(0, HALF * LEAF - CUT_AT)
    copies = fetch(
        [
            (roots_any, roots), (m0_any, m0), (s0_any, s0), (c0_any, c0),
            (gathered_any, gathered), (root_any, root), (f2_any, f2), (lv2_any, lv2), (f1_any, f1), (lv1_any, lv1),
            (own_any.at[:, ends], own_near.at[:, ends]), (rest_any.at[:, late], other_near.at[:, ends]),
            (basis_any, basis), (own_any.at[:, body], own_near.at[:, body]),
            (first_any, other_near.at[:, pl.ds(0, CUT_AT)]),
            (rest_any.at[:, rest_body], other_near.at[:, second]),
        ],
        sems,
    )
    for copy in copies:
        copy.start()

    for copy in copies[:4]:
        copy.wait()
    me = lax.axis_index("leaf")
    one = jnp.where(lax.broadcasted_iota(jnp.int32, (8, RANK), 0) == 0, 1.0, 0.0)
    pair = roots[:, pl.ds(pl.multiple_of((me // 2) * 128, 128), 128)]
    own = jnp.where(lax.broadcasted_iota(jnp.int32, (DIM, 128), 1) // RANK == lax.rem(me, 2), pair, 0.0)
    own_side = augment(own[:, :RANK] + own[:, RANK:], one, None)[0].T
    kernels = []

    def root_part(part):
        lanes = slice(part * 512, (part + 1) * 512)
        first = lax.broadcasted_iota(jnp.int32, (8, 512), 0) == 0
        cluster = part * 8 + lax.broadcasted_iota(jnp.int32, (8, 512), 1) // RANK
        penalty = jnp.where(first & (jnp.abs(cluster - me) < 2), CUT, 0.0)
        kernels.append(weights(mul(own_side, augment(roots[:, lanes], None, penalty)[1])))

    couple_level(m0, s0, c0, f0, root_part)

    for copy in copies[4:]:
        copy.wait()
    top = jnp.zeros((RHS_DEV, RANK), F32)
    for part, (high, low) in enumerate(kernels):
        pieces = []
        for chip in range(8 * part, 8 * part + 8):
            pieces.append(jnp.concatenate([gathered[chip, :, :RANK], gathered[chip, :, RANK:]], 0))
        cof_high, cof_low = split(jnp.concatenate(pieces, 1))
        both = mul(jnp.concatenate([cof_high, cof_low], 0), high, NT)
        top = top + both[:RHS_DEV] + both[RHS_DEV:] + mul(cof_high, low, NT)

    def coupled(ref, place):
        width = ref.shape[1]
        lanes = slice(LANES // 2 + place * EDGE, LANES // 2 + (place + 1) * EDGE)
        mine, theirs = own_near[:, lanes], other_near[:, lanes]
        ref[:, :EDGE] += jnp.where(core == 0, mine, theirs)
        ref[:, width - EDGE :] += jnp.where(core == 0, theirs, mine)

    coupled(f2, 2)
    field2[...] = f2[...] + mul3(top, root[...])

    def down_level(parents, transfer, coupled, children, count):
        for pair in range(count // 2):
            lanes = [slice((2 * pair + side) * 128, (2 * pair + side + 1) * 128) for side in range(2)]
            above = parents[:, pair * 128 : (pair + 1) * 128]
            for at, below in zip(lanes, pair_products(above, [transfer[:, at] for at in lanes])):
                children[:, at] = coupled[:, at] + below

    coupled(f1, 1)
    down_level(field2, lv2, f1, field1, LEAVES_DEV // 4)
    coupled(f0, 0)
    down_level(field1, lv1, f0, field0, LEAVES_DEV // 2)

    stores = []
    for part in range(4):
        near, near_from = (own_near, other_near)[part // 2], part % 2 * quarter
        start = pl.multiple_of((core if part < 2 else 1 - core) * 2 * quarter + near_from, quarter)
        for pair in range(LEAVES_DEV // 8):
            fields = field0[:, pl.ds(pl.multiple_of(start // 4 + pair * 128, 128), 128)]
            offsets = [(2 * pair + side) * LEAF for side in range(2)]
            lanes = [pl.ds(pl.multiple_of(start + offset, LEAF), LEAF) for offset in offsets]
            for offset, at, far in zip(offsets, lanes, pair_products(fields, [basis[:, at] for at in lanes])):
                out[:, at] = near[:, near_from + offset : near_from + offset + LEAF] + far
        lanes = pl.ds(start, quarter)
        store = pltpu.make_async_copy(out.at[:, lanes], out_any.at[:, lanes], out_sems.at[part])
        store.start()
        stores.append(store)
    for store in stores:
        store.wait()


def shapes(*dims):
    return [jax.ShapeDtypeStruct(dim, F32) for dim in dims]


def cost(flops, bytes_accessed, transcendentals=0):
    return pl.CostEstimate(flops=flops, bytes_accessed=bytes_accessed, transcendentals=transcendentals)


SWAP = [(0, 1), (1, 0)]
NEAR_WAY = [pair for i in range(CHIPS - 1) for pair in ((2 * i, 2 * i + 2), (2 * i + 3, 2 * i + 1))]
CROSS_WAY = [pair for i in range(CHIPS - 1) for pair in ((2 * i + 1, 2 * i + 2), (2 * i + 2, 2 * i + 1))]


def call(kernel, outputs, inputs, scratch, estimate, name):
    def spec(place):
        return pl.BlockSpec(memory_space=place)

    several = isinstance(outputs, list)
    return pl.pallas_call(
        kernel,
        out_shape=outputs,
        in_specs=[spec(pl.ANY)] * len(inputs),
        out_specs=[spec(pl.ANY)] * len(outputs) if several else spec(pl.ANY),
        scratch_shapes=scratch,
        compiler_params=pltpu.CompilerParams(vmem_limit_bytes=64 * 2**20),
        cost_estimate=estimate,
        name=name,
    )(*inputs)


def vmem(*dims):
    return [pltpu.VMEM(dim, F32) for dim in dims]


def like(*arrays):
    return [pltpu.VMEM(array.shape, array.dtype) for array in arrays]


def dma_sems(count):
    return pltpu.SemaphoreType.DMA((count,))


def up_call(vec, basis, lv1, lv2, root, pts, s0, s1, s2):
    coeffs = ((RHS_DEV, 2048), (RHS_DEV, 1024), (RHS_DEV, 512))
    return call(
        up_kernel,
        shapes(*coeffs, (CHIPS, RHS_DEV // 2, 2 * RANK), (DIM, HALO + 5 * EDGE), (DIM, HALO + 2 * EDGE)),
        (vec, basis, lv1, lv2, root, pts, s0, s1, s2),
        like(vec, basis, lv1, lv2, root)
        + vmem(*coeffs, (CHIPS, RHS_DEV // 2, 2 * RANK), (DIM, HALO + 5 * EDGE), (DIM, HALO + 2 * EDGE))
        + [dma_sems(14), dma_sems(9)],
        cost(6 * 10**8, 6 * 10**6),
        "up",
    )


def near_call(mask, m0, m1, m2, s0, s1, s2, c1, c2, pts, vec, other_pts, other_vec, near_msg, cross_msg):
    return call(
        near_kernel,
        shapes((32, NEAR_OUT), (32, CUT_AT), (32, NEAR_OUT - CUT_AT), c1.shape, c2.shape),
        (mask, m0, m1, m2, s0, s1, s2, c1, c2, pts, vec, other_pts, other_vec, near_msg, cross_msg),
        vmem((32, NEAR_OUT), (32, NEAR_OUT))
        + like(c1, c2, m1, m2, s1, s2, c1, c2)
        + vmem((DIM, WINDOW * LEAF), (64, WINDOW * LEAF))
        + [
            pltpu.VMEM((WINDOW + 1, LEAF, 4 * DIM), BF16),
            pltpu.VMEM((HALF, 4 * DIM, LEAF), BF16),
            pltpu.VMEM((WINDOW + 1, 128, LEAF), BF16),
        ]
        + [pltpu.SMEM(array.shape, jnp.int32) for array in (mask, m0, m1, m2)]
        + vmem((DIM, 3 * EDGE), (DIM, 3 * EDGE), (DIM, 2 * EDGE), (DIM, 2 * EDGE))
        + [pltpu.SMEM((HALF * (2 * REACH + 1) + REST,), jnp.int32), dma_sems(24), dma_sems(5)],
        cost(10**10, 5 * 10**6, 5 * 10**6),
        "near",
    )


def down_call(gathered, roots, m0, s0, c0, lv1, lv2, root, basis, f1, f2, own_near, first, rest):
    inputs = (gathered, roots, m0, s0, c0, lv1, lv2, root, basis, f1, f2, own_near, first, rest)
    return call(
        down_kernel,
        jax.ShapeDtypeStruct((RHS_DEV, LANES), F32),
        inputs,
        like(c0, c0, f1, f2, *inputs[:-2], own_near) + vmem((RHS_DEV, LANES)) + [dma_sems(16), dma_sems(4)],
        cost(2 * 10**9, 8 * 10**6),
        "down",
    )


def per_device(
    points, vectors, leaf_basis, skel_lv0, skel_lv1, skel_lv2, transfer_lv1, transfer_lv2,
    transfer_root, root_skeleton_points, near_mask, far_lv0, far_lv1, far_lv2,
):
    pts, vec, basis = points.T, vectors.T, leaf_basis.T
    skels = (skel_lv0.T, skel_lv1.T, skel_lv2.T)
    lv1, lv2, root = transfer_lv1.T, transfer_lv2.T, transfer_root.T
    far = (far_lv0.T, far_lv1.T, far_lv2.T)
    both = ("leaf", "rhs")

    other_pts = lax.ppermute(pts, "rhs", SWAP)
    other_vec = lax.ppermute(vec, "rhs", SWAP)
    c0, c1, c2, blocks, near_msg, cross_msg = up_call(vec, basis, lv1, lv2, root, pts, *skels)
    near_msg = lax.ppermute(near_msg, both, NEAR_WAY)
    cross_msg = lax.ppermute(cross_msg, both, CROSS_WAY)
    gathered = lax.all_to_all(blocks, "leaf", split_axis=0, concat_axis=0, tiled=True)
    own_near, first, rest, f1, f2 = near_call(
        near_mask.T, *far, *skels, c1, c2, pts, vec, other_pts, other_vec, near_msg, cross_msg
    )
    first = lax.ppermute(first, "rhs", SWAP)
    rest = lax.ppermute(rest, "rhs", SWAP)
    return down_call(
        gathered, root_skeleton_points.T, far[0], skels[0], c0, lv1, lv2, root, basis, f1, f2, own_near, first, rest
    ).T


def solution(mesh):
    split_both = P("leaf", "rhs")
    placed = (split_both, split_both) + (P("leaf", None),) * 7 + (P(),) + (P("leaf", None),) * 4
    return jax.shard_map(per_device, mesh=mesh, in_specs=placed, out_specs=split_both, check_vma=False)
```

```python
import math

import jax
import jax.numpy as jnp
from jax import lax
from jax.experimental import pallas as pl
from jax.experimental.pallas import tpu as pltpu
from jax.sharding import PartitionSpec as P

DIM = 64
RANK = 64
LEAF = 256
REACH = 4
FREACH = 2
LEAVES_DEV = 32
RHS_DEV = 32
CHIPS = 64

HALF = LEAVES_DEV // 2
WINDOW = HALF + 2 * REACH
HALO = REACH * LEAF
EDGE = FREACH * RANK
LANES = LEAVES_DEV * LEAF
NEAR_OUT = HALF * LEAF + 3 * EDGE
CUT_AT = HALF * LEAF // 2
GROUP = 32
REST = 8
SCALE = math.sqrt(2.0 / 24.0 * math.log2(math.e))
CUT = -32768.0

F32 = jnp.float32
BF16 = jnp.bfloat16

NN = (((1,), (0,)), ((), ()))
NT = (((1,), (1,)), ((), ()))


def mul(left, right, dims=NN):
    return lax.dot_general(left, right, dims, preferred_element_type=F32)


def split(x):
    high = x.astype(BF16)
    return high, (x - high.astype(F32)).astype(BF16)


def mul3(left, right, dims=NN):
    rows = left.shape[0]
    left_high, left_low = split(left)
    right_high, right_low = split(right)
    both = mul(jnp.concatenate([left_high, left_low], 0), right_high, dims)
    return both[:rows] + both[rows:] + mul(left_high, right_low, dims)


def low_lanes(rows):
    return lax.broadcasted_iota(jnp.int32, (rows, 2 * RANK), 1) < RANK


def stack(x):
    return jnp.concatenate(split(x), 0)


def pair_products(pair, rights):
    turned = pltpu.roll(pair, RANK, 1)
    rows = pair.shape[0]
    low = low_lanes(rows)
    out = []
    for left, right in zip((jnp.where(low, pair, turned), jnp.where(low, turned, pair)), rights):
        both = mul(stack(left), stack(right))
        out.append(both[:rows] + both[rows:])
    return out


def augment(points, source_extra=None, target_extra=None):
    high, low = split(points * SCALE)
    high_f, low_f = high.astype(F32), low.astype(F32)
    norm = 0.5 * jnp.sum(high_f * (high_f + 2.0 * low_f), axis=0, keepdims=True)
    first = norm.astype(BF16).astype(F32)
    second = (norm - first).astype(BF16).astype(F32)
    third = (norm - first - second).astype(BF16).astype(F32)
    width = points.shape[1]
    row = lax.broadcasted_iota(jnp.int32, (8, width), 0)

    def rows_of(start, ones):
        picked = jnp.where(row == start, -first, 0.0)
        picked = jnp.where(row == start + 1, -second, picked)
        picked = jnp.where(row == start + 2, -third, picked)
        return jnp.where((row >= ones) & (row < ones + 3), 1.0, picked)

    nothing = jnp.zeros((8, width), F32)
    rest = jnp.zeros((DIM - 16, width), BF16)

    def block(start, ones, extra):
        tail = jnp.concatenate([rows_of(start, ones), nothing if extra is None else extra], 0)
        return tail.astype(BF16), rest

    source = jnp.concatenate([high, low, high, *block(0, 3, source_extra)], 0)
    target = jnp.concatenate([high, high, low, *block(3, 0, target_extra)], 0)
    return source, target


def weights(exponent):
    return split(jnp.exp2(exponent))


def fetch(jobs, sems):
    return [pltpu.make_async_copy(src, dst, sems.at[k]) for k, (src, dst) in enumerate(jobs)]


def edge_lanes(last, width, size):
    return pl.ds(pl.multiple_of(jnp.where(last, width - size, 0), size), size)


def up_kernel(
    vec, basis, lv1, lv2, root, pts, s0, s1, s2,
    c0, c1, c2, blocks, near_msg, cross_msg,
    vec_v, basis_v, lv1_v, lv2_v, root_v, coeff0, coeff1, coeff2, top_v, near_v, cross_v, sems, out_sems,
):
    core = lax.axis_index("rhs")
    near_last, cross_last = core == 0, core == 1
    jobs = []
    for chunk in range(2):
        lanes = pl.ds(chunk * 4096, 4096)
        jobs.append((vec.at[:, lanes], vec_v.at[:, lanes]))
        jobs.append((basis.at[:, lanes], basis_v.at[:, lanes]))
    jobs += [(lv1, lv1_v), (lv2, lv2_v), (root, root_v)]
    for place, skel in enumerate((s0, s1, s2)):
        lanes = edge_lanes(near_last, skel.shape[1], EDGE)
        jobs.append((skel.at[:, lanes], near_v.at[:, pl.ds(HALO + (2 + place) * EDGE, EDGE)]))
    for msg, last in ((near_v, near_last), (cross_v, cross_last)):
        for part, array in enumerate((pts, vec)):
            lanes = edge_lanes(last, LANES, HALO)
            jobs.append((array.at[:, lanes], msg.at[pl.ds(part * 32, 32), pl.ds(0, HALO)]))
    copies = fetch(jobs, sems)
    for copy in copies:
        copy.start()

    for chunk in range(2):
        copies[2 * chunk].wait()
        copies[2 * chunk + 1].wait()
        for pair in range(8 * chunk, 8 * chunk + 8):
            parts = []
            for side in range(2):
                lanes = slice((2 * pair + side) * LEAF, (2 * pair + side + 1) * LEAF)
                parts.append(mul3(vec_v[:, lanes], basis_v[:, lanes], NT))
            coeff0[:, pair * 128 : (pair + 1) * 128] = jnp.concatenate(parts, 1)

    def up_level(children, transfer, parents, count):
        for pair in range(count // 2):
            parts = []
            for side in range(2):
                lanes = slice((2 * pair + side) * 128, (2 * pair + side + 1) * 128)
                parts.append(mul3(children[:, lanes], transfer[:, lanes], NT))
            parents[:, pair * 128 : (pair + 1) * 128] = jnp.concatenate(parts, 1)

    for copy in copies[7:]:
        copy.wait()
    body, ends_at, skel_at = pl.ds(0, HALO), pl.ds(HALO, 2 * EDGE), pl.ds(HALO + 2 * EDGE, 3 * EDGE)
    stores = fetch(
        [
            (near_v.at[:, body], near_msg.at[:, body]), (cross_v.at[:, body], cross_msg.at[:, body]),
            (near_v.at[:, skel_at], near_msg.at[:, skel_at]), (coeff0, c0), (coeff1, c1), (coeff2, c2),
            (near_v.at[:, ends_at], near_msg.at[:, ends_at]),
            (cross_v.at[:, ends_at], cross_msg.at[:, ends_at]), (top_v, blocks),
        ],
        out_sems,
    )
    for store in stores[:4]:
        store.start()
    copies[4].wait()
    up_level(coeff0, lv1_v, coeff1, LEAVES_DEV // 2)
    copies[5].wait()
    up_level(coeff1, lv2_v, coeff2, LEAVES_DEV // 4)
    for msg, last in ((near_v, near_last), (cross_v, cross_last)):
        ends = [
            jnp.where(last, ref[:, ref.shape[1] - EDGE :], ref[:, :EDGE]) for ref in (coeff0, coeff1, coeff2)
        ]
        msg[:RHS_DEV, HALO : HALO + EDGE] = ends[0]
        msg[RHS_DEV:, HALO : HALO + EDGE] = ends[1]
        msg[:RHS_DEV, HALO + EDGE : HALO + 2 * EDGE] = ends[2]
        msg[RHS_DEV:, HALO + EDGE : HALO + 2 * EDGE] = jnp.zeros((RHS_DEV, EDGE), F32)
    for store in stores[4:8]:
        store.start()
    copies[6].wait()
    top = mul3(coeff2[...], root_v[...], NT)
    packed = jnp.concatenate([top[: RHS_DEV // 2], top[RHS_DEV // 2 :]], 1)
    top_v[...] = jnp.broadcast_to(packed[None], (CHIPS, RHS_DEV // 2, 2 * RANK))
    stores[8].start()
    for store in stores:
        store.wait()


def edge_penalty(mask, core):
    count = mask.shape[1]
    first = core == 0
    chip = lax.axis_index("leaf")
    outside = jnp.where(first, chip == 0, chip == CHIPS - 1)
    linked = [
        [jnp.where(first, mask[0, 0], mask[3, count - 2]), jnp.where(first, 0, mask[2, count - 1])],
        [jnp.where(first, mask[1, 0], 0), jnp.where(first, mask[0, 1], mask[3, count - 1])],
    ]
    row = lax.broadcasted_iota(jnp.int32, (8, EDGE), 0)
    cluster = lax.broadcasted_iota(jnp.int32, (8, EDGE), 1) // RANK
    penalty = jnp.zeros((8, EDGE), F32)
    for source in range(2):
        for target in range(2):
            value = jnp.where((linked[source][target] > 0) & jnp.logical_not(outside), 0.0, CUT)
            penalty = jnp.where((row == source) & (cluster == target), value, penalty)
    return penalty


def near_kernel(
    mask_any, m0_any, m1_any, m2_any, s0, s1_any, s2_any, c1_any, c2_any, own_pts, own_vec, other_pts, other_vec,
    near_msg, cross_msg, own_any, first_any, rest_any, f1_any, f2_any,
    own_out, other_out, f1, f2, m1_v, m2_v, s1, s2, c1, c2, win_pts, win_vec, source, target, vec_t, mask, m0, m1, m2, skel_own, skel_halo,
    ends_own, ends_other, pairs, sems, out_sems,
):
    core = lax.axis_index("rhs")
    body_lanes = (WINDOW - REACH) * LEAF
    main_from = pl.multiple_of(core * (LANES - body_lanes), HALO)
    main_to = pl.multiple_of((1 - core) * HALO, HALO)
    halo_to = pl.multiple_of(core * body_lanes, HALO)
    jobs = [(mask_any, mask), (m0_any, m0), (m1_any, m1), (m2_any, m2)]
    jobs += [(m1_any, m1_v), (s1_any, s1), (c1_any, c1), (m2_any, m2_v), (s2_any, s2), (c2_any, c2)]
    for half, (pts, vecs, halo) in enumerate(
        ((own_pts, own_vec, near_msg), (other_pts, other_vec, cross_msg))
    ):
        rows = pl.ds(half * 32, 32)
        main = pl.ds(main_to, body_lanes)
        edge = pl.ds(halo_to, HALO)
        jobs.append((pts.at[:, pl.ds(main_from, body_lanes)], win_pts.at[rows, main]))
        jobs.append((vecs.at[:, pl.ds(main_from, body_lanes)], win_vec.at[rows, main]))
        jobs.append((halo.at[pl.ds(0, 32), pl.ds(0, HALO)], win_pts.at[rows, edge]))
        jobs.append((halo.at[pl.ds(32, 32), pl.ds(0, HALO)], win_vec.at[rows, edge]))
    ends_at = pl.ds(HALO, 2 * EDGE)
    jobs += [(near_msg.at[:, ends_at], ends_own), (cross_msg.at[:, ends_at], ends_other)]
    jobs.append((near_msg.at[:, pl.ds(HALO + 2 * EDGE, 3 * EDGE)], skel_halo))
    for place, skel in enumerate((s0, s1_any, s2_any)):
        lanes = edge_lanes(core == 1, skel.shape[1], EDGE)
        jobs.append((skel.at[:, lanes], skel_own.at[:, pl.ds(place * EDGE, EDGE)]))
    copies = fetch(jobs, sems)
    for copy in copies:
        copy.start()

    own_out[:, : LANES // 2] = jnp.zeros((32, LANES // 2), F32)
    other_out[:, : LANES // 2] = jnp.zeros((32, LANES // 2), F32)

    copies[0].wait()
    count = jnp.int32(0)
    for leaf in range(HALF):
        for offset in range(-REACH, REACH + 1):
            pairs[count] = (leaf + REACH + offset) * 32 + leaf
            if offset == 0:
                count = count + 1
            else:
                column = REACH + offset if offset < 0 else REACH + offset - 1
                count = count + mask[column, core * HALF + leaf]
    for extra in range(REST):
        pairs[count + extra] = WINDOW * 32

    source[WINDOW] = jnp.zeros((4 * DIM, LEAF), BF16).reshape(LEAF, 4 * DIM)
    vec_t[WINDOW] = jnp.zeros((2 * 64, LEAF), BF16)

    for copy in copies[4:10]:
        copy.wait()
    couple_level(m2_v, s2, c2, f2)
    couple_level(m1_v, s1, c1, f1)
    stores = fetch(
        [
            (f1, f1_any), (f2, f2_any), (own_out, own_any), (other_out.at[:, pl.ds(0, CUT_AT)], first_any),
            (other_out.at[:, pl.ds(CUT_AT, NEAR_OUT - CUT_AT)], rest_any),
        ],
        out_sems,
    )
    for store in stores[:2]:
        store.start()
    for copy in copies[1:4] + copies[10:]:
        copy.wait()

    for leaf in range(WINDOW):
        lanes = slice(leaf * LEAF, (leaf + 1) * LEAF)
        from_side, to_side = augment(win_pts[:, lanes])
        source[leaf] = from_side.T
        if REACH <= leaf < WINDOW - REACH:
            target[leaf - REACH] = to_side
        vec_t[leaf] = jnp.concatenate(split(win_vec[:, lanes]), 0)

    row = lax.broadcasted_iota(jnp.int32, (8, EDGE), 0)
    indicator = jnp.where(row == lax.broadcasted_iota(jnp.int32, (8, EDGE), 1) // RANK, 1.0, 0.0)
    for place, far_mask in enumerate((m0, m1, m2)):
        lanes = slice(place * EDGE, (place + 1) * EDGE)
        from_side, _ = augment(skel_halo[:, lanes], indicator, None)
        _, to_side = augment(skel_own[:, lanes], None, edge_penalty(far_mask, core))
        high, low = weights(mul(from_side.T, to_side))
        rows = slice(place % 2 * 32, place % 2 * 32 + 32)
        at = slice(place // 2 * EDGE, (place // 2 + 1) * EDGE)
        cof_high, cof_low = split(jnp.concatenate([ends_own[rows, at], ends_other[rows, at]], 0))
        both = mul(jnp.concatenate([cof_high, cof_low], 0), high)
        term = both[:64] + both[64:] + mul(cof_high, low)
        lanes = slice(LANES // 2 + place * EDGE, LANES // 2 + (place + 1) * EDGE)
        own_out[:, lanes] = term[:32]
        other_out[:, lanes] = term[32:]

    def steps(start, size, number):
        def step(index, carry):
            found = []
            for k in range(size):
                code = pairs[start + index * size + k]
                src, tgt = lax.shift_right_logical(code, 5), lax.bitwise_and(code, 31)
                high, low = weights(mul(source[src], target[tgt]))
                both = mul(vec_t[src], high)
                found.append((tgt, both[:64] + both[64:] + mul(vec_t[src, :64], low)))
            for tgt, term in found:
                lanes = pl.ds(pl.multiple_of(tgt * LEAF, LEAF), LEAF)
                own_out[:, lanes] += term[:32]
                other_out[:, lanes] += term[32:]
            return carry

        lax.fori_loop(0, number, step, 0)

    done = jnp.int32(0)
    for size in (GROUP, GROUP // 2, REST):
        number = (count - done + REST - 1) // size
        steps(done, size, number)
        done = done + number * size
    for store in stores[2:]:
        store.start()
    for store in stores:
        store.wait()


def couple_level(mask, skel, coeff, out, beside=None):
    width = skel.shape[1]
    count = width // RANK
    cluster = lax.broadcasted_iota(jnp.int32, (count, width), 0)
    owner = lax.broadcasted_iota(jnp.int32, (count, width), 1) // RANK
    spread = jnp.where(cluster == owner, 1.0, 0.0).astype(BF16)
    allowed = mul(mask[...].astype(F32).astype(BF16), spread)
    row = lax.broadcasted_iota(jnp.int32, (8, width), 0)
    owner = lax.broadcasted_iota(jnp.int32, (8, width), 1) // RANK
    penalty = jnp.full((8, width), CUT, F32)
    for column, offset in enumerate((-2, -1, 1, 2)):
        linked = (row == lax.bitwise_and(owner + offset, 7)) & (allowed[column : column + 1] > 0.5)
        penalty = jnp.where(linked, 0.0, penalty)
    target = augment(skel[...], None, penalty)[1]

    wide = width + 2 * EDGE
    row = lax.broadcasted_iota(jnp.int32, (8, wide), 0)
    owner = lax.broadcasted_iota(jnp.int32, (8, wide), 1) // RANK - FREACH
    indicator = jnp.where(row == lax.bitwise_and(owner, 7), 1.0, 0.0)
    gap = jnp.zeros((DIM, EDGE), F32)
    source = augment(jnp.concatenate([gap, skel[...], gap], 1), indicator, None)[0]
    source = [source[:, k * 256 : (k + 1) * 256].T for k in range(wide // 256)]
    gap = gap[:RHS_DEV]
    cof_high, cof_low = split(jnp.concatenate([gap, coeff[...], gap], 1))
    cof = jnp.concatenate([cof_high, cof_low], 0)
    for group in range(count // 4):
        lanes = slice(group * 256, (group + 1) * 256)
        around = slice(group * 256, group * 256 + 512)
        high, low = weights(mul(jnp.concatenate(source[group : group + 2], 0), target[:, lanes]))
        both = mul(cof[:, around], high)
        out[:, lanes] = both[:RHS_DEV] + both[RHS_DEV:] + mul(cof_high[:, around], low)
        if beside is not None:
            beside(group)


def down_kernel(
    gathered_any, roots_any, m0_any, s0_any, c0_any, lv1_any, lv2_any, root_any, basis_any, f1_any, f2_any, own_any,
    first_any, rest_any, out_any, f0, field0, field1, field2, gathered, roots, m0, s0, c0, lv1, lv2, root, basis, f1, f2,
    own_near, other_near, out, sems, out_sems,
):
    core = lax.axis_index("rhs")
    quarter = LANES // 4
    body, ends = pl.ds(0, HALF * LEAF), pl.ds(HALF * LEAF, 3 * EDGE)
    late = pl.ds(HALF * LEAF - CUT_AT, 3 * EDGE)
    second, rest_body = pl.ds(CUT_AT, HALF * LEAF - CUT_AT), pl.ds(0, HALF * LEAF - CUT_AT)
    copies = fetch(
        [
            (roots_any, roots), (m0_any, m0), (s0_any, s0), (c0_any, c0),
            (gathered_any, gathered), (root_any, root), (f2_any, f2), (lv2_any, lv2), (f1_any, f1), (lv1_any, lv1),
            (own_any.at[:, ends], own_near.at[:, ends]), (rest_any.at[:, late], other_near.at[:, ends]),
            (basis_any, basis), (own_any.at[:, body], own_near.at[:, body]),
            (first_any, other_near.at[:, pl.ds(0, CUT_AT)]),
            (rest_any.at[:, rest_body], other_near.at[:, second]),
        ],
        sems,
    )
    for copy in copies:
        copy.start()

    for copy in copies[:4]:
        copy.wait()
    me = lax.axis_index("leaf")
    one = jnp.where(lax.broadcasted_iota(jnp.int32, (8, RANK), 0) == 0, 1.0, 0.0)
    pair = roots[:, pl.ds(pl.multiple_of((me // 2) * 128, 128), 128)]
    own = jnp.where(lax.broadcasted_iota(jnp.int32, (DIM, 128), 1) // RANK == lax.rem(me, 2), pair, 0.0)
    own_side = augment(own[:, :RANK] + own[:, RANK:], one, None)[0].T
    kernels = []

    def root_part(part):
        lanes = slice(part * 512, (part + 1) * 512)
        first = lax.broadcasted_iota(jnp.int32, (8, 512), 0) == 0
        cluster = part * 8 + lax.broadcasted_iota(jnp.int32, (8, 512), 1) // RANK
        penalty = jnp.where(first & (jnp.abs(cluster - me) < 2), CUT, 0.0)
        kernels.append(weights(mul(own_side, augment(roots[:, lanes], None, penalty)[1])))

    couple_level(m0, s0, c0, f0, root_part)

    for copy in copies[4:]:
        copy.wait()
    top = jnp.zeros((RHS_DEV, RANK), F32)
    for part, (high, low) in enumerate(kernels):
        pieces = []
        for chip in range(8 * part, 8 * part + 8):
            pieces.append(jnp.concatenate([gathered[chip, :, :RANK], gathered[chip, :, RANK:]], 0))
        cof_high, cof_low = split(jnp.concatenate(pieces, 1))
        both = mul(jnp.concatenate([cof_high, cof_low], 0), high, NT)
        top = top + both[:RHS_DEV] + both[RHS_DEV:] + mul(cof_high, low, NT)

    def coupled(ref, place):
        width = ref.shape[1]
        lanes = slice(LANES // 2 + place * EDGE, LANES // 2 + (place + 1) * EDGE)
        mine, theirs = own_near[:, lanes], other_near[:, lanes]
        ref[:, :EDGE] += jnp.where(core == 0, mine, theirs)
        ref[:, width - EDGE :] += jnp.where(core == 0, theirs, mine)

    coupled(f2, 2)
    field2[...] = f2[...] + mul3(top, root[...])

    def down_level(parents, transfer, coupled, children, count):
        for pair in range(count // 2):
            lanes = [slice((2 * pair + side) * 128, (2 * pair + side + 1) * 128) for side in range(2)]
            above = parents[:, pair * 128 : (pair + 1) * 128]
            for at, below in zip(lanes, pair_products(above, [transfer[:, at] for at in lanes])):
                children[:, at] = coupled[:, at] + below

    coupled(f1, 1)
    down_level(field2, lv2, f1, field1, LEAVES_DEV // 4)
    coupled(f0, 0)
    down_level(field1, lv1, f0, field0, LEAVES_DEV // 2)

    stores = []
    for part in range(4):
        near, near_from = (own_near, other_near)[part // 2], part % 2 * quarter
        start = pl.multiple_of((core if part < 2 else 1 - core) * 2 * quarter + near_from, quarter)
        for pair in range(LEAVES_DEV // 8):
            fields = field0[:, pl.ds(pl.multiple_of(start // 4 + pair * 128, 128), 128)]
            offsets = [(2 * pair + side) * LEAF for side in range(2)]
            lanes = [pl.ds(pl.multiple_of(start + offset, LEAF), LEAF) for offset in offsets]
            for offset, at, far in zip(offsets, lanes, pair_products(fields, [basis[:, at] for at in lanes])):
                out[:, at] = near[:, near_from + offset : near_from + offset + LEAF] + far
        lanes = pl.ds(start, quarter)
        store = pltpu.make_async_copy(out.at[:, lanes], out_any.at[:, lanes], out_sems.at[part])
        store.start()
        stores.append(store)
    for store in stores:
        store.wait()


def shapes(*dims):
    return [jax.ShapeDtypeStruct(dim, F32) for dim in dims]


def cost(flops, bytes_accessed, transcendentals=0):
    return pl.CostEstimate(flops=flops, bytes_accessed=bytes_accessed, transcendentals=transcendentals)


SWAP = [(0, 1), (1, 0)]
LAST = 2 * CHIPS - 1
STEPS = range(0, LAST - 1, 2)
NEAR_WAY = [pair for i in STEPS for pair in ((i, i + 2), (i + 3, i + 1))] + [(1, 0), (LAST - 1, LAST)]
CROSS_WAY = [pair for i in STEPS for pair in ((i + 1, i + 2), (i + 2, i + 1))] + [(0, LAST), (LAST, 0)]


def call(kernel, outputs, inputs, scratch, estimate, name):
    def spec(place):
        return pl.BlockSpec(memory_space=place)

    several = isinstance(outputs, list)
    return pl.pallas_call(
        kernel,
        out_shape=outputs,
        in_specs=[spec(pl.ANY)] * len(inputs),
        out_specs=[spec(pl.ANY)] * len(outputs) if several else spec(pl.ANY),
        scratch_shapes=scratch,
        compiler_params=pltpu.CompilerParams(vmem_limit_bytes=64 * 2**20),
        cost_estimate=estimate,
        name=name,
    )(*inputs)


def vmem(*dims):
    return [pltpu.VMEM(dim, F32) for dim in dims]


def like(*arrays):
    return [pltpu.VMEM(array.shape, array.dtype) for array in arrays]


def dma_sems(count):
    return pltpu.SemaphoreType.DMA((count,))


def up_call(vec, basis, lv1, lv2, root, pts, s0, s1, s2):
    coeffs = ((RHS_DEV, 2048), (RHS_DEV, 1024), (RHS_DEV, 512))
    return call(
        up_kernel,
        shapes(*coeffs, (CHIPS, RHS_DEV // 2, 2 * RANK), (DIM, HALO + 5 * EDGE), (DIM, HALO + 2 * EDGE)),
        (vec, basis, lv1, lv2, root, pts, s0, s1, s2),
        like(vec, basis, lv1, lv2, root)
        + vmem(*coeffs, (CHIPS, RHS_DEV // 2, 2 * RANK), (DIM, HALO + 5 * EDGE), (DIM, HALO + 2 * EDGE))
        + [dma_sems(14), dma_sems(9)],
        cost(6 * 10**8, 6 * 10**6),
        "up",
    )


def near_call(mask, m0, m1, m2, s0, s1, s2, c1, c2, pts, vec, other_pts, other_vec, near_msg, cross_msg):
    return call(
        near_kernel,
        shapes((32, NEAR_OUT), (32, CUT_AT), (32, NEAR_OUT - CUT_AT), c1.shape, c2.shape),
        (mask, m0, m1, m2, s0, s1, s2, c1, c2, pts, vec, other_pts, other_vec, near_msg, cross_msg),
        vmem((32, NEAR_OUT), (32, NEAR_OUT))
        + like(c1, c2, m1, m2, s1, s2, c1, c2)
        + vmem((DIM, WINDOW * LEAF), (64, WINDOW * LEAF))
        + [
            pltpu.VMEM((WINDOW + 1, LEAF, 4 * DIM), BF16),
            pltpu.VMEM((HALF, 4 * DIM, LEAF), BF16),
            pltpu.VMEM((WINDOW + 1, 128, LEAF), BF16),
        ]
        + [pltpu.SMEM(array.shape, jnp.int32) for array in (mask, m0, m1, m2)]
        + vmem((DIM, 3 * EDGE), (DIM, 3 * EDGE), (DIM, 2 * EDGE), (DIM, 2 * EDGE))
        + [pltpu.SMEM((HALF * (2 * REACH + 1) + REST,), jnp.int32), dma_sems(24), dma_sems(5)],
        cost(10**10, 5 * 10**6, 5 * 10**6),
        "near",
    )


def down_call(gathered, roots, m0, s0, c0, lv1, lv2, root, basis, f1, f2, own_near, first, rest):
    inputs = (gathered, roots, m0, s0, c0, lv1, lv2, root, basis, f1, f2, own_near, first, rest)
    return call(
        down_kernel,
        jax.ShapeDtypeStruct((RHS_DEV, LANES), F32),
        inputs,
        like(c0, c0, f1, f2, *inputs[:-2], own_near) + vmem((RHS_DEV, LANES)) + [dma_sems(16), dma_sems(4)],
        cost(2 * 10**9, 8 * 10**6),
        "down",
    )


def per_device(
    points, vectors, leaf_basis, skel_lv0, skel_lv1, skel_lv2, transfer_lv1, transfer_lv2,
    transfer_root, root_skeleton_points, near_mask, far_lv0, far_lv1, far_lv2,
):
    pts, vec, basis = points.T, vectors.T, leaf_basis.T
    skels = (skel_lv0.T, skel_lv1.T, skel_lv2.T)
    lv1, lv2, root = transfer_lv1.T, transfer_lv2.T, transfer_root.T
    far = (far_lv0.T, far_lv1.T, far_lv2.T)
    both = ("leaf", "rhs")

    other_pts = lax.ppermute(pts, "rhs", SWAP)
    other_vec = lax.ppermute(vec, "rhs", SWAP)
    c0, c1, c2, blocks, near_msg, cross_msg = up_call(vec, basis, lv1, lv2, root, pts, *skels)
    near_msg = lax.ppermute(near_msg, both, NEAR_WAY)
    cross_msg = lax.ppermute(cross_msg, both, CROSS_WAY)
    gathered = lax.all_to_all(blocks, "leaf", split_axis=0, concat_axis=0, tiled=True)
    own_near, first, rest, f1, f2 = near_call(
        near_mask.T, *far, *skels, c1, c2, pts, vec, other_pts, other_vec, near_msg, cross_msg
    )
    first = lax.ppermute(first, "rhs", SWAP)
    rest = lax.ppermute(rest, "rhs", SWAP)
    return down_call(
        gathered, root_skeleton_points.T, far[0], skels[0], c0, lv1, lv2, root, basis, f1, f2, own_near, first, rest
    ).T


def solution(mesh):
    split_both = P("leaf", "rhs")
    placed = (split_both, split_both) + (P("leaf", None),) * 7 + (P(),) + (P("leaf", None),) * 4
    return jax.shard_map(per_device, mesh=mesh, in_specs=placed, out_specs=split_both, check_vma=False)
```

```python
import math

import jax
import jax.numpy as jnp
from jax import lax
from jax.experimental import pallas as pl
from jax.experimental.pallas import tpu as pltpu
from jax.sharding import PartitionSpec as P

DIM = 64
RANK = 64
LEAF = 256
REACH = 4
FREACH = 2
LEAVES_DEV = 32
RHS_DEV = 32
CHIPS = 64

HALF = LEAVES_DEV // 2
WINDOW = HALF + 2 * REACH
HALO = REACH * LEAF
EDGE = FREACH * RANK
LANES = LEAVES_DEV * LEAF
NEAR_OUT = HALF * LEAF + 3 * EDGE
CUT_AT = HALF * LEAF // 2
GROUP = 64
REST = 8
SCALE = math.sqrt(2.0 / 24.0 * math.log2(math.e))
CUT = -32768.0

F32 = jnp.float32
BF16 = jnp.bfloat16

NN = (((1,), (0,)), ((), ()))
NT = (((1,), (1,)), ((), ()))


def mul(left, right, dims=NN):
    return lax.dot_general(left, right, dims, preferred_element_type=F32)


def split(x):
    high = x.astype(BF16)
    return high, (x - high.astype(F32)).astype(BF16)


def mul3(left, right, dims=NN):
    rows = left.shape[0]
    left_high, left_low = split(left)
    right_high, right_low = split(right)
    both = mul(jnp.concatenate([left_high, left_low], 0), right_high, dims)
    return both[:rows] + both[rows:] + mul(left_high, right_low, dims)


def low_lanes(rows):
    return lax.broadcasted_iota(jnp.int32, (rows, 2 * RANK), 1) < RANK


def stack(x):
    return jnp.concatenate(split(x), 0)


def pair_products(pair, rights):
    turned = pltpu.roll(pair, RANK, 1)
    rows = pair.shape[0]
    low = low_lanes(rows)
    out = []
    for left, right in zip((jnp.where(low, pair, turned), jnp.where(low, turned, pair)), rights):
        both = mul(stack(left), stack(right))
        out.append(both[:rows] + both[rows:])
    return out


def augment(points, source_extra=None, target_extra=None):
    high, low = split(points * SCALE)
    high_f, low_f = high.astype(F32), low.astype(F32)
    norm = 0.5 * jnp.sum(high_f * (high_f + 2.0 * low_f), axis=0, keepdims=True)
    first = norm.astype(BF16).astype(F32)
    second = (norm - first).astype(BF16).astype(F32)
    third = (norm - first - second).astype(BF16).astype(F32)
    width = points.shape[1]
    row = lax.broadcasted_iota(jnp.int32, (8, width), 0)

    def rows_of(start, ones):
        picked = jnp.where(row == start, -first, 0.0)
        picked = jnp.where(row == start + 1, -second, picked)
        picked = jnp.where(row == start + 2, -third, picked)
        return jnp.where((row >= ones) & (row < ones + 3), 1.0, picked)

    nothing = jnp.zeros((8, width), F32)
    rest = jnp.zeros((DIM - 16, width), BF16)

    def block(start, ones, extra):
        tail = jnp.concatenate([rows_of(start, ones), nothing if extra is None else extra], 0)
        return tail.astype(BF16), rest

    source = jnp.concatenate([high, low, high, *block(0, 3, source_extra)], 0)
    target = jnp.concatenate([high, high, low, *block(3, 0, target_extra)], 0)
    return source, target


def weights(exponent):
    return split(jnp.exp2(exponent))


def fetch(jobs, sems):
    return [pltpu.make_async_copy(src, dst, sems.at[k]) for k, (src, dst) in enumerate(jobs)]


def edge_lanes(last, width, size):
    return pl.ds(pl.multiple_of(jnp.where(last, width - size, 0), size), size)


def up_kernel(
    vec, basis, lv1, lv2, root, pts, s0, s1, s2,
    c0, c1, c2, blocks, near_msg, cross_msg,
    vec_v, basis_v, lv1_v, lv2_v, root_v, coeff0, coeff1, coeff2, top_v, near_v, cross_v, sems, out_sems,
):
    core = lax.axis_index("rhs")
    near_last, cross_last = core == 0, core == 1
    jobs = []
    for chunk in range(2):
        lanes = pl.ds(chunk * 4096, 4096)
        jobs.append((vec.at[:, lanes], vec_v.at[:, lanes]))
        jobs.append((basis.at[:, lanes], basis_v.at[:, lanes]))
    jobs += [(lv1, lv1_v), (lv2, lv2_v), (root, root_v)]
    for place, skel in enumerate((s0, s1, s2)):
        lanes = edge_lanes(near_last, skel.shape[1], EDGE)
        jobs.append((skel.at[:, lanes], near_v.at[:, pl.ds(HALO + (2 + place) * EDGE, EDGE)]))
    for msg, last in ((near_v, near_last), (cross_v, cross_last)):
        for part, array in enumerate((pts, vec)):
            lanes = edge_lanes(last, LANES, HALO)
            jobs.append((array.at[:, lanes], msg.at[pl.ds(part * 32, 32), pl.ds(0, HALO)]))
    copies = fetch(jobs, sems)
    for copy in copies:
        copy.start()

    for chunk in range(2):
        copies[2 * chunk].wait()
        copies[2 * chunk + 1].wait()
        for pair in range(8 * chunk, 8 * chunk + 8):
            parts = []
            for side in range(2):
                lanes = slice((2 * pair + side) * LEAF, (2 * pair + side + 1) * LEAF)
                parts.append(mul3(vec_v[:, lanes], basis_v[:, lanes], NT))
            coeff0[:, pair * 128 : (pair + 1) * 128] = jnp.concatenate(parts, 1)

    def up_level(children, transfer, parents, count):
        for pair in range(count // 2):
            parts = []
            for side in range(2):
                lanes = slice((2 * pair + side) * 128, (2 * pair + side + 1) * 128)
                parts.append(mul3(children[:, lanes], transfer[:, lanes], NT))
            parents[:, pair * 128 : (pair + 1) * 128] = jnp.concatenate(parts, 1)

    for copy in copies[7:]:
        copy.wait()
    body, ends_at, skel_at = pl.ds(0, HALO), pl.ds(HALO, 2 * EDGE), pl.ds(HALO + 2 * EDGE, 3 * EDGE)
    stores = fetch(
        [
            (near_v.at[:, body], near_msg.at[:, body]), (cross_v.at[:, body], cross_msg.at[:, body]),
            (near_v.at[:, skel_at], near_msg.at[:, skel_at]), (coeff0, c0), (coeff1, c1), (coeff2, c2),
            (near_v.at[:, ends_at], near_msg.at[:, ends_at]),
            (cross_v.at[:, ends_at], cross_msg.at[:, ends_at]), (top_v, blocks),
        ],
        out_sems,
    )
    for store in stores[:4]:
        store.start()
    copies[4].wait()
    up_level(coeff0, lv1_v, coeff1, LEAVES_DEV // 2)
    copies[5].wait()
    up_level(coeff1, lv2_v, coeff2, LEAVES_DEV // 4)
    for msg, last in ((near_v, near_last), (cross_v, cross_last)):
        ends = [
            jnp.where(last, ref[:, ref.shape[1] - EDGE :], ref[:, :EDGE]) for ref in (coeff0, coeff1, coeff2)
        ]
        msg[:RHS_DEV, HALO : HALO + EDGE] = ends[0]
        msg[RHS_DEV:, HALO : HALO + EDGE] = ends[1]
        msg[:RHS_DEV, HALO + EDGE : HALO + 2 * EDGE] = ends[2]
        msg[RHS_DEV:, HALO + EDGE : HALO + 2 * EDGE] = jnp.zeros((RHS_DEV, EDGE), F32)
    for store in stores[4:8]:
        store.start()
    copies[6].wait()
    top = mul3(coeff2[...], root_v[...], NT)
    packed = jnp.concatenate([top[: RHS_DEV // 2], top[RHS_DEV // 2 :]], 1)
    top_v[...] = jnp.broadcast_to(packed[None], (CHIPS, RHS_DEV // 2, 2 * RANK))
    stores[8].start()
    for store in stores:
        store.wait()


def edge_penalty(mask, core):
    count = mask.shape[1]
    first = core == 0
    chip = lax.axis_index("leaf")
    outside = jnp.where(first, chip == 0, chip == CHIPS - 1)
    linked = [
        [jnp.where(first, mask[0, 0], mask[3, count - 2]), jnp.where(first, 0, mask[2, count - 1])],
        [jnp.where(first, mask[1, 0], 0), jnp.where(first, mask[0, 1], mask[3, count - 1])],
    ]
    row = lax.broadcasted_iota(jnp.int32, (8, EDGE), 0)
    cluster = lax.broadcasted_iota(jnp.int32, (8, EDGE), 1) // RANK
    penalty = jnp.zeros((8, EDGE), F32)
    for source in range(2):
        for target in range(2):
            value = jnp.where((linked[source][target] > 0) & jnp.logical_not(outside), 0.0, CUT)
            penalty = jnp.where((row == source) & (cluster == target), value, penalty)
    return penalty


def near_kernel(
    mask_any, m0_any, m1_any, m2_any, s0, s1_any, s2_any, c1_any, c2_any, own_pts, own_vec, other_pts, other_vec,
    near_msg, cross_msg, own_any, first_any, rest_any, f1_any, f2_any,
    own_out, other_out, f1, f2, m1_v, m2_v, s1, s2, c1, c2, win_pts, win_vec, source, target, vec_t, mask, m0, m1, m2, skel_own, skel_halo,
    ends_own, ends_other, pairs, sems, out_sems,
):
    core = lax.axis_index("rhs")
    body_lanes = (WINDOW - REACH) * LEAF
    main_from = pl.multiple_of(core * (LANES - body_lanes), HALO)
    main_to = pl.multiple_of((1 - core) * HALO, HALO)
    halo_to = pl.multiple_of(core * body_lanes, HALO)
    jobs = [(mask_any, mask), (m0_any, m0), (m1_any, m1), (m2_any, m2)]
    jobs += [(m1_any, m1_v), (s1_any, s1), (c1_any, c1), (m2_any, m2_v), (s2_any, s2), (c2_any, c2)]
    for half, (pts, vecs, halo) in enumerate(
        ((own_pts, own_vec, near_msg), (other_pts, other_vec, cross_msg))
    ):
        rows = pl.ds(half * 32, 32)
        main = pl.ds(main_to, body_lanes)
        edge = pl.ds(halo_to, HALO)
        jobs.append((pts.at[:, pl.ds(main_from, body_lanes)], win_pts.at[rows, main]))
        jobs.append((vecs.at[:, pl.ds(main_from, body_lanes)], win_vec.at[rows, main]))
        jobs.append((halo.at[pl.ds(0, 32), pl.ds(0, HALO)], win_pts.at[rows, edge]))
        jobs.append((halo.at[pl.ds(32, 32), pl.ds(0, HALO)], win_vec.at[rows, edge]))
    ends_at = pl.ds(HALO, 2 * EDGE)
    jobs += [(near_msg.at[:, ends_at], ends_own), (cross_msg.at[:, ends_at], ends_other)]
    jobs.append((near_msg.at[:, pl.ds(HALO + 2 * EDGE, 3 * EDGE)], skel_halo))
    for place, skel in enumerate((s0, s1_any, s2_any)):
        lanes = edge_lanes(core == 1, skel.shape[1], EDGE)
        jobs.append((skel.at[:, lanes], skel_own.at[:, pl.ds(place * EDGE, EDGE)]))
    copies = fetch(jobs, sems)
    for copy in copies:
        copy.start()

    own_out[:, : LANES // 2] = jnp.zeros((32, LANES // 2), F32)
    other_out[:, : LANES // 2] = jnp.zeros((32, LANES // 2), F32)

    copies[0].wait()
    count = jnp.int32(0)
    for leaf in range(HALF):
        for offset in range(-REACH, REACH + 1):
            pairs[count] = (leaf + REACH + offset) * 32 + leaf
            if offset == 0:
                count = count + 1
            else:
                column = REACH + offset if offset < 0 else REACH + offset - 1
                count = count + mask[column, core * HALF + leaf]
    for extra in range(REST):
        pairs[count + extra] = WINDOW * 32

    source[WINDOW] = jnp.zeros((4 * DIM, LEAF), BF16).reshape(LEAF, 4 * DIM)
    vec_t[WINDOW] = jnp.zeros((2 * 64, LEAF), BF16)

    for copy in copies[4:10]:
        copy.wait()
    couple_level(m2_v, s2, c2, f2)
    couple_level(m1_v, s1, c1, f1)
    stores = fetch(
        [
            (f1, f1_any), (f2, f2_any), (own_out, own_any), (other_out.at[:, pl.ds(0, CUT_AT)], first_any),
            (other_out.at[:, pl.ds(CUT_AT, NEAR_OUT - CUT_AT)], rest_any),
        ],
        out_sems,
    )
    for store in stores[:2]:
        store.start()
    for copy in copies[1:4] + copies[10:]:
        copy.wait()

    for leaf in range(WINDOW):
        lanes = slice(leaf * LEAF, (leaf + 1) * LEAF)
        from_side, to_side = augment(win_pts[:, lanes])
        source[leaf] = from_side.T
        if REACH <= leaf < WINDOW - REACH:
            target[leaf - REACH] = to_side
        vec_t[leaf] = jnp.concatenate(split(win_vec[:, lanes]), 0)

    row = lax.broadcasted_iota(jnp.int32, (8, EDGE), 0)
    indicator = jnp.where(row == lax.broadcasted_iota(jnp.int32, (8, EDGE), 1) // RANK, 1.0, 0.0)
    for place, far_mask in enumerate((m0, m1, m2)):
        lanes = slice(place * EDGE, (place + 1) * EDGE)
        from_side, _ = augment(skel_halo[:, lanes], indicator, None)
        _, to_side = augment(skel_own[:, lanes], None, edge_penalty(far_mask, core))
        high, low = weights(mul(from_side.T, to_side))
        rows = slice(place % 2 * 32, place % 2 * 32 + 32)
        at = slice(place // 2 * EDGE, (place // 2 + 1) * EDGE)
        cof_high, cof_low = split(jnp.concatenate([ends_own[rows, at], ends_other[rows, at]], 0))
        both = mul(jnp.concatenate([cof_high, cof_low], 0), high)
        term = both[:64] + both[64:] + mul(cof_high, low)
        lanes = slice(LANES // 2 + place * EDGE, LANES // 2 + (place + 1) * EDGE)
        own_out[:, lanes] = term[:32]
        other_out[:, lanes] = term[32:]

    def steps(start, size, number):
        def step(index, carry):
            found = []
            for k in range(size):
                code = pairs[start + index * size + k]
                src, tgt = lax.shift_right_logical(code, 5), lax.bitwise_and(code, 31)
                high, low = weights(mul(source[src], target[tgt]))
                both = mul(vec_t[src], high)
                found.append((tgt, both[:64] + both[64:] + mul(vec_t[src, :64], low)))
            for tgt, term in found:
                lanes = pl.ds(pl.multiple_of(tgt * LEAF, LEAF), LEAF)
                own_out[:, lanes] += term[:32]
                other_out[:, lanes] += term[32:]
            return carry

        lax.fori_loop(0, number, step, 0)

    done = jnp.int32(0)
    for size in (GROUP, GROUP // 2, GROUP // 4, REST):
        number = (count - done + REST - 1) // size
        steps(done, size, number)
        done = done + number * size
    for store in stores[2:]:
        store.start()
    for store in stores:
        store.wait()


def couple_level(mask, skel, coeff, out, beside=None):
    width = skel.shape[1]
    count = width // RANK
    cluster = lax.broadcasted_iota(jnp.int32, (count, width), 0)
    owner = lax.broadcasted_iota(jnp.int32, (count, width), 1) // RANK
    spread = jnp.where(cluster == owner, 1.0, 0.0).astype(BF16)
    allowed = mul(mask[...].astype(F32).astype(BF16), spread)
    row = lax.broadcasted_iota(jnp.int32, (8, width), 0)
    owner = lax.broadcasted_iota(jnp.int32, (8, width), 1) // RANK
    penalty = jnp.full((8, width), CUT, F32)
    for column, offset in enumerate((-2, -1, 1, 2)):
        linked = (row == lax.bitwise_and(owner + offset, 7)) & (allowed[column : column + 1] > 0.5)
        penalty = jnp.where(linked, 0.0, penalty)
    target = augment(skel[...], None, penalty)[1]

    wide = width + 2 * EDGE
    row = lax.broadcasted_iota(jnp.int32, (8, wide), 0)
    owner = lax.broadcasted_iota(jnp.int32, (8, wide), 1) // RANK - FREACH
    indicator = jnp.where(row == lax.bitwise_and(owner, 7), 1.0, 0.0)
    gap = jnp.zeros((DIM, EDGE), F32)
    source = augment(jnp.concatenate([gap, skel[...], gap], 1), indicator, None)[0]
    source = [source[:, k * 256 : (k + 1) * 256].T for k in range(wide // 256)]
    gap = gap[:RHS_DEV]
    cof_high, cof_low = split(jnp.concatenate([gap, coeff[...], gap], 1))
    cof = jnp.concatenate([cof_high, cof_low], 0)
    for group in range(count // 4):
        lanes = slice(group * 256, (group + 1) * 256)
        around = slice(group * 256, group * 256 + 512)
        high, low = weights(mul(jnp.concatenate(source[group : group + 2], 0), target[:, lanes]))
        both = mul(cof[:, around], high)
        out[:, lanes] = both[:RHS_DEV] + both[RHS_DEV:] + mul(cof_high[:, around], low)
        if beside is not None:
            beside(group)


def down_kernel(
    gathered_any, roots_any, m0_any, s0_any, c0_any, lv1_any, lv2_any, root_any, basis_any, f1_any, f2_any, own_any,
    first_any, rest_any, out_any, f0, field0, field1, field2, gathered, roots, m0, s0, c0, lv1, lv2, root, basis, f1, f2,
    own_near, other_near, out, sems, out_sems,
):
    core = lax.axis_index("rhs")
    quarter = LANES // 4
    body, ends = pl.ds(0, HALF * LEAF), pl.ds(HALF * LEAF, 3 * EDGE)
    late = pl.ds(HALF * LEAF - CUT_AT, 3 * EDGE)
    second, rest_body = pl.ds(CUT_AT, HALF * LEAF - CUT_AT), pl.ds(0, HALF * LEAF - CUT_AT)
    copies = fetch(
        [
            (roots_any, roots), (m0_any, m0), (s0_any, s0), (c0_any, c0),
            (gathered_any, gathered), (root_any, root), (f2_any, f2), (lv2_any, lv2), (f1_any, f1), (lv1_any, lv1),
            (own_any.at[:, ends], own_near.at[:, ends]), (rest_any.at[:, late], other_near.at[:, ends]),
            (basis_any, basis), (own_any.at[:, body], own_near.at[:, body]),
            (first_any, other_near.at[:, pl.ds(0, CUT_AT)]),
            (rest_any.at[:, rest_body], other_near.at[:, second]),
        ],
        sems,
    )
    for copy in copies:
        copy.start()

    for copy in copies[:4]:
        copy.wait()
    me = lax.axis_index("leaf")
    one = jnp.where(lax.broadcasted_iota(jnp.int32, (8, RANK), 0) == 0, 1.0, 0.0)
    pair = roots[:, pl.ds(pl.multiple_of((me // 2) * 128, 128), 128)]
    own = jnp.where(lax.broadcasted_iota(jnp.int32, (DIM, 128), 1) // RANK == lax.rem(me, 2), pair, 0.0)
    own_side = augment(own[:, :RANK] + own[:, RANK:], one, None)[0].T
    kernels = []

    def root_part(part):
        lanes = slice(part * 512, (part + 1) * 512)
        first = lax.broadcasted_iota(jnp.int32, (8, 512), 0) == 0
        cluster = part * 8 + lax.broadcasted_iota(jnp.int32, (8, 512), 1) // RANK
        penalty = jnp.where(first & (jnp.abs(cluster - me) < 2), CUT, 0.0)
        kernels.append(weights(mul(own_side, augment(roots[:, lanes], None, penalty)[1])))

    couple_level(m0, s0, c0, f0, root_part)

    for copy in copies[4:]:
        copy.wait()
    top = jnp.zeros((RHS_DEV, RANK), F32)
    for part, (high, low) in enumerate(kernels):
        pieces = []
        for chip in range(8 * part, 8 * part + 8):
            pieces.append(jnp.concatenate([gathered[chip, :, :RANK], gathered[chip, :, RANK:]], 0))
        cof_high, cof_low = split(jnp.concatenate(pieces, 1))
        both = mul(jnp.concatenate([cof_high, cof_low], 0), high, NT)
        top = top + both[:RHS_DEV] + both[RHS_DEV:] + mul(cof_high, low, NT)

    def coupled(ref, place):
        width = ref.shape[1]
        lanes = slice(LANES // 2 + place * EDGE, LANES // 2 + (place + 1) * EDGE)
        mine, theirs = own_near[:, lanes], other_near[:, lanes]
        ref[:, :EDGE] += jnp.where(core == 0, mine, theirs)
        ref[:, width - EDGE :] += jnp.where(core == 0, theirs, mine)

    coupled(f2, 2)
    field2[...] = f2[...] + mul3(top, root[...])

    def down_level(parents, transfer, coupled, children, count):
        for pair in range(count // 2):
            lanes = [slice((2 * pair + side) * 128, (2 * pair + side + 1) * 128) for side in range(2)]
            above = parents[:, pair * 128 : (pair + 1) * 128]
            for at, below in zip(lanes, pair_products(above, [transfer[:, at] for at in lanes])):
                children[:, at] = coupled[:, at] + below

    coupled(f1, 1)
    down_level(field2, lv2, f1, field1, LEAVES_DEV // 4)
    coupled(f0, 0)
    down_level(field1, lv1, f0, field0, LEAVES_DEV // 2)

    stores = []
    for part in range(4):
        near, near_from = (own_near, other_near)[part // 2], part % 2 * quarter
        start = pl.multiple_of((core if part < 2 else 1 - core) * 2 * quarter + near_from, quarter)
        for pair in range(LEAVES_DEV // 8):
            fields = field0[:, pl.ds(pl.multiple_of(start // 4 + pair * 128, 128), 128)]
            offsets = [(2 * pair + side) * LEAF for side in range(2)]
            lanes = [pl.ds(pl.multiple_of(start + offset, LEAF), LEAF) for offset in offsets]
            for offset, at, far in zip(offsets, lanes, pair_products(fields, [basis[:, at] for at in lanes])):
                out[:, at] = near[:, near_from + offset : near_from + offset + LEAF] + far
        lanes = pl.ds(start, quarter)
        store = pltpu.make_async_copy(out.at[:, lanes], out_any.at[:, lanes], out_sems.at[part])
        store.start()
        stores.append(store)
    for store in stores:
        store.wait()


def shapes(*dims):
    return [jax.ShapeDtypeStruct(dim, F32) for dim in dims]


def cost(flops, bytes_accessed, transcendentals=0):
    return pl.CostEstimate(flops=flops, bytes_accessed=bytes_accessed, transcendentals=transcendentals)


SWAP = [(0, 1), (1, 0)]
LAST = 2 * CHIPS - 1
STEPS = range(0, LAST - 1, 2)
NEAR_WAY = [pair for i in STEPS for pair in ((i, i + 2), (i + 3, i + 1))] + [(1, 0), (LAST - 1, LAST)]
CROSS_WAY = [pair for i in STEPS for pair in ((i + 1, i + 2), (i + 2, i + 1))] + [(0, LAST), (LAST, 0)]


def call(kernel, outputs, inputs, scratch, estimate, name):
    def spec(place):
        return pl.BlockSpec(memory_space=place)

    several = isinstance(outputs, list)
    return pl.pallas_call(
        kernel,
        out_shape=outputs,
        in_specs=[spec(pl.ANY)] * len(inputs),
        out_specs=[spec(pl.ANY)] * len(outputs) if several else spec(pl.ANY),
        scratch_shapes=scratch,
        compiler_params=pltpu.CompilerParams(vmem_limit_bytes=64 * 2**20),
        cost_estimate=estimate,
        name=name,
    )(*inputs)


def vmem(*dims):
    return [pltpu.VMEM(dim, F32) for dim in dims]


def like(*arrays):
    return [pltpu.VMEM(array.shape, array.dtype) for array in arrays]


def dma_sems(count):
    return pltpu.SemaphoreType.DMA((count,))


def up_call(vec, basis, lv1, lv2, root, pts, s0, s1, s2):
    coeffs = ((RHS_DEV, 2048), (RHS_DEV, 1024), (RHS_DEV, 512))
    return call(
        up_kernel,
        shapes(*coeffs, (CHIPS, RHS_DEV // 2, 2 * RANK), (DIM, HALO + 5 * EDGE), (DIM, HALO + 2 * EDGE)),
        (vec, basis, lv1, lv2, root, pts, s0, s1, s2),
        like(vec, basis, lv1, lv2, root)
        + vmem(*coeffs, (CHIPS, RHS_DEV // 2, 2 * RANK), (DIM, HALO + 5 * EDGE), (DIM, HALO + 2 * EDGE))
        + [dma_sems(14), dma_sems(9)],
        cost(6 * 10**8, 6 * 10**6),
        "up",
    )


def near_call(mask, m0, m1, m2, s0, s1, s2, c1, c2, pts, vec, other_pts, other_vec, near_msg, cross_msg):
    return call(
        near_kernel,
        shapes((32, NEAR_OUT), (32, CUT_AT), (32, NEAR_OUT - CUT_AT), c1.shape, c2.shape),
        (mask, m0, m1, m2, s0, s1, s2, c1, c2, pts, vec, other_pts, other_vec, near_msg, cross_msg),
        vmem((32, NEAR_OUT), (32, NEAR_OUT))
        + like(c1, c2, m1, m2, s1, s2, c1, c2)
        + vmem((DIM, WINDOW * LEAF), (64, WINDOW * LEAF))
        + [
            pltpu.VMEM((WINDOW + 1, LEAF, 4 * DIM), BF16),
            pltpu.VMEM((HALF, 4 * DIM, LEAF), BF16),
            pltpu.VMEM((WINDOW + 1, 128, LEAF), BF16),
        ]
        + [pltpu.SMEM(array.shape, jnp.int32) for array in (mask, m0, m1, m2)]
        + vmem((DIM, 3 * EDGE), (DIM, 3 * EDGE), (DIM, 2 * EDGE), (DIM, 2 * EDGE))
        + [pltpu.SMEM((HALF * (2 * REACH + 1) + REST,), jnp.int32), dma_sems(24), dma_sems(5)],
        cost(10**10, 5 * 10**6, 5 * 10**6),
        "near",
    )


def down_call(gathered, roots, m0, s0, c0, lv1, lv2, root, basis, f1, f2, own_near, first, rest):
    inputs = (gathered, roots, m0, s0, c0, lv1, lv2, root, basis, f1, f2, own_near, first, rest)
    return call(
        down_kernel,
        jax.ShapeDtypeStruct((RHS_DEV, LANES), F32),
        inputs,
        like(c0, c0, f1, f2, *inputs[:-2], own_near) + vmem((RHS_DEV, LANES)) + [dma_sems(16), dma_sems(4)],
        cost(2 * 10**9, 8 * 10**6),
        "down",
    )


def per_device(
    points, vectors, leaf_basis, skel_lv0, skel_lv1, skel_lv2, transfer_lv1, transfer_lv2,
    transfer_root, root_skeleton_points, near_mask, far_lv0, far_lv1, far_lv2,
):
    pts, vec, basis = points.T, vectors.T, leaf_basis.T
    skels = (skel_lv0.T, skel_lv1.T, skel_lv2.T)
    lv1, lv2, root = transfer_lv1.T, transfer_lv2.T, transfer_root.T
    far = (far_lv0.T, far_lv1.T, far_lv2.T)
    both = ("leaf", "rhs")

    other_pts = lax.ppermute(pts, "rhs", SWAP)
    other_vec = lax.ppermute(vec, "rhs", SWAP)
    c0, c1, c2, blocks, near_msg, cross_msg = up_call(vec, basis, lv1, lv2, root, pts, *skels)
    near_msg = lax.ppermute(near_msg, both, NEAR_WAY)
    cross_msg = lax.ppermute(cross_msg, both, CROSS_WAY)
    gathered = lax.all_to_all(blocks, "leaf", split_axis=0, concat_axis=0, tiled=True)
    own_near, first, rest, f1, f2 = near_call(
        near_mask.T, *far, *skels, c1, c2, pts, vec, other_pts, other_vec, near_msg, cross_msg
    )
    first = lax.ppermute(first, "rhs", SWAP)
    rest = lax.ppermute(rest, "rhs", SWAP)
    return down_call(
        gathered, root_skeleton_points.T, far[0], skels[0], c0, lv1, lv2, root, basis, f1, f2, own_near, first, rest
    ).T


def solution(mesh):
    split_both = P("leaf", "rhs")
    placed = (split_both, split_both) + (P("leaf", None),) * 7 + (P(),) + (P("leaf", None),) * 4
    return jax.shard_map(per_device, mesh=mesh, in_specs=placed, out_specs=split_both, check_vma=False)
```

```python
import math

import jax
import jax.numpy as jnp
from jax import lax
from jax.experimental import pallas as pl
from jax.experimental.pallas import tpu as pltpu
from jax.sharding import PartitionSpec as P

DIM = 64
RANK = 64
LEAF = 256
REACH = 4
FREACH = 2
LEAVES_DEV = 32
RHS_DEV = 32
CHIPS = 64

HALF = LEAVES_DEV // 2
WINDOW = HALF + 2 * REACH
HALO = REACH * LEAF
EDGE = FREACH * RANK
LANES = LEAVES_DEV * LEAF
NEAR_OUT = HALF * LEAF + 3 * EDGE
CUT_AT = HALF * LEAF // 2
GROUP = 32
REST = 8
SCALE = math.sqrt(2.0 / 24.0 * math.log2(math.e))
CUT = -32768.0

F32 = jnp.float32
BF16 = jnp.bfloat16

NN = (((1,), (0,)), ((), ()))
NT = (((1,), (1,)), ((), ()))


def mul(left, right, dims=NN):
    return lax.dot_general(left, right, dims, preferred_element_type=F32)


def split(x):
    high = x.astype(BF16)
    return high, (x - high.astype(F32)).astype(BF16)


def mul3(left, right, dims=NN):
    rows = left.shape[0]
    left_high, left_low = split(left)
    right_high, right_low = split(right)
    both = mul(jnp.concatenate([left_high, left_low], 0), right_high, dims)
    return both[:rows] + both[rows:] + mul(left_high, right_low, dims)


def low_lanes(rows):
    return lax.broadcasted_iota(jnp.int32, (rows, 2 * RANK), 1) < RANK


def stack(x):
    return jnp.concatenate(split(x), 0)


def pair_products(pair, rights):
    turned = pltpu.roll(pair, RANK, 1)
    rows = pair.shape[0]
    low = low_lanes(rows)
    out = []
    for left, right in zip((jnp.where(low, pair, turned), jnp.where(low, turned, pair)), rights):
        both = mul(stack(left), stack(right))
        out.append(both[:rows] + both[rows:])
    return out


def augment(points, source_extra=None, target_extra=None):
    high, low = split(points * SCALE)
    high_f, low_f = high.astype(F32), low.astype(F32)
    norm = 0.5 * jnp.sum(high_f * (high_f + 2.0 * low_f), axis=0, keepdims=True)
    first = norm.astype(BF16).astype(F32)
    second = (norm - first).astype(BF16).astype(F32)
    third = (norm - first - second).astype(BF16).astype(F32)
    width = points.shape[1]
    row = lax.broadcasted_iota(jnp.int32, (8, width), 0)

    def rows_of(start, ones):
        picked = jnp.where(row == start, -first, 0.0)
        picked = jnp.where(row == start + 1, -second, picked)
        picked = jnp.where(row == start + 2, -third, picked)
        return jnp.where((row >= ones) & (row < ones + 3), 1.0, picked)

    nothing = jnp.zeros((8, width), F32)
    rest = jnp.zeros((DIM - 16, width), BF16)

    def block(start, ones, extra):
        tail = jnp.concatenate([rows_of(start, ones), nothing if extra is None else extra], 0)
        return tail.astype(BF16), rest

    source = jnp.concatenate([high, low, high, *block(0, 3, source_extra)], 0)
    target = jnp.concatenate([high, high, low, *block(3, 0, target_extra)], 0)
    return source, target


def weights(exponent):
    return split(jnp.exp2(exponent))


def fetch(jobs, sems):
    return [pltpu.make_async_copy(src, dst, sems.at[k]) for k, (src, dst) in enumerate(jobs)]


def edge_lanes(last, width, size):
    return pl.ds(pl.multiple_of(jnp.where(last, width - size, 0), size), size)


def up_kernel(
    vec, basis, lv1, lv2, root, pts, s0, s1, s2,
    c0, c1, c2, blocks, near_msg, cross_msg,
    vec_v, basis_v, lv1_v, lv2_v, root_v, coeff0, coeff1, coeff2, top_v, near_v, cross_v, sems, out_sems,
):
    core = lax.axis_index("rhs")
    near_last, cross_last = core == 0, core == 1
    jobs = []
    for chunk in range(2):
        lanes = pl.ds(chunk * 4096, 4096)
        jobs.append((vec.at[:, lanes], vec_v.at[:, lanes]))
        jobs.append((basis.at[:, lanes], basis_v.at[:, lanes]))
    jobs += [(lv1, lv1_v), (lv2, lv2_v), (root, root_v)]
    for place, skel in enumerate((s0, s1, s2)):
        lanes = edge_lanes(near_last, skel.shape[1], EDGE)
        jobs.append((skel.at[:, lanes], near_v.at[:, pl.ds(HALO + (2 + place) * EDGE, EDGE)]))
    for msg, last in ((near_v, near_last), (cross_v, cross_last)):
        for part, array in enumerate((pts, vec)):
            lanes = edge_lanes(last, LANES, HALO)
            jobs.append((array.at[:, lanes], msg.at[pl.ds(part * 32, 32), pl.ds(0, HALO)]))
    copies = fetch(jobs, sems)
    for copy in copies:
        copy.start()

    for chunk in range(2):
        copies[2 * chunk].wait()
        copies[2 * chunk + 1].wait()
        for pair in range(8 * chunk, 8 * chunk + 8):
            parts = []
            for side in range(2):
                lanes = slice((2 * pair + side) * LEAF, (2 * pair + side + 1) * LEAF)
                parts.append(mul3(vec_v[:, lanes], basis_v[:, lanes], NT))
            coeff0[:, pair * 128 : (pair + 1) * 128] = jnp.concatenate(parts, 1)

    def up_level(children, transfer, parents, count):
        for pair in range(count // 2):
            parts = []
            for side in range(2):
                lanes = slice((2 * pair + side) * 128, (2 * pair + side + 1) * 128)
                parts.append(mul3(children[:, lanes], transfer[:, lanes], NT))
            parents[:, pair * 128 : (pair + 1) * 128] = jnp.concatenate(parts, 1)

    for copy in copies[7:]:
        copy.wait()
    body, ends_at, skel_at = pl.ds(0, HALO), pl.ds(HALO, 2 * EDGE), pl.ds(HALO + 2 * EDGE, 3 * EDGE)
    stores = fetch(
        [
            (near_v.at[:, body], near_msg.at[:, body]), (cross_v.at[:, body], cross_msg.at[:, body]),
            (near_v.at[:, skel_at], near_msg.at[:, skel_at]), (coeff0, c0), (coeff1, c1), (coeff2, c2),
            (near_v.at[:, ends_at], near_msg.at[:, ends_at]),
            (cross_v.at[:, ends_at], cross_msg.at[:, ends_at]), (top_v, blocks),
        ],
        out_sems,
    )
    for store in stores[:4]:
        store.start()
    copies[4].wait()
    up_level(coeff0, lv1_v, coeff1, LEAVES_DEV // 2)
    copies[5].wait()
    up_level(coeff1, lv2_v, coeff2, LEAVES_DEV // 4)
    for msg, last in ((near_v, near_last), (cross_v, cross_last)):
        ends = [
            jnp.where(last, ref[:, ref.shape[1] - EDGE :], ref[:, :EDGE]) for ref in (coeff0, coeff1, coeff2)
        ]
        msg[:RHS_DEV, HALO : HALO + EDGE] = ends[0]
        msg[RHS_DEV:, HALO : HALO + EDGE] = ends[1]
        msg[:RHS_DEV, HALO + EDGE : HALO + 2 * EDGE] = ends[2]
        msg[RHS_DEV:, HALO + EDGE : HALO + 2 * EDGE] = jnp.zeros((RHS_DEV, EDGE), F32)
    for store in stores[4:8]:
        store.start()
    copies[6].wait()
    top = mul3(coeff2[...], root_v[...], NT)
    packed = jnp.concatenate([top[: RHS_DEV // 2], top[RHS_DEV // 2 :]], 1)
    top_v[...] = jnp.broadcast_to(packed[None], (CHIPS, RHS_DEV // 2, 2 * RANK))
    stores[8].start()
    for store in stores:
        store.wait()


def edge_penalty(mask, core):
    count = mask.shape[1]
    first = core == 0
    chip = lax.axis_index("leaf")
    outside = jnp.where(first, chip == 0, chip == CHIPS - 1)
    linked = [
        [jnp.where(first, mask[0, 0], mask[3, count - 2]), jnp.where(first, 0, mask[2, count - 1])],
        [jnp.where(first, mask[1, 0], 0), jnp.where(first, mask[0, 1], mask[3, count - 1])],
    ]
    row = lax.broadcasted_iota(jnp.int32, (8, EDGE), 0)
    cluster = lax.broadcasted_iota(jnp.int32, (8, EDGE), 1) // RANK
    penalty = jnp.zeros((8, EDGE), F32)
    for source in range(2):
        for target in range(2):
            value = jnp.where((linked[source][target] > 0) & jnp.logical_not(outside), 0.0, CUT)
            penalty = jnp.where((row == source) & (cluster == target), value, penalty)
    return penalty


def near_kernel(
    mask_any, m0_any, m1_any, m2_any, s0, s1_any, s2_any, c1_any, c2_any, own_pts, own_vec, other_pts, other_vec,
    near_msg, cross_msg, own_any, first_any, rest_any, f1_any, f2_any,
    own_out, other_out, f1, f2, m1_v, m2_v, s1, s2, c1, c2, win_pts, win_vec, source, target, vec_t, mask, m0, m1, m2, skel_own, skel_halo,
    ends_own, ends_other, pairs, sems, out_sems,
):
    core = lax.axis_index("rhs")
    body_lanes = (WINDOW - REACH) * LEAF
    main_from = pl.multiple_of(core * (LANES - body_lanes), HALO)
    main_to = pl.multiple_of((1 - core) * HALO, HALO)
    halo_to = pl.multiple_of(core * body_lanes, HALO)
    jobs = [(mask_any, mask), (m0_any, m0), (m1_any, m1), (m2_any, m2)]
    jobs += [(m1_any, m1_v), (s1_any, s1), (c1_any, c1), (m2_any, m2_v), (s2_any, s2), (c2_any, c2)]
    for half, (pts, vecs, halo) in enumerate(
        ((own_pts, own_vec, near_msg), (other_pts, other_vec, cross_msg))
    ):
        rows = pl.ds(half * 32, 32)
        main = pl.ds(main_to, body_lanes)
        edge = pl.ds(halo_to, HALO)
        jobs.append((pts.at[:, pl.ds(main_from, body_lanes)], win_pts.at[rows, main]))
        jobs.append((vecs.at[:, pl.ds(main_from, body_lanes)], win_vec.at[rows, main]))
        jobs.append((halo.at[pl.ds(0, 32), pl.ds(0, HALO)], win_pts.at[rows, edge]))
        jobs.append((halo.at[pl.ds(32, 32), pl.ds(0, HALO)], win_vec.at[rows, edge]))
    ends_at = pl.ds(HALO, 2 * EDGE)
    jobs += [(near_msg.at[:, ends_at], ends_own), (cross_msg.at[:, ends_at], ends_other)]
    jobs.append((near_msg.at[:, pl.ds(HALO + 2 * EDGE, 3 * EDGE)], skel_halo))
    for place, skel in enumerate((s0, s1_any, s2_any)):
        lanes = edge_lanes(core == 1, skel.shape[1], EDGE)
        jobs.append((skel.at[:, lanes], skel_own.at[:, pl.ds(place * EDGE, EDGE)]))
    copies = fetch(jobs, sems)
    for copy in copies:
        copy.start()

    own_out[:, : LANES // 2] = jnp.zeros((32, LANES // 2), F32)
    other_out[:, : LANES // 2] = jnp.zeros((32, LANES // 2), F32)

    copies[0].wait()
    count = jnp.int32(0)
    for leaf in range(HALF):
        for offset in range(-REACH, REACH + 1):
            pairs[count] = (leaf + REACH + offset) * 32 + leaf
            if offset == 0:
                count = count + 1
            else:
                column = REACH + offset if offset < 0 else REACH + offset - 1
                count = count + mask[column, core * HALF + leaf]
    for extra in range(REST):
        pairs[count + extra] = WINDOW * 32

    source[WINDOW] = jnp.zeros((4 * DIM, LEAF), BF16).reshape(LEAF, 4 * DIM)
    vec_t[WINDOW] = jnp.zeros((2 * 64, LEAF), BF16)

    for copy in copies[4:10]:
        copy.wait()
    couple_level(m2_v, s2, c2, f2)
    couple_level(m1_v, s1, c1, f1)
    stores = fetch(
        [
            (f1, f1_any), (f2, f2_any), (own_out, own_any), (other_out.at[:, pl.ds(0, CUT_AT)], first_any),
            (other_out.at[:, pl.ds(CUT_AT, NEAR_OUT - CUT_AT)], rest_any),
        ],
        out_sems,
    )
    for store in stores[:2]:
        store.start()
    for copy in copies[1:4] + copies[10:]:
        copy.wait()

    for leaf in range(WINDOW):
        lanes = slice(leaf * LEAF, (leaf + 1) * LEAF)
        from_side, to_side = augment(win_pts[:, lanes])
        source[leaf] = from_side.T
        if REACH <= leaf < WINDOW - REACH:
            target[leaf - REACH] = to_side
        vec_t[leaf] = jnp.concatenate(split(win_vec[:, lanes]), 0)

    row = lax.broadcasted_iota(jnp.int32, (8, EDGE), 0)
    indicator = jnp.where(row == lax.broadcasted_iota(jnp.int32, (8, EDGE), 1) // RANK, 1.0, 0.0)
    for place, far_mask in enumerate((m0, m1, m2)):
        lanes = slice(place * EDGE, (place + 1) * EDGE)
        from_side, _ = augment(skel_halo[:, lanes], indicator, None)
        _, to_side = augment(skel_own[:, lanes], None, edge_penalty(far_mask, core))
        high, low = weights(mul(from_side.T, to_side))
        rows = slice(place % 2 * 32, place % 2 * 32 + 32)
        at = slice(place // 2 * EDGE, (place // 2 + 1) * EDGE)
        cof_high, cof_low = split(jnp.concatenate([ends_own[rows, at], ends_other[rows, at]], 0))
        both = mul(jnp.concatenate([cof_high, cof_low], 0), high)
        term = both[:64] + both[64:] + mul(cof_high, low)
        lanes = slice(LANES // 2 + place * EDGE, LANES // 2 + (place + 1) * EDGE)
        own_out[:, lanes] = term[:32]
        other_out[:, lanes] = term[32:]

    def steps(start, size, number):
        def step(index, carry):
            found = []
            for k in range(size):
                code = pairs[start + index * size + k]
                src, tgt = lax.shift_right_logical(code, 5), lax.bitwise_and(code, 31)
                high, low = weights(mul(source[src], target[tgt]))
                both = mul(vec_t[src], high)
                found.append((tgt, both[:64] + both[64:] + mul(vec_t[src, :64], low)))
            for tgt, term in found:
                lanes = pl.ds(pl.multiple_of(tgt * LEAF, LEAF), LEAF)
                own_out[:, lanes] += term[:32]
                other_out[:, lanes] += term[32:]
            return carry

        lax.fori_loop(0, number, step, 0)

    done = jnp.int32(0)
    for size in (GROUP, GROUP // 2, REST):
        number = (count - done + REST - 1) // size
        steps(done, size, number)
        done = done + number * size
    for store in stores[2:]:
        store.start()
    for store in stores:
        store.wait()


def couple_level(mask, skel, coeff, out, beside=None):
    width = skel.shape[1]
    count = width // RANK
    cluster = lax.broadcasted_iota(jnp.int32, (count, width), 0)
    owner = lax.broadcasted_iota(jnp.int32, (count, width), 1) // RANK
    spread = jnp.where(cluster == owner, 1.0, 0.0).astype(BF16)
    allowed = mul(mask[...].astype(F32).astype(BF16), spread)
    row = lax.broadcasted_iota(jnp.int32, (8, width), 0)
    owner = lax.broadcasted_iota(jnp.int32, (8, width), 1) // RANK
    penalty = jnp.full((8, width), CUT, F32)
    for column, offset in enumerate((-2, -1, 1, 2)):
        linked = (row == lax.bitwise_and(owner + offset, 7)) & (allowed[column : column + 1] > 0.5)
        penalty = jnp.where(linked, 0.0, penalty)
    target = augment(skel[...], None, penalty)[1]

    wide = width + 2 * EDGE
    row = lax.broadcasted_iota(jnp.int32, (8, wide), 0)
    owner = lax.broadcasted_iota(jnp.int32, (8, wide), 1) // RANK - FREACH
    indicator = jnp.where(row == lax.bitwise_and(owner, 7), 1.0, 0.0)
    gap = jnp.zeros((DIM, EDGE), F32)
    source = augment(jnp.concatenate([gap, skel[...], gap], 1), indicator, None)[0]
    source = [source[:, k * 256 : (k + 1) * 256].T for k in range(wide // 256)]
    gap = gap[:RHS_DEV]
    cof_high, cof_low = split(jnp.concatenate([gap, coeff[...], gap], 1))
    cof = jnp.concatenate([cof_high, cof_low], 0)
    for group in range(count // 4):
        lanes = slice(group * 256, (group + 1) * 256)
        around = slice(group * 256, group * 256 + 512)
        high, low = weights(mul(jnp.concatenate(source[group : group + 2], 0), target[:, lanes]))
        both = mul(cof[:, around], high)
        out[:, lanes] = both[:RHS_DEV] + both[RHS_DEV:] + mul(cof_high[:, around], low)
        if beside is not None:
            beside(group)


def down_kernel(
    gathered_any, roots_any, m0_any, s0_any, c0_any, lv1_any, lv2_any, root_any, basis_any, f1_any, f2_any, own_any,
    first_any, rest_any, out_any, f0, field0, field1, field2, gathered, roots, m0, s0, c0, lv1, lv2, root, basis, f1, f2,
    own_near, other_near, out, sems, out_sems,
):
    core = lax.axis_index("rhs")
    quarter = LANES // 4
    body, ends = pl.ds(0, HALF * LEAF), pl.ds(HALF * LEAF, 3 * EDGE)
    late = pl.ds(HALF * LEAF - CUT_AT, 3 * EDGE)
    second, rest_body = pl.ds(CUT_AT, HALF * LEAF - CUT_AT), pl.ds(0, HALF * LEAF - CUT_AT)
    copies = fetch(
        [
            (roots_any, roots), (m0_any, m0), (s0_any, s0), (c0_any, c0),
            (gathered_any, gathered), (root_any, root), (f2_any, f2), (lv2_any, lv2), (f1_any, f1), (lv1_any, lv1),
            (own_any.at[:, ends], own_near.at[:, ends]), (rest_any.at[:, late], other_near.at[:, ends]),
            (basis_any, basis), (own_any.at[:, body], own_near.at[:, body]),
            (first_any, other_near.at[:, pl.ds(0, CUT_AT)]),
            (rest_any.at[:, rest_body], other_near.at[:, second]),
        ],
        sems,
    )
    for copy in copies:
        copy.start()

    for copy in copies[:4]:
        copy.wait()
    me = lax.axis_index("leaf")
    one = jnp.where(lax.broadcasted_iota(jnp.int32, (8, RANK), 0) == 0, 1.0, 0.0)
    pair = roots[:, pl.ds(pl.multiple_of((me // 2) * 128, 128), 128)]
    own = jnp.where(lax.broadcasted_iota(jnp.int32, (DIM, 128), 1) // RANK == lax.rem(me, 2), pair, 0.0)
    own_side = augment(own[:, :RANK] + own[:, RANK:], one, None)[0].T
    kernels = []

    def root_part(part):
        lanes = slice(part * 512, (part + 1) * 512)
        first = lax.broadcasted_iota(jnp.int32, (8, 512), 0) == 0
        cluster = part * 8 + lax.broadcasted_iota(jnp.int32, (8, 512), 1) // RANK
        penalty = jnp.where(first & (jnp.abs(cluster - me) < 2), CUT, 0.0)
        kernels.append(weights(mul(own_side, augment(roots[:, lanes], None, penalty)[1])))

    couple_level(m0, s0, c0, f0, root_part)

    for copy in copies[4:]:
        copy.wait()
    top = jnp.zeros((RHS_DEV, RANK), F32)
    for part, (high, low) in enumerate(kernels):
        pieces = []
        for chip in range(8 * part, 8 * part + 8):
            pieces.append(jnp.concatenate([gathered[chip, :, :RANK], gathered[chip, :, RANK:]], 0))
        cof_high, cof_low = split(jnp.concatenate(pieces, 1))
        both = mul(jnp.concatenate([cof_high, cof_low], 0), high, NT)
        top = top + both[:RHS_DEV] + both[RHS_DEV:] + mul(cof_high, low, NT)

    def coupled(ref, place):
        width = ref.shape[1]
        lanes = slice(LANES // 2 + place * EDGE, LANES // 2 + (place + 1) * EDGE)
        mine, theirs = own_near[:, lanes], other_near[:, lanes]
        ref[:, :EDGE] += jnp.where(core == 0, mine, theirs)
        ref[:, width - EDGE :] += jnp.where(core == 0, theirs, mine)

    coupled(f2, 2)
    field2[...] = f2[...] + mul3(top, root[...])

    def down_level(parents, transfer, coupled, children, count):
        for pair in range(count // 2):
            lanes = [slice((2 * pair + side) * 128, (2 * pair + side + 1) * 128) for side in range(2)]
            above = parents[:, pair * 128 : (pair + 1) * 128]
            for at, below in zip(lanes, pair_products(above, [transfer[:, at] for at in lanes])):
                children[:, at] = coupled[:, at] + below

    coupled(f1, 1)
    down_level(field2, lv2, f1, field1, LEAVES_DEV // 4)
    coupled(f0, 0)
    down_level(field1, lv1, f0, field0, LEAVES_DEV // 2)

    stores = []
    for part in range(4):
        near, near_from = (own_near, other_near)[part // 2], part % 2 * quarter
        start = pl.multiple_of((core if part < 2 else 1 - core) * 2 * quarter + near_from, quarter)
        for pair in range(LEAVES_DEV // 8):
            fields = field0[:, pl.ds(pl.multiple_of(start // 4 + pair * 128, 128), 128)]
            offsets = [(2 * pair + side) * LEAF for side in range(2)]
            lanes = [pl.ds(pl.multiple_of(start + offset, LEAF), LEAF) for offset in offsets]
            for offset, at, far in zip(offsets, lanes, pair_products(fields, [basis[:, at] for at in lanes])):
                out[:, at] = near[:, near_from + offset : near_from + offset + LEAF] + far
        lanes = pl.ds(start, quarter)
        store = pltpu.make_async_copy(out.at[:, lanes], out_any.at[:, lanes], out_sems.at[part])
        store.start()
        stores.append(store)
    for store in stores:
        store.wait()


def shapes(*dims):
    return [jax.ShapeDtypeStruct(dim, F32) for dim in dims]


def cost(flops, bytes_accessed, transcendentals=0):
    return pl.CostEstimate(flops=flops, bytes_accessed=bytes_accessed, transcendentals=transcendentals)


SWAP = [(0, 1), (1, 0)]
LAST = 2 * CHIPS - 1
STEPS = range(0, LAST - 1, 2)
NEAR_WAY = [pair for i in STEPS for pair in ((i, i + 2), (i + 3, i + 1))] + [(1, 0), (LAST - 1, LAST)]
CROSS_WAY = [pair for i in STEPS for pair in ((i + 1, i + 2), (i + 2, i + 1))] + [(0, 0), (LAST, LAST)]


def call(kernel, outputs, inputs, scratch, estimate, name):
    def spec(place):
        return pl.BlockSpec(memory_space=place)

    several = isinstance(outputs, list)
    return pl.pallas_call(
        kernel,
        out_shape=outputs,
        in_specs=[spec(pl.ANY)] * len(inputs),
        out_specs=[spec(pl.ANY)] * len(outputs) if several else spec(pl.ANY),
        scratch_shapes=scratch,
        compiler_params=pltpu.CompilerParams(vmem_limit_bytes=64 * 2**20),
        cost_estimate=estimate,
        name=name,
    )(*inputs)


def vmem(*dims):
    return [pltpu.VMEM(dim, F32) for dim in dims]


def like(*arrays):
    return [pltpu.VMEM(array.shape, array.dtype) for array in arrays]


def dma_sems(count):
    return pltpu.SemaphoreType.DMA((count,))


def up_call(vec, basis, lv1, lv2, root, pts, s0, s1, s2):
    coeffs = ((RHS_DEV, 2048), (RHS_DEV, 1024), (RHS_DEV, 512))
    return call(
        up_kernel,
        shapes(*coeffs, (CHIPS, RHS_DEV // 2, 2 * RANK), (DIM, HALO + 5 * EDGE), (DIM, HALO + 2 * EDGE)),
        (vec, basis, lv1, lv2, root, pts, s0, s1, s2),
        like(vec, basis, lv1, lv2, root)
        + vmem(*coeffs, (CHIPS, RHS_DEV // 2, 2 * RANK), (DIM, HALO + 5 * EDGE), (DIM, HALO + 2 * EDGE))
        + [dma_sems(14), dma_sems(9)],
        cost(6 * 10**8, 6 * 10**6),
        "up",
    )


def near_call(mask, m0, m1, m2, s0, s1, s2, c1, c2, pts, vec, other_pts, other_vec, near_msg, cross_msg):
    return call(
        near_kernel,
        shapes((32, NEAR_OUT), (32, CUT_AT), (32, NEAR_OUT - CUT_AT), c1.shape, c2.shape),
        (mask, m0, m1, m2, s0, s1, s2, c1, c2, pts, vec, other_pts, other_vec, near_msg, cross_msg),
        vmem((32, NEAR_OUT), (32, NEAR_OUT))
        + like(c1, c2, m1, m2, s1, s2, c1, c2)
        + vmem((DIM, WINDOW * LEAF), (64, WINDOW * LEAF))
        + [
            pltpu.VMEM((WINDOW + 1, LEAF, 4 * DIM), BF16),
            pltpu.VMEM((HALF, 4 * DIM, LEAF), BF16),
            pltpu.VMEM((WINDOW + 1, 128, LEAF), BF16),
        ]
        + [pltpu.SMEM(array.shape, jnp.int32) for array in (mask, m0, m1, m2)]
        + vmem((DIM, 3 * EDGE), (DIM, 3 * EDGE), (DIM, 2 * EDGE), (DIM, 2 * EDGE))
        + [pltpu.SMEM((HALF * (2 * REACH + 1) + REST,), jnp.int32), dma_sems(24), dma_sems(5)],
        cost(10**10, 5 * 10**6, 5 * 10**6),
        "near",
    )


def down_call(gathered, roots, m0, s0, c0, lv1, lv2, root, basis, f1, f2, own_near, first, rest):
    inputs = (gathered, roots, m0, s0, c0, lv1, lv2, root, basis, f1, f2, own_near, first, rest)
    return call(
        down_kernel,
        jax.ShapeDtypeStruct((RHS_DEV, LANES), F32),
        inputs,
        like(c0, c0, f1, f2, *inputs[:-2], own_near) + vmem((RHS_DEV, LANES)) + [dma_sems(16), dma_sems(4)],
        cost(2 * 10**9, 8 * 10**6),
        "down",
    )


def per_device(
    points, vectors, leaf_basis, skel_lv0, skel_lv1, skel_lv2, transfer_lv1, transfer_lv2,
    transfer_root, root_skeleton_points, near_mask, far_lv0, far_lv1, far_lv2,
):
    pts, vec, basis = points.T, vectors.T, leaf_basis.T
    skels = (skel_lv0.T, skel_lv1.T, skel_lv2.T)
    lv1, lv2, root = transfer_lv1.T, transfer_lv2.T, transfer_root.T
    far = (far_lv0.T, far_lv1.T, far_lv2.T)
    both = ("leaf", "rhs")

    other_pts = lax.ppermute(pts, "rhs", SWAP)
    other_vec = lax.ppermute(vec, "rhs", SWAP)
    c0, c1, c2, blocks, near_msg, cross_msg = up_call(vec, basis, lv1, lv2, root, pts, *skels)
    near_msg = lax.ppermute(near_msg, both, NEAR_WAY)
    cross_msg = lax.ppermute(cross_msg, both, CROSS_WAY)
    gathered = lax.all_to_all(blocks, "leaf", split_axis=0, concat_axis=0, tiled=True)
    own_near, first, rest, f1, f2 = near_call(
        near_mask.T, *far, *skels, c1, c2, pts, vec, other_pts, other_vec, near_msg, cross_msg
    )
    first = lax.ppermute(first, "rhs", SWAP)
    rest = lax.ppermute(rest, "rhs", SWAP)
    return down_call(
        gathered, root_skeleton_points.T, far[0], skels[0], c0, lv1, lv2, root, basis, f1, f2, own_near, first, rest
    ).T


def solution(mesh):
    split_both = P("leaf", "rhs")
    placed = (split_both, split_both) + (P("leaf", None),) * 7 + (P(),) + (P("leaf", None),) * 4
    return jax.shard_map(per_device, mesh=mesh, in_specs=placed, out_specs=split_both, check_vma=False)
```
